256 devices in a mesh: ctx: 16 (over y_hi, z), tp: 8 (over x, core), grp: 2 (over y_lo).
Axes of the slice: x: 4, y: 4 (y_hi: 2, y_lo: 2; y = y_hi * 2 + y_lo), z: 8, core: 2. Of those that a mesh axis runs over, the one named last changes fastest.
Arguments:
- span_queries: bfloat16 [2, 1024, 8192], P('grp', 'ctx', 'tp'), may hold values from -100 to 100
- span_keys: bfloat16 [2, 1024, 1024], P('grp', 'ctx', 'tp'), may hold values from -7 to 7
- span_values: bfloat16 [2, 1024, 1024], P('grp', 'ctx', 'tp'), may hold values from -6 to 6
- prompt_keys: bfloat16 [2, 32768, 1024], P('grp', 'ctx', 'tp'), may hold values from -7 to 7
- prompt_values: bfloat16 [2, 32768, 1024], P('grp', 'ctx', 'tp'), may hold values from -6 to 6
- block_owner: int32 [2, 64], replicated, may hold values from 0 to 15, as said below
- block_slot: int32 [2, 64], replicated, may hold values from 0 to 7, as said below
- decode_queries: bfloat16 [2, 256, 4, 8192], P('grp', 'ctx', None, 'tp'), may hold values from -100 to 100
- decode_new_keys: bfloat16 [2, 256, 4, 1024], P('grp', 'ctx', None, 'tp'), may hold values from -8 to 8
- decode_new_values: bfloat16 [2, 256, 4, 1024], P('grp', 'ctx', None, 'tp'), may hold values from -6 to 6
- cache_keys: bfloat16 [2, 256, 256, 1024], P('grp', 'ctx', None, 'tp'), may hold values from -7 to 7
- cache_values: bfloat16 [2, 256, 256, 1024], P('grp', 'ctx', None, 'tp'), may hold values from -6 to 6
- cache_len: int32 [2, 256], P('grp', 'ctx'), may hold values from 64 to 256, as said below
- out_weight: bfloat16 [8192, 4096], P('tp'), may hold values from -0.0625 to 0.0625
Outputs:
- prefill_out: bfloat16 [2, 1024, 4096], P('grp', ('ctx', 'tp'))
- decode_out: bfloat16 [2, 256, 4, 4096], P('grp', ('ctx', 'tp'))
The draws below stay inside these ranges and needn't reach their ends.
Inputs may be any that keep to these rules, and one draw needn't show every extreme that they name: `block_owner`: in each pool at most 8 blocks name one replica, and exactly 8 blocks name some replica. `block_slot`: blocks of one pool that name the same replica have different slots. `cache_len`: some row of each pool has 256 live slots.
All inputs are finite; a program needn't handle non-finite values.
Results may differ from the reference program's by a relative error of at most 0.02.
Values may be sent and summed in bfloat16 or wider, within the bound.
A program may use at most 128 MiB of HBM per device.

```python
import jax
import jax.numpy as jnp
from jax import lax

HEADS = 64
KVH = 8
HD = 128
O_COLS = 4096
BLOCK = 16
STEPS = 4
DEC_ROWS = 16
CACHE = 256
POOLS = 2
PROMPT = 32768
SPAN = 1024
KB = 64
SLOTS = 8
ROWS = 256
N_CTX = 16


def prompt_shared(key):
    base_keys = jnp.clip(jax.random.normal(jax.random.fold_in(key, 101), (POOLS, PROMPT, KVH * HD), jnp.float32), -6.0, 6.0)
    return base_keys


def cache_shared(key):
    base_keys = jnp.clip(jax.random.normal(jax.random.fold_in(key, 103), (POOLS, ROWS, CACHE, KVH * HD), jnp.float32), -6.0, 6.0)
    return base_keys


def slot_layout(key):
    slot_total = 2 * KB

    def layout_pool(pool_key):
        full_owner = jax.random.randint(jax.random.fold_in(pool_key, 1), (), 0, slot_total // SLOTS)
        ranking = jax.random.permutation(jax.random.fold_in(pool_key, 2), slot_total)
        positions = jnp.arange(slot_total, dtype=jnp.int32)
        priority = jnp.where(positions // SLOTS == full_owner, positions % SLOTS, SLOTS + ranking)
        chosen = jnp.argsort(priority, stable=True)[:KB]
        shuffle = jax.random.permutation(jax.random.fold_in(pool_key, 3), KB)
        return jnp.take(chosen, shuffle)
    picked = jax.vmap(layout_pool)(jax.random.split(jax.random.fold_in(key, 200), POOLS))
    return picked.astype(jnp.int32)


def draw_prompt_keys(key, part):
    base_keys = prompt_shared(key)
    return base_keys.astype(jnp.bfloat16)


def draw_span_queries(key, part):
    key = jax.random.fold_in(key, 2)
    normal_part = jnp.clip(3.0 * jax.random.normal(key, (POOLS, SPAN, HEADS * HD), jnp.float32), -18.0, 18.0)
    return normal_part.astype(jnp.bfloat16)


def draw_cache_keys(key, part):
    base_keys = cache_shared(key)
    return base_keys.astype(jnp.bfloat16)


def draw_decode_queries(key, part):
    key = jax.random.fold_in(key, 4)
    normal_part = jnp.clip(3.0 * jax.random.normal(key, (POOLS, ROWS, STEPS, HEADS * HD), jnp.float32), -18.0, 18.0)
    return normal_part.astype(jnp.bfloat16)


def draw_block_owner(key, part):
    picked = slot_layout(key)
    return (picked // SLOTS).astype(jnp.int32)


def draw_block_slot(key, part):
    picked = slot_layout(key)
    return (picked % SLOTS).astype(jnp.int32)


def draw_cache_len(key, part):
    key = jax.random.fold_in(key, 7)
    lengths = jax.random.randint(jax.random.fold_in(key, 1), (POOLS, ROWS), CACHE // 4, CACHE + 1)
    full_row = jax.random.randint(jax.random.fold_in(key, 2), (POOLS,), 0, ROWS)
    lengths = jnp.where(jnp.arange(ROWS, dtype=jnp.int32)[None, :] == full_row[:, None], CACHE, lengths)
    return lengths.astype(jnp.int32)


def level_of(stream_key, extent, cuts, smallest, top_value):
    level = 1.0
    for dim, shards_of in cuts:
        draws = jax.random.uniform(jax.random.fold_in(jax.random.fold_in(stream_key, 6), dim), (shards_of,), jnp.float32, smallest / len(cuts), top_value / len(cuts))
        level = level * jnp.repeat(jnp.exp(draws), extent[dim] // shards_of).reshape((-1,) + (1,) * (len(extent) - 1 - dim))
    return level


def centred(key, shape, width, bound, cuts=(), held_as=jnp.bfloat16):
    gain = level_of(key, shape, cuts, -0.22, 0.18) if cuts else 1.0
    entries = jax.random.normal(key, shape, jnp.float32) * width * gain
    return jnp.minimum(jnp.maximum(entries, -bound), bound).astype(held_as)


def setup_inputs(seed: int = 0) -> dict:
    streams_of = jax.random.split(jax.random.key(seed), 15)
    span_queries = draw_span_queries(jax.random.fold_in(streams_of[14], 71), 0)
    span_keys = centred(streams_of[1], (POOLS, SPAN, KVH * HD), 1.2, 7.0, ((0, 2), (1, 16), (2, 8)))
    span_values = centred(streams_of[2], (POOLS, SPAN, KVH * HD), 1.0, 6.0, ((0, 2), (1, 16), (2, 8)))
    prompt_keys = draw_prompt_keys(jax.random.fold_in(streams_of[14], 71), 0)
    prompt_values = centred(streams_of[4], (POOLS, PROMPT, KVH * HD), 1.0, 6.0, ((0, 2), (1, 16), (2, 8)))
    block_owner = draw_block_owner(jax.random.fold_in(streams_of[14], 71), 0)
    block_slot = draw_block_slot(jax.random.fold_in(streams_of[14], 71), 0)
    decode_queries = draw_decode_queries(jax.random.fold_in(streams_of[14], 71), 0)
    decode_new_keys = centred(streams_of[8], (POOLS, ROWS, STEPS, KVH * HD), 1.5, 8.0, ((0, 2), (1, 16), (3, 8)))
    decode_new_values = centred(streams_of[9], (POOLS, ROWS, STEPS, KVH * HD), 1.0, 6.0, ((0, 2), (1, 16), (3, 8)))
    cache_keys = draw_cache_keys(jax.random.fold_in(streams_of[14], 71), 0)
    cache_values = centred(streams_of[11], (POOLS, ROWS, CACHE, KVH * HD), 1.0, 6.0, ((0, 2), (1, 16), (3, 8)))
    cache_len = draw_cache_len(jax.random.fold_in(streams_of[14], 71), 0)
    out_weight = centred(streams_of[13], (HEADS * HD, O_COLS), (HEADS * HD) ** -0.5, 0.0625, ((0, 8),))
    return {"span_queries": span_queries, "span_keys": span_keys, "span_values": span_values, "prompt_keys": prompt_keys, "prompt_values": prompt_values, "block_owner": block_owner, "block_slot": block_slot, "decode_queries": decode_queries, "decode_new_keys": decode_new_keys, "decode_new_values": decode_new_values, "cache_keys": cache_keys, "cache_values": cache_values, "cache_len": cache_len, "out_weight": out_weight}


def prefill_pool(queries, prompt_k, prompt_v, span_k, span_v):
    group_size = HEADS // KVH
    score_scale = HD ** -0.5
    key_total = PROMPT + SPAN
    key_rows = jnp.concatenate([prompt_k, span_k], axis=0).reshape(key_total, KVH, HD).astype(jnp.float32)
    value_rows = jnp.concatenate([prompt_v, span_v], axis=0).reshape(key_total, KVH, HD).astype(jnp.float32)
    block_width = min(16, SPAN)
    query_blocks = queries.reshape(SPAN // block_width, block_width, KVH, group_size, HD)
    key_pos = jnp.arange(key_total, dtype=jnp.int32)

    def handle(inputs):
        query_block, block_index = inputs
        query_pos = PROMPT + block_index * block_width + jnp.arange(block_width, dtype=jnp.int32)
        scores = jnp.einsum("tkgd,skd->tkgs", query_block.astype(jnp.float32), key_rows) * score_scale
        visible = (key_pos[None, :] <= query_pos[:, None])[:, None, None, :]
        scores = jnp.where(visible, scores, -1e30)
        highest = jnp.max(scores, axis=-1, keepdims=True)
        weights = jnp.where(visible, jnp.exp(scores - highest), 0.0)
        weight_sum = jnp.sum(weights, axis=-1)
        rounded = lax.optimization_barrier(weights.astype(jnp.bfloat16)).astype(jnp.float32)
        blended = jnp.einsum("tkgs,skd->tkgd", rounded, value_rows)
        return (blended / weight_sum[..., None]).astype(jnp.bfloat16).reshape(block_width, HEADS * HD)

    outputs = lax.map(handle, (query_blocks, jnp.arange(SPAN // block_width, dtype=jnp.int32)))
    return outputs.reshape(SPAN, HEADS * HD)


def decode_replica(inputs):
    queries, cache_k, cache_v, lengths, slot_k, slot_v, occupied, new_k, new_v = inputs
    group_size = HEADS // KVH
    score_scale = HD ** -0.5
    query_rows = queries.reshape(DEC_ROWS, STEPS, KVH, group_size, HD).astype(jnp.float32)
    cache_kf = cache_k.reshape(DEC_ROWS, CACHE, KVH, HD).astype(jnp.float32)
    cache_vf = cache_v.reshape(DEC_ROWS, CACHE, KVH, HD).astype(jnp.float32)
    slot_kf = slot_k.astype(jnp.float32)
    slot_vf = slot_v.astype(jnp.float32)
    new_kf = new_k.reshape(DEC_ROWS, STEPS, KVH, HD).astype(jnp.float32)
    new_vf = new_v.reshape(DEC_ROWS, STEPS, KVH, HD).astype(jnp.float32)
    score_cache = jnp.einsum("rtkgd,rckd->rtkgc", query_rows, cache_kf) * score_scale
    score_slot = jnp.einsum("rtkgd,skd->rtkgs", query_rows, slot_kf) * score_scale
    score_new = jnp.einsum("rtkgd,rukd->rtkgu", query_rows, new_kf) * score_scale
    see_cache = (jnp.arange(CACHE, dtype=jnp.int32)[None, :] < lengths[:, None])[:, None, None, None, :]
    see_slot = occupied[None, None, None, None, :]
    step_ids = jnp.arange(STEPS, dtype=jnp.int32)
    see_new = (step_ids[None, :] <= step_ids[:, None])[None, :, None, None, :]
    score_cache = jnp.where(see_cache, score_cache, -1e30)
    score_slot = jnp.where(see_slot, score_slot, -1e30)
    score_new = jnp.where(see_new, score_new, -1e30)
    highest = jnp.maximum(jnp.maximum(jnp.max(score_cache, axis=-1), jnp.max(score_slot, axis=-1)), jnp.max(score_new, axis=-1))
    weight_cache = jnp.where(see_cache, jnp.exp(score_cache - highest[..., None]), 0.0)
    weight_slot = jnp.where(see_slot, jnp.exp(score_slot - highest[..., None]), 0.0)
    weight_new = jnp.where(see_new, jnp.exp(score_new - highest[..., None]), 0.0)
    weight_sum = jnp.sum(weight_cache, axis=-1) + jnp.sum(weight_slot, axis=-1) + jnp.sum(weight_new, axis=-1)
    round_cache = lax.optimization_barrier(weight_cache.astype(jnp.bfloat16)).astype(jnp.float32)
    round_slot = lax.optimization_barrier(weight_slot.astype(jnp.bfloat16)).astype(jnp.float32)
    round_new = lax.optimization_barrier(weight_new.astype(jnp.bfloat16)).astype(jnp.float32)
    blended = jnp.einsum("rtkgc,rckd->rtkgd", round_cache, cache_vf)
    blended = blended + jnp.einsum("rtkgs,skd->rtkgd", round_slot, slot_vf)
    blended = blended + jnp.einsum("rtkgu,rukd->rtkgd", round_new, new_vf)
    return (blended / weight_sum[..., None]).astype(jnp.bfloat16).reshape(DEC_ROWS, STEPS, HEADS * HD)


def reference(span_queries, span_keys, span_values, prompt_keys, prompt_values, block_owner, block_slot, decode_queries, decode_new_keys, decode_new_values, cache_keys, cache_values, cache_len, out_weight):
    prefill_list = []
    decode_list = []
    for pool_index in range(POOLS):
        attention = prefill_pool(span_queries[pool_index], prompt_keys[pool_index], prompt_values[pool_index], span_keys[pool_index], span_values[pool_index])
        prefill_list.append(jnp.dot(attention, out_weight, preferred_element_type=jnp.float32).astype(jnp.bfloat16))
        source_pool = POOLS - 1 - pool_index
        owner_ids = block_owner[source_pool]
        slot_ids = block_slot[source_pool]
        matches = (owner_ids[None, None, :] == jnp.arange(N_CTX, dtype=jnp.int32)[:, None, None]) & (slot_ids[None, None, :] == jnp.arange(SLOTS, dtype=jnp.int32)[None, :, None])
        picker = matches.astype(jnp.float32)
        flat_keys = span_keys[source_pool].reshape(KB, BLOCK * KVH * HD).astype(jnp.float32)
        flat_values = span_values[source_pool].reshape(KB, BLOCK * KVH * HD).astype(jnp.float32)
        slot_k = jnp.einsum("rsb,bx->rsx", picker, flat_keys).astype(jnp.bfloat16).reshape(N_CTX, SLOTS * BLOCK, KVH, HD)
        slot_v = jnp.einsum("rsb,bx->rsx", picker, flat_values).astype(jnp.bfloat16).reshape(N_CTX, SLOTS * BLOCK, KVH, HD)
        occupied = jnp.repeat(jnp.any(matches, axis=2), BLOCK, axis=1)
        inputs = (
            decode_queries[pool_index].reshape(N_CTX, DEC_ROWS, STEPS, HEADS * HD),
            cache_keys[pool_index].reshape(N_CTX, DEC_ROWS, CACHE, KVH * HD),
            cache_values[pool_index].reshape(N_CTX, DEC_ROWS, CACHE, KVH * HD),
            cache_len[pool_index].reshape(N_CTX, DEC_ROWS),
            slot_k,
            slot_v,
            occupied,
            decode_new_keys[pool_index].reshape(N_CTX, DEC_ROWS, STEPS, KVH * HD),
            decode_new_values[pool_index].reshape(N_CTX, DEC_ROWS, STEPS, KVH * HD),
        )
        attention_dec = lax.map(decode_replica, inputs).reshape(ROWS * STEPS, HEADS * HD)
        projected = jnp.dot(attention_dec, out_weight, preferred_element_type=jnp.float32).astype(jnp.bfloat16)
        decode_list.append(projected.reshape(ROWS, STEPS, O_COLS))
    return jnp.stack(prefill_list), jnp.stack(decode_list)
```

```python
import math

import jax
import jax.numpy as jnp
from jax import lax
from jax.experimental import pallas as pl
from jax.experimental.pallas import tpu as pltpu
from jax.sharding import PartitionSpec as P

HD = 128
BLOCK = 16
SLOTS = 8
HEADS_DEV = 8
PIECES = 8
NEG = -1e30
SCALE2 = HD**-0.5 * math.log2(math.e)
MESH = pl.DeviceIdType.MESH
BF = jnp.bfloat16
F32 = jnp.float32


def dot_nt(a, b):
    return lax.dot_general(a, b, (((1,), (1,)), ((), ())), preferred_element_type=F32)


def dot_nn(a, b):
    return jnp.dot(a, b, preferred_element_type=F32)


def split_query(q):
    scaled = q.astype(F32) * SCALE2
    high = scaled.astype(BF)
    low = (scaled - high.astype(F32)).astype(BF)
    return jnp.concatenate([high, low], axis=1)


def kernel(
    ring, tp_count,
    q_ref, sk_ref, sv_ref, pk_ref, pv_ref, owner_ref, slot_ref, dq_ref, dk_ref, dv_ref, ck_hbm, cv_hbm, len_ref, w_hbm,
    pout_ref, dout_ref,
    qall, skv, skv_par, gath, rel, par, k_own, v_own, k_par, v_par,
    acc, mx, sm, in_m, in_l, obuf, sbuf, oin, sin,
    w, ck, cv, att, part, got,
    q_send, q_recv, s_send, s_recv, sp_send, sp_recv, g_send, g_recv, r_send, r_recv, f_send, f_recv,
    o_send, o_recv, st_send, st_recv, p_send, p_recv, load,
):
    me = lax.axis_index("ctx")
    pool = lax.axis_index("grp")
    tp = lax.axis_index("tp")
    y_hi = me // ring
    z = me % ring
    y = y_hi * 2 + pool
    tokens = q_ref.shape[0]
    rows = tokens * HEADS_DEV
    prompt = pk_ref.shape[0]
    chunk = prompt // 4

    def along_z(step):
        return {"ctx": y_hi * ring + (z + step + ring) % ring}

    def along_y(step):
        there = (y + step + 4) % 4
        return {"ctx": (there // 2) * ring + z, "grp": there % 2}

    def remote(src, dst, send, recv, device):
        return pltpu.make_async_remote_copy(
            src_ref=src, dst_ref=dst, send_sem=send, recv_sem=recv, device_id=device, device_id_type=MESH
        )

    barrier = pltpu.get_barrier_semaphore()
    for device in (along_z(1), along_z(-1), along_y(1), along_y(-1)):
        pl.semaphore_signal(barrier, inc=1, device_id=device, device_id_type=MESH)
    for k in range(1, tp_count):
        pl.semaphore_signal(barrier, inc=1, device_id={"tp": (tp + k) % tp_count}, device_id_type=MESH)
    pl.semaphore_wait(barrier, 4 + tp_count - 1)

    def way(i):
        return 2 * (i % 2) - 1

    def source_z(i):
        return (z - way(i) * ((i + 1) // 2) + ring) % ring

    def query_copy(i, src):
        return remote(src, qall.at[i], q_send.at[i], q_recv.at[i], along_z(way(i)))

    def span_copy(k):
        return remote(skv, gath.at[z, y_hi], s_send.at[k], s_recv.at[k], along_y(1 - 2 * k))

    def span_relay():
        return remote(gath.at[z, ((y + 3) % 4) // 2], skv_par, sp_send.at[0], sp_recv.at[0], along_y(1))

    def gather_copy(i, at):
        return remote(gath.at[at], gath.at[at], g_send.at[i], g_recv.at[i], along_z(way(i)))

    def piece_rows(p):
        return (p % 2) * 2 * chunk + (p // 4) * chunk

    def piece_copy(p):
        src = (pk_ref if (p // 2) % 2 == 0 else pv_ref).at[pl.ds(piece_rows(p), chunk)]
        return remote(src, rel.at[p], r_send.at[p], r_recv.at[p], along_y(1 - 2 * (p % 2)))

    def piece_relay(p):
        return remote(rel.at[p], par.at[p], f_send.at[p], f_recv.at[p], along_y(1 - 2 * (p % 2)))

    def forward_piece(p):
        remote(rel.at[p], rel.at[p], r_send.at[p], r_recv.at[p], along_y(1)).wait_recv()
        piece_relay(p).start()

    query_copy(1, q_ref).start()
    query_copy(2, q_ref).start()
    skv[0:tokens, :] = sk_ref[...]
    skv[tokens : 2 * tokens, :] = sv_ref[...]
    span_copy(0).start()
    span_copy(1).start()
    for p in range(PIECES):
        piece_copy(p).start()
    loads = [
        pltpu.make_async_copy(ck_hbm, ck, load.at[0]),
        pltpu.make_async_copy(cv_hbm, cv, load.at[1]),
        pltpu.make_async_copy(w_hbm, w, load.at[2]),
    ]
    for item in loads:
        item.start()

    qall[0] = q_ref[...]
    k_own[:, 0:HD] = pk_ref[...]
    k_own[:, HD : 2 * HD] = pk_ref[...]
    v_own[:, 0:HD] = pv_ref[...]
    v_own[:, HD : 2 * HD] = jnp.ones((prompt, HD), BF)
    v_par[:, HD : 2 * HD] = jnp.ones((v_par.shape[0], HD), BF)

    half_heads = HEADS_DEV // 2
    half = tokens * half_heads

    def unit_queries(i, b):
        parts = [qall[i, :, (b * half_heads + h) * HD : (b * half_heads + h + 1) * HD] for h in range(half_heads)]
        return split_query(jnp.concatenate(parts, axis=0))

    def attend_own(i):
        for b in range(2):
            at = pl.ds(b * half, half)
            scores = dot_nt(unit_queries(i, b), k_own[...])
            top = jnp.max(scores, axis=1, keepdims=True)
            out = dot_nn(jnp.exp2(scores - top).astype(BF), v_own[...])
            mx[i, at, :] = jnp.broadcast_to(top, (half, HD))
            acc[i, at, :] = out[:, 0:HD]
            sm[i, at, :] = out[:, HD : 2 * HD]

    def attend_partner(i):
        query_ctx = y_hi * ring + source_z(i)
        partner = (1 - y_hi) * ring + z
        for b in range(2):
            at = pl.ds(b * half, half)
            scores = dot_nt(unit_queries(i, b), k_par[...])
            token = lax.broadcasted_iota(jnp.int32, (half, 2 * tokens), 0) % tokens
            key = lax.broadcasted_iota(jnp.int32, (half, 2 * tokens), 1)
            key_pos = jnp.where(key < tokens, me * tokens + key, partner * tokens + key - tokens)
            span = jnp.where(key_pos <= query_ctx * tokens + token, scores[:, prompt:], NEG)
            before = mx[i, at, 0:1]
            top = jnp.maximum(
                jnp.max(scores[:, 0:prompt], axis=1, keepdims=True), jnp.max(span, axis=1, keepdims=True)
            )
            top = jnp.maximum(top, before)
            weights = jnp.concatenate(
                [jnp.exp2(scores[:, 0:prompt] - top).astype(BF), jnp.exp2(span - top).astype(BF)], axis=1
            )
            out = dot_nn(weights, v_par[...])
            keep = jnp.exp2(before - top)
            mx[i, at, :] = jnp.broadcast_to(top, (half, HD))
            acc[i, at, :] = acc[i, at, :] * keep + out[:, 0:HD]
            sm[i, at, :] = sm[i, at, :] * keep + out[:, HD : 2 * HD]

    attend_own(0)

    for k in range(2):
        span_copy(k).wait_recv()
    span_relay().start()
    gather_copy(1, z).start()
    gather_copy(2, z).start()

    def own_step(i, carry):
        query_copy(i, qall.at[i]).wait_recv()

        @pl.when(i + 2 < ring)
        def _():
            query_copy(i + 2, qall.at[i]).start()

        attend_own(i)
        forward_piece(i - 1)
        at = source_z(i)
        gather_copy(i, at).wait_recv()

        @pl.when(i + 2 < ring)
        def _():
            gather_copy(i + 2, at).start()

        return carry

    lax.fori_loop(1, ring, own_step, 0)
    for p in range(ring - 1, PIECES):
        forward_piece(p)

    def project(which):
        width = part.shape[3]
        each = tokens // tp_count
        step = min(512, width)

        def columns(j, carry):
            at = pl.multiple_of(j * step, step)
            first = dot_nn(att[...], w[:, pl.ds(at, step)])
            second = dot_nn(att[...], w[:, pl.ds(pl.multiple_of(at + width, step), step)])
            for k in range(tp_count):
                rows_of = slice(k * each, (k + 1) * each)
                part[which, k, :, pl.ds(at, step)] = jnp.concatenate([first[rows_of], second[rows_of]], axis=0).astype(BF)
            return carry

        lax.fori_loop(0, width // step, columns, 0)

    def sum_copy(which, k):
        there = (tp + k) % tp_count
        return remote(part.at[which, there], got.at[which, k], p_send.at[which, k], p_recv.at[which, k], {"tp": there})

    def send_sums(which):
        for k in range(1, tp_count):
            sum_copy(which, k).start()

    def finish_sums(which, out_ref):
        each = tokens // tp_count
        total = part[which, tp].astype(F32)
        for k in range(1, tp_count):
            sum_copy(which, k).wait_recv()
            total = total + got[which, k].astype(F32)
        width = part.shape[3]
        out_ref[:, 0:width] = total[0:each].astype(BF)
        out_ref[:, width : 2 * width] = total[each : 2 * each].astype(BF)

    for item in loads:
        item.wait()

    ctx_count = 2 * ring
    span_total = ctx_count * tokens
    blocks = owner_ref.shape[1]
    per_dev = tokens // BLOCK
    token_at = lax.broadcasted_iota(jnp.int32, (blocks, span_total), 1)
    block_at = lax.broadcasted_iota(jnp.int32, (blocks, span_total), 0)
    ring_at = token_at // (2 * tokens)
    side_at = (token_at // tokens) % 2
    block_of = (side_at * ring + ring_at) * per_dev + (token_at % tokens) // BLOCK
    expand = jnp.where(block_of == block_at, 1.0, 0.0).astype(BF)
    other = 1 - pool
    owner_row = jnp.where(other == 0, owner_ref[0:1, :], owner_ref[1:2, :])
    slot_row = jnp.where(other == 0, slot_ref[0:1, :], slot_ref[1:2, :])
    owners = dot_nn(jnp.broadcast_to(owner_row, (8, blocks)).astype(F32).astype(BF), expand)[0:1, :]
    slots = dot_nn(jnp.broadcast_to(slot_row, (8, blocks)).astype(F32).astype(BF), expand)[0:1, :]
    slot_tokens = SLOTS * BLOCK
    place = lax.broadcasted_iota(jnp.int32, (slot_tokens, span_total), 0)
    source = lax.broadcasted_iota(jnp.int32, (slot_tokens, span_total), 1)
    chosen = (
        (owners == me.astype(F32))
        & (slots == (place // BLOCK).astype(F32))
        & (place % BLOCK == source % BLOCK)
    )
    picked = jnp.where(chosen, 1.0, 0.0).astype(BF)
    gath_k = gath[:, :, 0:tokens, :].reshape(span_total, HD)
    gath_v = gath[:, :, tokens : 2 * tokens, :].reshape(span_total, HD)
    slot_k = dot_nn(picked, gath_k).astype(BF)
    slot_v = dot_nn(picked, gath_v).astype(BF)
    filled = dot_nt(jnp.ones((8, span_total), BF), picked)[0:1, :]

    steps = 4
    group = BLOCK // steps
    cache = ck.shape[1]
    new_pad = jnp.zeros((HD - dk_ref.shape[0], HD), BF)
    dec_rows = HEADS_DEV * BLOCK
    row_id = lax.broadcasted_iota(jnp.int32, (dec_rows, HD), 0)
    col_id = lax.broadcasted_iota(jnp.int32, (dec_rows, HD), 1)
    crow_id = lax.broadcasted_iota(jnp.int32, (dec_rows, group * cache), 0)
    ccol_id = lax.broadcasted_iota(jnp.int32, (dec_rows, group * cache), 1)

    def decode_group(g, carry):
        at = pl.ds(pl.multiple_of(g * BLOCK, BLOCK), BLOCK)
        queries = split_query(
            jnp.concatenate([dq_ref[at, h * HD : (h + 1) * HD] for h in range(HEADS_DEV)], axis=0)
        )
        keys = jnp.concatenate(
            [ck[pl.ds(g * group, group)].reshape(group * cache, HD), slot_k, dk_ref[...], new_pad], axis=0
        )
        values = jnp.concatenate(
            [cv[pl.ds(g * group, group)].reshape(group * cache, HD), slot_v, dv_ref[...], new_pad], axis=0
        )
        scores = dot_nt(queries, jnp.concatenate([keys, keys], axis=1))
        live = jnp.zeros((dec_rows, group * cache), jnp.int32)
        for r in range(group):
            live = jnp.where(ccol_id // cache == r, len_ref[0, g * group + r], live)
        own_row = (crow_id % BLOCK) // steps == ccol_id // cache
        s_cache = jnp.where(own_row & (ccol_id % cache < live), scores[:, 0 : group * cache], NEG)
        s_slot = jnp.where(filled > 0.5, scores[:, group * cache : group * cache + slot_tokens], NEG)
        here = g * BLOCK + row_id % BLOCK
        see_new = (here // steps == col_id // steps) & (col_id % steps <= here % steps)
        s_new = jnp.where(see_new, scores[:, group * cache + slot_tokens :], NEG)
        masked = jnp.concatenate([s_cache, s_slot, s_new], axis=1)
        top = jnp.max(masked, axis=1, keepdims=True)
        weights = jnp.exp2(masked - top)
        total = jnp.sum(weights, axis=1, keepdims=True)
        out = (dot_nn(weights.astype(BF), values) / total).astype(BF)
        for h in range(HEADS_DEV):
            att[at, h * HD : (h + 1) * HD] = out[h * BLOCK : (h + 1) * BLOCK]
        return carry

    lax.fori_loop(0, dq_ref.shape[0] // BLOCK, decode_group, 0)
    project(1)
    send_sums(1)

    span_relay().wait_recv()
    for p in range(PIECES):
        piece_relay(p).wait_recv()
        at = pl.ds(piece_rows(p), chunk)
        if (p // 2) % 2 == 0:
            k_par[at, 0:HD] = par[p]
            k_par[at, HD : 2 * HD] = par[p]
        else:
            v_par[at, 0:HD] = par[p]
    for c in range(2):
        k_par[prompt : prompt + tokens, c * HD : (c + 1) * HD] = sk_ref[...]
        k_par[prompt + tokens : prompt + 2 * tokens, c * HD : (c + 1) * HD] = skv_par[0:tokens, :]
    v_par[prompt : prompt + tokens, 0:HD] = sv_ref[...]
    v_par[prompt + tokens : prompt + 2 * tokens, 0:HD] = skv_par[tokens : 2 * tokens, :]

    def out_copy(i):
        return remote(obuf.at[i], oin.at[i], o_send.at[i], o_recv.at[i], along_z(-way(i)))

    def stat_copy(i):
        return remote(sbuf.at[i], sin.at[i], st_send.at[i], st_recv.at[i], along_z(-way(i)))

    lane = lax.broadcasted_iota(jnp.int32, (8, HD), 1)
    groups = tokens // 8

    def merge(i, box):
        out_copy(box).wait_recv()
        stat_copy(box).wait_recv()
        stats = sin[box]
        for h in range(HEADS_DEV):
            for g in range(groups):
                at = slice(h * tokens + g * 8, h * tokens + g * 8 + 8)
                a = g * 16 + h
                in_m[at, :] = jnp.broadcast_to(stats[:, a : a + 1], (8, HD))
                in_l[at, :] = jnp.broadcast_to(stats[:, a + 8 : a + 9], (8, HD))
        top = jnp.maximum(mx[i], in_m[...])
        keep = jnp.exp2(mx[i] - top)
        add = jnp.exp2(in_m[...] - top)
        acc[i] = acc[i] * keep + oin[box].astype(F32) * add
        sm[i] = sm[i] * keep + in_l[...] * add
        mx[i] = top

    def pack(i):
        obuf[i] = acc[i].astype(BF)
        stats = jnp.zeros((8, HD), F32)
        for h in range(HEADS_DEV):
            for g in range(groups):
                at = pl.ds(h * tokens + g * 8, 8)
                a = g * 16 + h
                stats = jnp.where(lane == a, mx[i, at, :], stats)
                stats = jnp.where(lane == a + 8, sm[i, at, :], stats)
        sbuf[i] = stats

    def partner_step(n, carry):
        i = ring - 1 - n
        attend_partner(i)

        @pl.when(i + 2 < ring)
        def _():
            merge(i, i + 2)

        pack(i)
        out_copy(i).start()
        stat_copy(i).start()
        return carry

    lax.fori_loop(0, ring - 1, partner_step, 0)
    attend_partner(0)
    merge(0, 1)
    merge(0, 2)
    done = (acc[0] / sm[0]).astype(BF)
    for h in range(HEADS_DEV):
        att[:, h * HD : (h + 1) * HD] = done[h * tokens : (h + 1) * tokens]
    project(0)
    send_sums(0)
    finish_sums(1, dout_ref)
    finish_sums(0, pout_ref)

    query_copy(1, q_ref).wait_send()
    query_copy(2, q_ref).wait_send()
    for i in range(3, ring):
        query_copy(i, qall.at[i]).wait_send()
    for k in range(2):
        span_copy(k).wait_send()
    span_relay().wait_send()
    for i in range(1, ring):
        gather_copy(i, z).wait_send()
        out_copy(i).wait_send()
        stat_copy(i).wait_send()
    for p in range(PIECES):
        piece_copy(p).wait_send()
        piece_relay(p).wait_send()
    for which in range(2):
        for k in range(1, tp_count):
            sum_copy(which, k).wait_send()


def on_device(
    span_queries,
    span_keys,
    span_values,
    prompt_keys,
    prompt_values,
    block_owner,
    block_slot,
    decode_queries,
    decode_new_keys,
    decode_new_values,
    cache_keys,
    cache_values,
    cache_len,
    out_weight,
):
    ring = lax.axis_size("ctx") // 2
    tp_count = lax.axis_size("tp")
    tokens = span_queries.shape[1]
    width = span_queries.shape[2]
    prompt = prompt_keys.shape[1]
    row_count, step_count = decode_queries.shape[1:3]
    cache = cache_keys.shape[2]
    columns = out_weight.shape[1]
    rows = tokens * HEADS_DEV
    each = tokens // tp_count
    vmem = pl.BlockSpec(memory_space=pltpu.VMEM)
    smem = pl.BlockSpec(memory_space=pltpu.SMEM)
    anywhere = pl.BlockSpec(memory_space=pl.ANY)
    dma = pltpu.SemaphoreType.DMA
    prefill, decode = pl.pallas_call(
        lambda *refs: kernel(ring, tp_count, *refs),
        out_shape=(
            jax.ShapeDtypeStruct((each, columns), BF),
            jax.ShapeDtypeStruct((each, columns), BF),
        ),
        in_specs=[vmem] * 10 + [anywhere, anywhere, smem, anywhere],
        out_specs=(vmem, vmem),
        scratch_shapes=[
            pltpu.VMEM((ring, tokens, width), BF),
            pltpu.VMEM((2 * tokens, HD), BF),
            pltpu.VMEM((2 * tokens, HD), BF),
            pltpu.VMEM((ring, 2, 2 * tokens, HD), BF),
            pltpu.VMEM((PIECES, prompt // 4, HD), BF),
            pltpu.VMEM((PIECES, prompt // 4, HD), BF),
            pltpu.VMEM((prompt, 2 * HD), BF),
            pltpu.VMEM((prompt, 2 * HD), BF),
            pltpu.VMEM((prompt + 2 * tokens, 2 * HD), BF),
            pltpu.VMEM((prompt + 2 * tokens, 2 * HD), BF),
            pltpu.VMEM((ring, rows, HD), F32),
            pltpu.VMEM((ring, rows, HD), F32),
            pltpu.VMEM((ring, rows, HD), F32),
            pltpu.VMEM((rows, HD), F32),
            pltpu.VMEM((rows, HD), F32),
            pltpu.VMEM((ring, rows, HD), BF),
            pltpu.VMEM((ring, 8, HD), F32),
            pltpu.VMEM((ring, rows, HD), BF),
            pltpu.VMEM((ring, 8, HD), F32),
            pltpu.VMEM((width, columns), BF),
            pltpu.VMEM((row_count, cache, HD), BF),
            pltpu.VMEM((row_count, cache, HD), BF),
            pltpu.VMEM((tokens, width), BF),
            pltpu.VMEM((2, tp_count, 2 * each, columns // 2), BF),
            pltpu.VMEM((2, tp_count, 2 * each, columns // 2), BF),
            dma((ring,)),
            dma((ring,)),
            dma((2,)),
            dma((2,)),
            dma((1,)),
            dma((1,)),
            dma((ring,)),
            dma((ring,)),
            dma((PIECES,)),
            dma((PIECES,)),
            dma((PIECES,)),
            dma((PIECES,)),
            dma((ring,)),
            dma((ring,)),
            dma((ring,)),
            dma((ring,)),
            dma((2, tp_count)),
            dma((2, tp_count)),
            dma((3,)),
        ],
        compiler_params=pltpu.CompilerParams(
            collective_id=0, has_side_effects=True, vmem_limit_bytes=60 * 1024 * 1024
        ),
        name="serve",
    )(
        span_queries[0],
        span_keys[0],
        span_values[0],
        prompt_keys[0],
        prompt_values[0],
        block_owner,
        block_slot,
        decode_queries.reshape(row_count * step_count, width),
        decode_new_keys.reshape(row_count * step_count, HD),
        decode_new_values.reshape(row_count * step_count, HD),
        cache_keys[0],
        cache_values[0],
        cache_len,
        out_weight,
    )
    return (prefill[None], decode.reshape(1, row_count // tp_count, step_count, columns))


def solution(mesh):
    in_specs = (
        P("grp", "ctx", "tp"),
        P("grp", "ctx", "tp"),
        P("grp", "ctx", "tp"),
        P("grp", "ctx", "tp"),
        P("grp", "ctx", "tp"),
        P(),
        P(),
        P("grp", "ctx", None, "tp"),
        P("grp", "ctx", None, "tp"),
        P("grp", "ctx", None, "tp"),
        P("grp", "ctx", None, "tp"),
        P("grp", "ctx", None, "tp"),
        P("grp", "ctx"),
        P("tp", None),
    )
    out_specs = (P("grp", ("ctx", "tp"), None), P("grp", ("ctx", "tp"), None, None))
    return jax.shard_map(
        on_device, mesh=mesh, in_specs=in_specs, out_specs=out_specs, check_vma=False
    )
```

```python
import math

import jax
import jax.numpy as jnp
from jax import lax
from jax.experimental import pallas as pl
from jax.experimental.pallas import tpu as pltpu
from jax.sharding import PartitionSpec as P

HD = 128
BLOCK = 16
SLOTS = 8
HEADS_DEV = 8
PIECES = 8
NEG = -1e30
SCALE2 = HD**-0.5 * math.log2(math.e)
MESH = pl.DeviceIdType.MESH
BF = jnp.bfloat16
F32 = jnp.float32


def dot_nt(a, b):
    return lax.dot_general(a, b, (((1,), (1,)), ((), ())), preferred_element_type=F32)


def dot_nn(a, b):
    return jnp.dot(a, b, preferred_element_type=F32)


def split_query(q):
    scaled = q.astype(F32) * SCALE2
    high = scaled.astype(BF)
    low = (scaled - high.astype(F32)).astype(BF)
    return jnp.concatenate([high, low], axis=1)


def kernel(
    ring, tp_count,
    q_ref, sk_ref, sv_ref, pk_ref, pv_ref, owner_ref, slot_ref, dq_ref, dk_ref, dv_ref, ck_hbm, cv_hbm, len_ref, w_hbm,
    out_ref,
    qbuf, skv, skv_par, gath, rel, par, k_raw, k_own, v_own, k_first, v_first, k_last, v_last,
    acc, mx, sm, in_m, in_l, obuf, sbuf, oin, sin,
    w, ck, cv, att, part, got,
    q_send, q_recv, s_send, s_recv, sp_send, sp_recv, g_send, g_recv, r_send, r_recv, f_send, f_recv,
    o_send, o_recv, st_send, st_recv, p_send, p_recv, load,
):
    me = lax.axis_index("ctx")
    pool = lax.axis_index("grp")
    tp = lax.axis_index("tp")
    y_hi = me // ring
    z = me % ring
    y = y_hi * 2 + pool
    far = ring // 2
    tokens = sk_ref.shape[0]
    prompt = pk_ref.shape[0]
    chunk = prompt // 4
    half_heads = HEADS_DEV // 2
    half_width = half_heads * HD
    half = tokens * half_heads

    def along_z(step):
        return {"ctx": y_hi * ring + (z + step + ring) % ring}

    def along_y(step):
        there = (y + step + 4) % 4
        return {"ctx": (there // 2) * ring + z, "grp": there % 2}

    def remote(src, dst, send, recv, device):
        return pltpu.make_async_remote_copy(
            src_ref=src, dst_ref=dst, send_sem=send, recv_sem=recv, device_id=device, device_id_type=MESH
        )

    def away(u):
        return 1 - 2 * ((u % 4) // 2)

    def source_z(u):
        return (z - away(u) * (u // 4) + 2 * ring) % ring

    def goes_on(u):
        d, r = u // 4, u % 4
        return jnp.logical_or(d + 1 < far, jnp.logical_and(d + 1 == far, r * (r - 3) == 0))

    def pair(n):
        first = 4 * ((n + 1) // 2) + 2 * ((n + 1) % 2) * ((n + ring - 2) // (ring - 1))
        return first, first + 1 + 2 * (n // (ring - 1))

    sent = [u for u in range(4, 4 * far + 4) if u // 4 < far or u % 4 in (0, 3)]

    def query_copy(u, src):
        return remote(src, qbuf.at[u], q_send.at[u], q_recv.at[u], along_z(away(u)))

    def span_copy(k):
        return remote(skv, gath.at[z, y_hi], s_send.at[k], s_recv.at[k], along_y(1 - 2 * k))

    def span_relay():
        return remote(gath.at[z, ((y + 3) % 4) // 2], skv_par, sp_send.at[0], sp_recv.at[0], along_y(1))

    def gather_copy(i, at):
        return remote(gath.at[at], gath.at[at], g_send.at[i], g_recv.at[i], along_z(2 * (i % 2) - 1))

    def gather_z(i):
        return (z - (2 * (i % 2) - 1) * ((i + 1) // 2) + ring) % ring

    def piece_copy(p):
        src = (pk_ref if (p // 2) % 2 == 0 else pv_ref).at[pl.ds(((p % 2) * 2 + p // 4) * chunk, chunk)]
        return remote(src, rel.at[p], r_send.at[p], r_recv.at[p], along_y(1 - 2 * (p % 2)))

    def piece_relay(p):
        return remote(rel.at[p], par.at[p], f_send.at[p], f_recv.at[p], along_y(1 - 2 * (p % 2)))

    def forward_piece(p):
        remote(rel.at[p], rel.at[p], r_send.at[p], r_recv.at[p], along_y(1)).wait_recv()
        piece_relay(p).start()

    def own_half(b):
        return q_ref.at[:, pl.ds(b * half_width, half_width)]

    loads = [
        pltpu.make_async_copy(pk_ref, k_raw, load.at[0]),
        pltpu.make_async_copy(pv_ref, v_own.at[:, pl.ds(0, HD)], load.at[1]),
        pltpu.make_async_copy(own_half(0), qbuf.at[0], load.at[2]),
        pltpu.make_async_copy(own_half(1), qbuf.at[1], load.at[3]),
        pltpu.make_async_copy(ck_hbm, ck, load.at[4]),
        pltpu.make_async_copy(cv_hbm, cv, load.at[5]),
        pltpu.make_async_copy(w_hbm, w, load.at[6]),
    ]
    for item in loads[:4]:
        item.start()

    barrier = pltpu.get_barrier_semaphore()
    for device in (along_z(1), along_z(-1), along_y(1), along_y(-1)):
        pl.semaphore_signal(barrier, inc=1, device_id=device, device_id_type=MESH)
    for k in range(1, tp_count):
        pl.semaphore_signal(barrier, inc=1, device_id={"tp": (tp + k) % tp_count}, device_id_type=MESH)
    skv[0:tokens, :] = sk_ref[...]
    skv[tokens : 2 * tokens, :] = sv_ref[...]
    pl.semaphore_wait(barrier, 4 + tp_count - 1)

    for u in range(4, 8):
        query_copy(u, own_half(u % 2)).start()
    span_copy(0).start()
    span_copy(1).start()
    for p in range(PIECES):
        piece_copy(p).start()
    for item in loads[4:]:
        item.start()

    v_own[:, HD : 2 * HD] = jnp.ones((prompt, HD), BF)
    v_first[:, HD : 2 * HD] = jnp.ones((v_first.shape[0], HD), BF)
    v_last[:, HD : 2 * HD] = jnp.ones((v_last.shape[0], HD), BF)
    for item in loads[:4]:
        item.wait()

    def put_keys(dst, at, rows):
        turned = rows.T
        size = rows.shape[0]
        dst[0:HD, at : at + size] = turned
        dst[HD : 2 * HD, at : at + size] = turned

    for c in range(4):
        put_keys(k_own, c * chunk, k_raw[c * chunk : (c + 1) * chunk])

    def queries_of(u):
        parts = [qbuf[u, :, h * HD : (h + 1) * HD] for h in range(half_heads)]
        return split_query(jnp.concatenate(parts, axis=0))

    def attend(u, keys, values, fresh, span):
        scores = dot_nn(queries_of(u), keys[...])
        if span:
            query_ctx = y_hi * ring + source_z(u)
            partner = (1 - y_hi) * ring + z
            token = lax.broadcasted_iota(jnp.int32, (half, 2 * tokens), 0) % tokens
            key = lax.broadcasted_iota(jnp.int32, (half, 2 * tokens), 1)
            key_pos = jnp.where(key < tokens, me * tokens + key, partner * tokens + key - tokens)
            seen = jnp.where(key_pos <= query_ctx * tokens + token, scores[:, prompt // 2 :], NEG)
            scores = jnp.concatenate([scores[:, 0 : prompt // 2], seen], axis=1)
        top = jnp.max(scores, axis=1, keepdims=True)
        if not fresh:
            before = mx[u, :, 0:1]
            top = jnp.maximum(top, before)
        out = dot_nn(jnp.exp2(scores - top).astype(BF), values[...])
        if fresh:
            acc[u] = out[:, 0:HD]
            sm[u] = out[:, HD : 2 * HD]
        else:
            keep = jnp.exp2(before - top)
            acc[u] = acc[u] * keep + out[:, 0:HD]
            sm[u] = sm[u] * keep + out[:, HD : 2 * HD]
        mx[u] = jnp.broadcast_to(top, (half, HD))

    def own_step(n, carry):
        halves = pair(n)

        @pl.when(n > 0)
        def _():
            for u in halves:
                query_copy(u, qbuf.at[u]).wait_recv()

                @pl.when(goes_on(u))
                def _():
                    query_copy(u + 4, qbuf.at[u]).start()

        for u in halves:
            attend(u, k_own, v_own, True, False)

        @pl.when(n == 0)
        def _():
            for k in range(2):
                span_copy(k).wait_recv()
            span_relay().start()
            gather_copy(1, z).start()
            gather_copy(2, z).start()

        @pl.when(n > 0)
        def _():
            forward_piece(n - 1)
            at = gather_z(n)
            gather_copy(n, at).wait_recv()

            @pl.when(n + 2 < ring)
            def _():
                gather_copy(n + 2, at).start()

        return carry

    lax.fori_loop(0, ring, own_step, 0)
    for p in range(ring - 1, PIECES):
        forward_piece(p)

    each = tokens // tp_count
    step = part.shape[4]
    width = w.shape[1] // 2

    def sum_copy(which, j, k):
        there = (tp + k) % tp_count
        return remote(
            part.at[which, j, there], got.at[which, j, k], p_send.at[which, j, k], p_recv.at[which, j, k], {"tp": there}
        )

    def project(which):
        def columns(j, carry):
            at = pl.multiple_of(j * step, step)
            first = dot_nn(att[...], w[:, pl.ds(at, step)])
            second = dot_nn(att[...], w[:, pl.ds(pl.multiple_of(at + width, step), step)])
            for k in range(tp_count):
                rows_of = slice(k * each, (k + 1) * each)
                part[which, j, k] = jnp.concatenate([first[rows_of], second[rows_of]], axis=0).astype(BF)
            for k in range(1, tp_count):
                sum_copy(which, j, k).start()
            return carry

        lax.fori_loop(0, width // step, columns, 0)

    def summed(which, j):
        total = part[which, j, tp].astype(F32)
        for k in range(1, tp_count):
            sum_copy(which, j, k).wait_recv()
            total = total + got[which, j, k].astype(F32)
        return total

    for item in loads[4:]:
        item.wait()

    ctx_count = 2 * ring
    span_total = ctx_count * tokens
    blocks = owner_ref.shape[1]
    per_dev = tokens // BLOCK
    token_at = lax.broadcasted_iota(jnp.int32, (blocks, span_total), 1)
    block_at = lax.broadcasted_iota(jnp.int32, (blocks, span_total), 0)
    ring_at = token_at // (2 * tokens)
    side_at = (token_at // tokens) % 2
    block_of = (side_at * ring + ring_at) * per_dev + (token_at % tokens) // BLOCK
    expand = jnp.where(block_of == block_at, 1.0, 0.0).astype(BF)
    other = 1 - pool
    owner_row = jnp.where(other == 0, owner_ref[0:1, :], owner_ref[1:2, :])
    slot_row = jnp.where(other == 0, slot_ref[0:1, :], slot_ref[1:2, :])
    owners = dot_nn(jnp.broadcast_to(owner_row, (8, blocks)).astype(F32).astype(BF), expand)[0:1, :]
    slots = dot_nn(jnp.broadcast_to(slot_row, (8, blocks)).astype(F32).astype(BF), expand)[0:1, :]
    slot_tokens = SLOTS * BLOCK
    place = lax.broadcasted_iota(jnp.int32, (slot_tokens, span_total), 0)
    source = lax.broadcasted_iota(jnp.int32, (slot_tokens, span_total), 1)
    chosen = (
        (owners == me.astype(F32))
        & (slots == (place // BLOCK).astype(F32))
        & (place % BLOCK == source % BLOCK)
    )
    picked = jnp.where(chosen, 1.0, 0.0).astype(BF)
    gath_k = gath[:, :, 0:tokens, :].reshape(span_total, HD)
    gath_v = gath[:, :, tokens : 2 * tokens, :].reshape(span_total, HD)
    slot_k = dot_nn(picked, gath_k).astype(BF)
    slot_v = dot_nn(picked, gath_v).astype(BF)
    filled = dot_nt(jnp.ones((8, span_total), BF), picked)[0:1, :]

    steps = 4
    group = BLOCK // steps
    cache = ck.shape[1]
    new_pad = jnp.zeros((HD - dk_ref.shape[0], HD), BF)
    dec_rows = HEADS_DEV * BLOCK
    row_id = lax.broadcasted_iota(jnp.int32, (dec_rows, HD), 0)
    col_id = lax.broadcasted_iota(jnp.int32, (dec_rows, HD), 1)
    crow_id = lax.broadcasted_iota(jnp.int32, (dec_rows, group * cache), 0)
    ccol_id = lax.broadcasted_iota(jnp.int32, (dec_rows, group * cache), 1)

    def decode_group(g, carry):
        at = pl.ds(pl.multiple_of(g * BLOCK, BLOCK), BLOCK)
        asked = dq_ref[pl.ds(g * group, group)].astype(F32).reshape(BLOCK, HEADS_DEV * HD)
        queries = jnp.concatenate([asked[:, h * HD : (h + 1) * HD] for h in range(HEADS_DEV)], axis=0).astype(BF)
        keys = jnp.concatenate(
            [ck[pl.ds(g * group, group)].reshape(group * cache, HD), slot_k, dk_ref[...], new_pad], axis=0
        )
        values = jnp.concatenate(
            [cv[pl.ds(g * group, group)].reshape(group * cache, HD), slot_v, dv_ref[...], new_pad], axis=0
        )
        scores = dot_nt(queries, keys) * SCALE2
        live = jnp.zeros((dec_rows, group * cache), jnp.int32)
        for r in range(group):
            live = jnp.where(ccol_id // cache == r, len_ref[0, g * group + r], live)
        own_row = (crow_id % BLOCK) // steps == ccol_id // cache
        s_cache = jnp.where(own_row & (ccol_id % cache < live), scores[:, 0 : group * cache], NEG)
        s_slot = jnp.where(filled > 0.5, scores[:, group * cache : group * cache + slot_tokens], NEG)
        here = g * BLOCK + row_id % BLOCK
        see_new = (here // steps == col_id // steps) & (col_id % steps <= here % steps)
        s_new = jnp.where(see_new, scores[:, group * cache + slot_tokens :], NEG)
        masked = jnp.concatenate([s_cache, s_slot, s_new], axis=1)
        top = jnp.max(masked, axis=1, keepdims=True)
        weights = jnp.exp2(masked - top)
        total = jnp.sum(weights, axis=1, keepdims=True)
        out = (dot_nn(weights.astype(BF), values) / total).astype(BF)
        for h in range(HEADS_DEV):
            att[at, h * HD : (h + 1) * HD] = out[h * BLOCK : (h + 1) * BLOCK]
        return carry

    lax.fori_loop(0, dq_ref.shape[0] // group, decode_group, 0)
    project(1)

    def place_piece(p, keys, values):
        piece_relay(p).wait_recv()
        at = (p % 2) * chunk
        if (p // 2) % 2 == 0:
            put_keys(keys, at, par[p])
        else:
            values[at : at + chunk, 0:HD] = par[p]

    for p in range(4):
        place_piece(p, k_first, v_first)

    def first_step(n, carry):
        for u in pair(n):
            attend(u, k_first, v_first, False, False)
        return carry

    lax.fori_loop(0, ring, first_step, 0)

    span_relay().wait_recv()
    put_keys(k_last, 2 * chunk, jnp.concatenate([sk_ref[...], skv_par[0:tokens, :]], axis=0))
    v_last[2 * chunk : 2 * chunk + tokens, 0:HD] = sv_ref[...]
    v_last[2 * chunk + tokens : 2 * chunk + 2 * tokens, 0:HD] = skv_par[tokens : 2 * tokens, :]
    for p in range(4, 8):
        place_piece(p, k_last, v_last)

    def out_copy(u):
        return remote(obuf.at[u], oin.at[u], o_send.at[u], o_recv.at[u], along_z(-away(u)))

    def stat_copy(u):
        return remote(sbuf.at[u], sin.at[u], st_send.at[u], st_recv.at[u], along_z(-away(u)))

    lane = lax.broadcasted_iota(jnp.int32, (8, HD), 1)

    def merge(u, box):
        out_copy(box).wait_recv()
        stat_copy(box).wait_recv()
        stats = sin[box]
        for a in range(half // 8):
            in_m[8 * a : 8 * a + 8, :] = jnp.broadcast_to(stats[:, a : a + 1], (8, HD))
            in_l[8 * a : 8 * a + 8, :] = jnp.broadcast_to(stats[:, a + 64 : a + 65], (8, HD))
        top = jnp.maximum(mx[u], in_m[...])
        keep = jnp.exp2(mx[u] - top)
        add = jnp.exp2(in_m[...] - top)
        acc[u] = acc[u] * keep + oin[box].astype(F32) * add
        sm[u] = sm[u] * keep + in_l[...] * add
        mx[u] = top

    def pack(u):
        obuf[u] = acc[u].astype(BF)
        stats = jnp.zeros((8, HD), F32)
        for a in range(half // 8):
            at = pl.ds(8 * a, 8)
            stats = jnp.where(lane == a, mx[u, at, :], stats)
            stats = jnp.where(lane == a + 64, sm[u, at, :], stats)
        sbuf[u] = stats

    def last_step(m, carry):
        n = ring - 1 - m
        halves = pair(n)
        for u in halves:
            attend(u, k_last, v_last, False, True)
        for u in halves:
            @pl.when(goes_on(u))
            def _():
                merge(u, u + 4)

            pack(u)
            out_copy(u).start()
            stat_copy(u).start()
        return carry

    lax.fori_loop(0, ring - 1, last_step, 0)
    for u in range(2):
        attend(u, k_last, v_last, False, True)
    for u in range(2):
        merge(u, u + 4)
        merge(u, u + 6)
        done = (acc[u] / sm[u]).astype(BF)
        for h in range(half_heads):
            column = (u * half_heads + h) * HD
            att[:, column : column + HD] = done[h * tokens : (h + 1) * tokens]
    project(0)
    for j in range(width // step):
        decode_sum = summed(1, j)
        prefill_sum = summed(0, j)
        for c in range(2):
            rows_of = slice(c * each, (c + 1) * each)
            both = jnp.concatenate([prefill_sum[rows_of], decode_sum[rows_of]], axis=0).astype(BF)
            out_ref[:, c * width + j * step : c * width + (j + 1) * step] = both

    for u in sent:
        query_copy(u, qbuf.at[u]).wait_send()
        out_copy(u).wait_send()
        stat_copy(u).wait_send()
    for k in range(2):
        span_copy(k).wait_send()
    span_relay().wait_send()
    for i in range(1, ring):
        gather_copy(i, z).wait_send()
    for p in range(PIECES):
        piece_copy(p).wait_send()
        piece_relay(p).wait_send()
    for which in range(2):
        for j in range(width // step):
            for k in range(1, tp_count):
                sum_copy(which, j, k).wait_send()


def separate(sums_ref, prefill_ref, decode_ref):
    each = prefill_ref.shape[0]
    sums = sums_ref[...].astype(F32)
    prefill_ref[...] = sums[0:each].astype(BF)
    steps = decode_ref.shape[1]
    for r in range(decode_ref.shape[0]):
        decode_ref[r] = sums[each + r * steps : each + (r + 1) * steps].astype(BF)


def on_device(
    span_queries,
    span_keys,
    span_values,
    prompt_keys,
    prompt_values,
    block_owner,
    block_slot,
    decode_queries,
    decode_new_keys,
    decode_new_values,
    cache_keys,
    cache_values,
    cache_len,
    out_weight,
):
    ring = lax.axis_size("ctx") // 2
    tp_count = lax.axis_size("tp")
    tokens = span_queries.shape[1]
    width = span_queries.shape[2]
    prompt = prompt_keys.shape[1]
    row_count, step_count = decode_queries.shape[1:3]
    cache = cache_keys.shape[2]
    columns = out_weight.shape[1]
    each = tokens // tp_count
    count = 4 * (ring // 2) + 4
    half = tokens * HEADS_DEV // 2
    step = min(512, columns // 2)
    blocks = columns // 2 // step
    span = 2 * tokens
    vmem = pl.BlockSpec(memory_space=pltpu.VMEM)
    smem = pl.BlockSpec(memory_space=pltpu.SMEM)
    anywhere = pl.BlockSpec(memory_space=pl.ANY)
    dma = pltpu.SemaphoreType.DMA
    sums = pl.pallas_call(
        lambda *refs: kernel(ring, tp_count, *refs),
        out_shape=jax.ShapeDtypeStruct((2 * each, columns), BF),
        in_specs=[anywhere, vmem, vmem, anywhere, anywhere] + [vmem] * 5 + [anywhere, anywhere, smem, anywhere],
        out_specs=vmem,
        scratch_shapes=[
            pltpu.VMEM((count, tokens, width // 2), BF),
            pltpu.VMEM((span, HD), BF),
            pltpu.VMEM((span, HD), BF),
            pltpu.VMEM((ring, 2, span, HD), BF),
            pltpu.VMEM((PIECES, prompt // 4, HD), BF),
            pltpu.VMEM((PIECES, prompt // 4, HD), BF),
            pltpu.VMEM((prompt, HD), BF),
            pltpu.VMEM((2 * HD, prompt), BF),
            pltpu.VMEM((prompt, 2 * HD), BF),
            pltpu.VMEM((2 * HD, prompt // 2), BF),
            pltpu.VMEM((prompt // 2, 2 * HD), BF),
            pltpu.VMEM((2 * HD, prompt // 2 + span), BF),
            pltpu.VMEM((prompt // 2 + span, 2 * HD), BF),
            pltpu.VMEM((count, half, HD), F32),
            pltpu.VMEM((count, half, HD), F32),
            pltpu.VMEM((count, half, HD), F32),
            pltpu.VMEM((half, HD), F32),
            pltpu.VMEM((half, HD), F32),
            pltpu.VMEM((count, half, HD), BF),
            pltpu.VMEM((count, 8, HD), F32),
            pltpu.VMEM((count, half, HD), BF),
            pltpu.VMEM((count, 8, HD), F32),
            pltpu.VMEM((width, columns), BF),
            pltpu.VMEM((row_count, cache, HD), BF),
            pltpu.VMEM((row_count, cache, HD), BF),
            pltpu.VMEM((tokens, width), BF),
            pltpu.VMEM((2, blocks, tp_count, 2 * each, step), BF),
            pltpu.VMEM((2, blocks, tp_count, 2 * each, step), BF),
            dma((count,)),
            dma((count,)),
            dma((2,)),
            dma((2,)),
            dma((1,)),
            dma((1,)),
            dma((ring,)),
            dma((ring,)),
            dma((PIECES,)),
            dma((PIECES,)),
            dma((PIECES,)),
            dma((PIECES,)),
            dma((count,)),
            dma((count,)),
            dma((count,)),
            dma((count,)),
            dma((2, blocks, tp_count)),
            dma((2, blocks, tp_count)),
            dma((7,)),
        ],
        compiler_params=pltpu.CompilerParams(
            collective_id=0, has_side_effects=True, vmem_limit_bytes=60 * 1024 * 1024
        ),
        name="serve",
    )(
        span_queries[0],
        span_keys[0],
        span_values[0],
        prompt_keys[0],
        prompt_values[0],
        block_owner,
        block_slot,
        decode_queries[0],
        decode_new_keys.reshape(row_count * step_count, HD),
        decode_new_values.reshape(row_count * step_count, HD),
        cache_keys[0],
        cache_values[0],
        cache_len,
        out_weight,
    )
    prefill, decode = pl.pallas_call(
        separate,
        out_shape=(
            jax.ShapeDtypeStruct((each, columns), BF),
            jax.ShapeDtypeStruct((row_count // tp_count, step_count, columns), BF),
        ),
        in_specs=[vmem],
        out_specs=(vmem, vmem),
        name="separate",
    )(sums)
    return (prefill[None], decode[None])


def solution(mesh):
    in_specs = (
        P("grp", "ctx", "tp"),
        P("grp", "ctx", "tp"),
        P("grp", "ctx", "tp"),
        P("grp", "ctx", "tp"),
        P("grp", "ctx", "tp"),
        P(),
        P(),
        P("grp", "ctx", None, "tp"),
        P("grp", "ctx", None, "tp"),
        P("grp", "ctx", None, "tp"),
        P("grp", "ctx", None, "tp"),
        P("grp", "ctx", None, "tp"),
        P("grp", "ctx"),
        P("tp", None),
    )
    out_specs = (P("grp", ("ctx", "tp"), None), P("grp", ("ctx", "tp"), None, None))
    return jax.shard_map(
        on_device, mesh=mesh, in_specs=in_specs, out_specs=out_specs, check_vma=False
    )
```

```python
import math

import jax
import jax.numpy as jnp
from jax import lax
from jax.experimental import pallas as pl
from jax.experimental.pallas import tpu as pltpu
from jax.sharding import PartitionSpec as P

HD = 128
BLOCK = 16
SLOTS = 8
HEADS_DEV = 8
PIECES = 4
TILE = 256
NEG = -1e30
SCALE2 = HD**-0.5 * math.log2(math.e)
MESH = pl.DeviceIdType.MESH
BF = jnp.bfloat16
F32 = jnp.float32


def dot_nt(a, b):
    return lax.dot_general(a, b, (((1,), (1,)), ((), ())), preferred_element_type=F32)


def dot_nn(a, b):
    return jnp.dot(a, b, preferred_element_type=F32)


def split_query(q):
    scaled = q.astype(F32) * SCALE2
    high = scaled.astype(BF)
    low = (scaled - high.astype(F32)).astype(BF)
    return jnp.concatenate([high, low], axis=1)


def low_bits(x, size):
    return jnp.bitwise_and(x, size - 1)


def high_bits(x, size):
    return lax.shift_right_logical(x, size.bit_length() - 1)


def kernel(
    ring, tp_count,
    q_ref, sk_ref, sv_ref, pk_ref, pv_ref, owner_ref, slot_ref, dq_ref, dk_ref, dv_ref, ck_hbm, cv_hbm, len_ref, w_hbm,
    out_ref,
    qbuf, skv, skv_par, gath, rel, par, k_raw, k_own, v_own, k_par, v_par, scores, weights,
    acc, mx, sm, in_m, in_l, obuf, oin,
    w, ck, cv, att, part, sib, pairs, got,
    q_send, q_recv, s_send, s_recv, sp_send, sp_recv, g_send, g_recv, r_send, r_recv, f_send, f_recv,
    o_send, o_recv, c_send, c_recv, p_send, p_recv, load,
):
    me = lax.axis_index("ctx")
    pool = lax.axis_index("grp")
    tp = lax.axis_index("tp")
    core = tp % 2
    chip = tp // 2
    chips = tp_count // 2
    y_hi = me // ring
    z = me % ring
    y = y_hi * 2 + pool
    far = ring // 2
    tokens = sk_ref.shape[0]
    prompt = pk_ref.shape[0]
    chunk = prompt // 2
    half_heads = HEADS_DEV // 2
    half_width = half_heads * HD
    half = tokens * half_heads
    right = y_hi * ring + (z + 1) % ring
    left = y_hi * ring + (z + ring - 1) % ring
    up_y = (y + 1) % 4
    down_y = (y + 3) % 4
    up = {"ctx": (up_y // 2) * ring + z, "grp": up_y % 2}
    down = {"ctx": (down_y // 2) * ring + z, "grp": down_y % 2}

    def remote(src, dst, send, recv, device):
        return pltpu.make_async_remote_copy(
            src_ref=src, dst_ref=dst, send_sem=send, recv_sem=recv, device_id=device, device_id_type=MESH
        )

    def pair(n):
        first = 4 * ((n + 1) // 2) + 2 * ((n + 1) % 2) * ((n + ring - 2) // (ring - 1))
        return first, first + 1 + 2 * (n // (ring - 1))

    def toward(n):
        return {"ctx": left + (right - left) * (n % 2)}

    def back(n):
        return {"ctx": right + (left - right) * (n % 2)}

    def whole_copy(n, src):
        u = pair(n)[0]
        return remote(src, qbuf.at[pl.ds(u, 2)], q_send.at[n], q_recv.at[n], toward(n))

    def half_copy(u, src):
        k = ring - 1 + (u % 4) // 3
        return remote(src, qbuf.at[u], q_send.at[k], q_recv.at[k], {"ctx": right + (left - right) * ((u % 4) // 3)})

    def span_copy(k):
        return remote(skv, gath.at[z, y_hi], s_send.at[k], s_recv.at[k], (up, down)[k])

    def span_relay():
        return remote(gath.at[z, down_y // 2], skv_par, sp_send.at[0], sp_recv.at[0], up)

    def gather_copy(i, at):
        return remote(gath.at[at], gath.at[at], g_send.at[i], g_recv.at[i], toward(i))

    def gather_z(i):
        return (z - (2 * (i % 2) - 1) * ((i + 1) // 2) + ring) % ring

    def piece_copy(p):
        src = (pk_ref if p // 2 == 0 else pv_ref).at[pl.ds((p % 2) * chunk, chunk)]
        return remote(src, rel.at[p], r_send.at[p], r_recv.at[p], (up, down)[p % 2])

    def piece_relay(p):
        return remote(rel.at[p], par.at[p], f_send.at[p], f_recv.at[p], (up, down)[p % 2])

    def forward_piece(p):
        piece_copy(p).wait_recv()
        piece_relay(p).start()

    loads = [
        pltpu.make_async_copy(pk_ref, k_raw, load.at[0]),
        pltpu.make_async_copy(pv_ref, v_own.at[:, pl.ds(0, HD)], load.at[1]),
        pltpu.make_async_copy(q_ref.at[:, pl.ds(0, half_width)], qbuf.at[0], load.at[2]),
        pltpu.make_async_copy(q_ref.at[:, pl.ds(half_width, half_width)], qbuf.at[1], load.at[3]),
        pltpu.make_async_copy(ck_hbm, ck, load.at[4]),
        pltpu.make_async_copy(cv_hbm, cv, load.at[5]),
        pltpu.make_async_copy(w_hbm, w, load.at[6]),
    ]
    for item in loads[:4]:
        item.start()

    other_core = {"tp": tp + 1 - 2 * core}
    other_chips = [{"tp": 2 * ((chip + k) % chips) + core} for k in range(1, chips)]
    barrier = pltpu.get_barrier_semaphore()
    for device in [{"ctx": right}, {"ctx": left}, up, down, other_core] + other_chips:
        pl.semaphore_signal(barrier, inc=1, device_id=device, device_id_type=MESH)
    skv[0:tokens, :] = sk_ref[...]
    skv[tokens : 2 * tokens, :] = sv_ref[...]
    for item in loads[2:4]:
        item.wait()
    pl.semaphore_wait(barrier, 4 + chips)

    whole_copy(1, qbuf.at[pl.ds(0, 2)]).start()
    whole_copy(2, qbuf.at[pl.ds(0, 2)]).start()
    for p in range(PIECES):
        piece_copy(p).start()
    span_copy(0).start()
    span_copy(1).start()
    for item in loads[4:]:
        item.start()

    v_own[:, HD : 2 * HD] = jnp.ones((prompt, HD), BF)
    v_par[:, HD : 2 * HD] = jnp.ones((v_par.shape[0], HD), BF)
    for item in loads[:2]:
        item.wait()

    def put_keys(dst, at, rows):
        turned = rows.T
        size = rows.shape[0]
        dst[0:HD, at : at + size] = turned
        dst[HD : 2 * HD, at : at + size] = turned

    for c in range(4):
        put_keys(k_own, c * (prompt // 4), k_raw[c * (prompt // 4) : (c + 1) * (prompt // 4)])

    def queries_of(u):
        parts = [qbuf[u, :, h * HD : (h + 1) * HD] for h in range(half_heads)]
        return split_query(jnp.concatenate(parts, axis=0))

    def attend(halves, keys, values, span):
        total = keys.shape[1]
        tiles = [(a, min(TILE, total - a)) for a in range(0, total, TILE)]
        queries = [queries_of(u) for u in halves]
        top = [None, None]
        before = [None, None]
        out = [None, None]

        def score(b, a, size):
            s = dot_nn(queries[b], keys[:, a : a + size])
            if span and a == prompt:
                r = halves[b] % 4
                query_z = (z - (1 - 2 * (r // 2)) * (halves[b] // 4) + 2 * ring) % ring
                query_ctx = y_hi * ring + query_z
                partner = (1 - y_hi) * ring + z
                token = low_bits(lax.broadcasted_iota(jnp.int32, (half, 2 * tokens), 0), tokens)
                key = lax.broadcasted_iota(jnp.int32, (half, 2 * tokens), 1)
                key_pos = jnp.where(key < tokens, me * tokens + key, partner * tokens + key - tokens)
                s = jnp.where(key_pos <= query_ctx * tokens + token, s, NEG)
            scores[b, :, a : a + size] = s
            for c in range(0, size, HD):
                part_of = s[:, c : c + HD]
                top[b] = part_of if top[b] is None else jnp.maximum(top[b], part_of)

        def settle(b):
            top[b] = jnp.max(top[b], axis=1, keepdims=True)
            if span:
                before[b] = mx[halves[b], :, 0:1]
                top[b] = jnp.maximum(top[b], before[b])

        def weigh(b, a, size):
            weights[b, :, a : a + size] = jnp.exp2(scores[b, :, a : a + size] - top[b]).astype(BF)

        def blend(b, a, size):
            piece = dot_nn(weights[b, :, a : a + size], values[a : a + size, :])
            out[b] = piece if out[b] is None else out[b] + piece

        wide = [(a, min(2 * TILE, total - a)) for a in range(0, total, 2 * TILE)]
        for tile in tiles:
            score(0, *tile)
        settle(0)
        for tile in tiles:
            score(1, *tile)
            weigh(0, *tile)
        settle(1)
        for j, tile in enumerate(tiles):
            if j % 2 == 0:
                blend(0, *wide[j // 2])
            weigh(1, *tile)
        for tile in wide:
            blend(1, *tile)
        for b, u in enumerate(halves):
            if span:
                keep = jnp.exp2(before[b] - top[b])
                acc[u] = acc[u] * keep + out[b][:, 0:HD]
                sm[u] = sm[u] * keep + out[b][:, HD : 2 * HD]
            else:
                acc[u] = out[b][:, 0:HD]
                sm[u] = out[b][:, HD : 2 * HD]
            mx[u] = jnp.broadcast_to(top[b], (half, HD))

    def own_step(n, carry):
        halves = pair(n)

        @pl.when(jnp.logical_and(n > 0, n < ring - 1))
        def _():
            whole_copy(n, qbuf.at[pl.ds(0, 2)]).wait_recv()

        @pl.when(n == ring - 1)
        def _():
            for u in (4 * far, 4 * far + 3):
                half_copy(u, qbuf.at[0]).wait_recv()

        @pl.when(jnp.logical_and(n > 0, n + 2 < ring - 1))
        def _():
            whole_copy(n + 2, qbuf.at[pl.ds(halves[0], 2)]).start()

        @pl.when(n == ring - 3)
        def _():
            half_copy(4 * far, qbuf.at[4 * far - 4]).start()

        @pl.when(n == ring - 2)
        def _():
            half_copy(4 * far + 3, qbuf.at[4 * far - 1]).start()

        attend(halves, k_own, v_own, False)

        @pl.when(n == 0)
        def _():
            for k in range(2):
                span_copy(k).wait_recv()
            span_relay().start()
            gather_copy(1, z).start()
            gather_copy(2, z).start()

        for p in range(2):
            @pl.when(n == ring // 2 + p)
            def _():
                forward_piece(p)

        @pl.when(n > 0)
        def _():
            at = gather_z(n)
            gather_copy(n, at).wait_recv()

            @pl.when(n + 2 < ring)
            def _():
                gather_copy(n + 2, at).start()

        return carry

    lax.fori_loop(0, ring, own_step, 0)
    for p in range(2, PIECES):
        forward_piece(p)

    each = tokens // tp_count
    parts = part.shape[1]
    wide_part = part.shape[5]
    step = min(512, wide_part)
    width = w.shape[1] // 2

    def core_copy(which, j):
        return remote(part.at[which, j, 1 - core], sib.at[which, j], c_send.at[which, j], c_recv.at[which, j], other_core)

    def chip_copy(which, j, k):
        return remote(
            pairs.at[which, j, (chip + k) % chips],
            got.at[which, j, k],
            p_send.at[which, j, k],
            p_recv.at[which, j, k],
            other_chips[k - 1],
        )

    def project(which):
        for j in range(parts):
            def columns(i, carry):
                at = pl.multiple_of(i * step, step)
                from_w = pl.multiple_of(at + j * wide_part, step)
                first = dot_nn(att[...], w[:, pl.ds(from_w, step)])
                second = dot_nn(att[...], w[:, pl.ds(pl.multiple_of(from_w + width, step), step)])
                for k in range(tp_count):
                    rows_of = slice(k * each, (k + 1) * each)
                    both = jnp.concatenate([first[rows_of], second[rows_of]], axis=0).astype(BF)
                    part[which, j, k % 2, k // 2, :, pl.ds(at, step)] = both
                return carry

            lax.fori_loop(0, wide_part // step, columns, 0)
            core_copy(which, j).start()

    def add_cores(which, j):
        core_copy(which, j).wait_recv()
        pairs[which, j] = (part[which, j, core].astype(F32) + sib[which, j].astype(F32)).astype(BF)
        for k in range(1, chips):
            chip_copy(which, j, k).start()

    def summed(which, j):
        total = part[which, j, core, chip].astype(F32) + sib[which, j, chip].astype(F32)
        for k in range(1, chips):
            chip_copy(which, j, k).wait_recv()
            total = total + got[which, j, k].astype(F32)
        return total

    for item in loads[4:]:
        item.wait()

    ctx_count = 2 * ring
    span_total = ctx_count * tokens
    blocks = owner_ref.shape[1]
    per_dev = tokens // BLOCK
    token_at = lax.broadcasted_iota(jnp.int32, (blocks, span_total), 1)
    block_at = lax.broadcasted_iota(jnp.int32, (blocks, span_total), 0)
    ring_at = high_bits(token_at, 2 * tokens)
    side_at = low_bits(high_bits(token_at, tokens), 2)
    block_of = (side_at * ring + ring_at) * per_dev + high_bits(low_bits(token_at, tokens), BLOCK)
    expand = jnp.where(block_of == block_at, 1.0, 0.0).astype(BF)
    other = 1 - pool
    owner_row = jnp.where(other == 0, owner_ref[0:1, :], owner_ref[1:2, :])
    slot_row = jnp.where(other == 0, slot_ref[0:1, :], slot_ref[1:2, :])
    owners = dot_nn(jnp.broadcast_to(owner_row, (8, blocks)).astype(F32).astype(BF), expand)[0:1, :]
    slots = dot_nn(jnp.broadcast_to(slot_row, (8, blocks)).astype(F32).astype(BF), expand)[0:1, :]
    slot_tokens = SLOTS * BLOCK
    wanted = jnp.where(owners == me.astype(F32), slots, -1.0).astype(jnp.int32)
    source = lax.broadcasted_iota(jnp.int32, (1, span_total), 1)
    wanted = wanted * BLOCK + low_bits(source, BLOCK)
    place = lax.broadcasted_iota(jnp.int32, (slot_tokens, span_total), 0)
    picked = jnp.where(place == wanted, 1.0, 0.0).astype(BF)
    gath_k = gath[:, :, 0:tokens, :].reshape(span_total, HD)
    gath_v = gath[:, :, tokens : 2 * tokens, :].reshape(span_total, HD)
    slot_k = dot_nn(picked, gath_k).astype(BF)
    slot_v = dot_nn(picked, gath_v).astype(BF)
    filled = dot_nt(jnp.ones((8, span_total), BF), picked)[0:1, :]

    steps = 4
    group = BLOCK // steps
    cache = ck.shape[1]
    new_pad = jnp.zeros((HD - dk_ref.shape[0], HD), BF)
    dec_rows = HEADS_DEV * BLOCK
    row_id = low_bits(lax.broadcasted_iota(jnp.int32, (dec_rows, HD), 0), BLOCK)
    col_id = lax.broadcasted_iota(jnp.int32, (dec_rows, HD), 1)
    crow_id = high_bits(low_bits(lax.broadcasted_iota(jnp.int32, (dec_rows, group * cache), 0), BLOCK), steps)
    ccol_id = high_bits(lax.broadcasted_iota(jnp.int32, (dec_rows, group * cache), 1), cache)
    one_row = lax.broadcasted_iota(jnp.int32, (1, group * cache), 1)

    def decode_group(g, carry):
        at = pl.ds(pl.multiple_of(g * BLOCK, BLOCK), BLOCK)
        asked = dq_ref[pl.ds(g * group, group)].astype(F32).reshape(BLOCK, HEADS_DEV * HD)
        queries = jnp.concatenate([asked[:, h * HD : (h + 1) * HD] for h in range(HEADS_DEV)], axis=0).astype(BF)
        keys = jnp.concatenate(
            [ck[pl.ds(g * group, group)].reshape(group * cache, HD), slot_k, dk_ref[...], new_pad], axis=0
        )
        values = jnp.concatenate(
            [cv[pl.ds(g * group, group)].reshape(group * cache, HD), slot_v, dv_ref[...], new_pad], axis=0
        )
        raw = dot_nt(queries, keys) * SCALE2
        live = jnp.zeros((1, group * cache), jnp.int32)
        for r in range(group):
            live = jnp.where(high_bits(one_row, cache) == r, len_ref[0, g * group + r], live)
        key_row = jnp.where(low_bits(one_row, cache) < live, high_bits(one_row, cache), -1)
        s_cache = jnp.where(crow_id == key_row, raw[:, 0 : group * cache], NEG)
        s_slot = jnp.where(filled > 0.5, raw[:, group * cache : group * cache + slot_tokens], NEG)
        here = g * BLOCK + row_id
        see_new = (high_bits(here, steps) == high_bits(col_id, steps)) & (col_id <= here)
        s_new = jnp.where(see_new, raw[:, group * cache + slot_tokens :], NEG)
        masked = jnp.concatenate([s_cache, s_slot, s_new], axis=1)
        top = jnp.max(masked, axis=1, keepdims=True)
        shares = jnp.exp2(masked - top)
        total = jnp.sum(shares, axis=1, keepdims=True)
        out = (dot_nn(shares.astype(BF), values) / total).astype(BF)
        for h in range(HEADS_DEV):
            att[at, h * HD : (h + 1) * HD] = out[h * BLOCK : (h + 1) * BLOCK]
        return carry

    lax.fori_loop(0, dq_ref.shape[0] // group, decode_group, 0)
    project(1)

    span_relay().wait_recv()
    span = 2 * tokens
    put_keys(k_par, prompt, jnp.concatenate([sk_ref[...], skv_par[0:tokens, :]], axis=0))
    v_par[prompt : prompt + tokens, 0:HD] = sv_ref[...]
    v_par[prompt + tokens : prompt + span, 0:HD] = skv_par[tokens:span, :]
    for j in range(parts):
        add_cores(1, j)
    for p in range(PIECES):
        piece_relay(p).wait_recv()
        at = (p % 2) * chunk
        if p // 2 == 0:
            for c in range(2):
                put_keys(k_par, at + c * (chunk // 2), par[p, c * (chunk // 2) : (c + 1) * (chunk // 2)])
        else:
            v_par[at : at + chunk, 0:HD] = par[p]

    def out_copy(u):
        return remote(
            obuf.at[u], oin.at[u], o_send.at[u], o_recv.at[u], {"ctx": left + (right - left) * ((u % 4) // 2)}
        )

    lane = lax.broadcasted_iota(jnp.int32, (8, HD), 1)

    def merge(u, box):
        out_copy(box).wait_recv()
        carried = oin[box, half : half + 32, :].astype(F32)
        stats = carried[0:8] + carried[8:16] + carried[16:24]
        for a in range(half // 8):
            in_m[8 * a : 8 * a + 8, :] = jnp.broadcast_to(stats[:, a : a + 1], (8, HD))
            in_l[8 * a : 8 * a + 8, :] = jnp.broadcast_to(stats[:, a + 64 : a + 65], (8, HD))
        top = jnp.maximum(mx[u], in_m[...])
        keep = jnp.exp2(mx[u] - top)
        add = jnp.exp2(in_m[...] - top)
        acc[u] = acc[u] * keep + oin[box, 0:half, :].astype(F32) * add
        sm[u] = sm[u] * keep + in_l[...] * add
        mx[u] = top

    def pack(u):
        obuf[u, 0:half, :] = acc[u].astype(BF)
        stats = jnp.zeros((8, HD), F32)
        for a in range(half // 8):
            at = pl.ds(8 * a, 8)
            stats = jnp.where(lane == a, mx[u, at, :], stats)
            stats = jnp.where(lane == a + 64, sm[u, at, :], stats)
        first = stats.astype(BF).astype(F32)
        second = (stats - first).astype(BF).astype(F32)
        third = stats - first - second
        obuf[u, half : half + 32, :] = jnp.concatenate(
            [first, second, third, jnp.zeros((8, HD), F32)], axis=0
        ).astype(BF)

    def last_step(m, carry):
        n = ring - 1 - m
        halves = pair(n)
        attend(halves, k_par, v_par, True)
        for u in halves:
            d, r = u // 4, u % 4

            @pl.when(jnp.logical_or(d + 1 < far, jnp.logical_and(d + 1 == far, r * (r - 3) == 0)))
            def _():
                merge(u, u + 4)

            pack(u)
            out_copy(u).start()
        return carry

    lax.fori_loop(0, ring - 1, last_step, 0)
    attend((0, 1), k_par, v_par, True)
    for u in range(2):
        merge(u, u + 4)
        merge(u, u + 6)
        done = (acc[u] / sm[u]).astype(BF)
        for h in range(half_heads):
            column = (u * half_heads + h) * HD
            att[:, column : column + HD] = done[h * tokens : (h + 1) * tokens]
    project(0)
    for j in range(parts):
        add_cores(0, j)
    for j in range(parts):
        decode_sum = summed(1, j)
        prefill_sum = summed(0, j)
        for c in range(2):
            rows_of = slice(c * each, (c + 1) * each)
            both = jnp.concatenate([prefill_sum[rows_of], decode_sum[rows_of]], axis=0).astype(BF)
            out_ref[:, c * width + j * wide_part : c * width + (j + 1) * wide_part] = both

    for n in range(1, ring - 1):
        whole_copy(n, qbuf.at[pl.ds(0, 2)]).wait_send()
        for u in pair(n):
            out_copy(u).wait_send()
    for u in (4 * far, 4 * far + 3):
        half_copy(u, qbuf.at[0]).wait_send()
        out_copy(u).wait_send()
    for k in range(2):
        span_copy(k).wait_send()
    span_relay().wait_send()
    for i in range(1, ring):
        gather_copy(i, z).wait_send()
    for p in range(PIECES):
        piece_copy(p).wait_send()
        piece_relay(p).wait_send()
    for which in range(2):
        for j in range(parts):
            core_copy(which, j).wait_send()
            for k in range(1, chips):
                chip_copy(which, j, k).wait_send()


def separate(sums_ref, prefill_ref, decode_ref):
    each = prefill_ref.shape[0]
    sums = sums_ref[...].astype(F32)
    prefill_ref[...] = sums[0:each].astype(BF)
    steps = decode_ref.shape[1]
    for r in range(decode_ref.shape[0]):
        decode_ref[r] = sums[each + r * steps : each + (r + 1) * steps].astype(BF)


def on_device(
    span_queries,
    span_keys,
    span_values,
    prompt_keys,
    prompt_values,
    block_owner,
    block_slot,
    decode_queries,
    decode_new_keys,
    decode_new_values,
    cache_keys,
    cache_values,
    cache_len,
    out_weight,
):
    ring = lax.axis_size("ctx") // 2
    tp_count = lax.axis_size("tp")
    tokens = span_queries.shape[1]
    width = span_queries.shape[2]
    prompt = prompt_keys.shape[1]
    row_count, step_count = decode_queries.shape[1:3]
    cache = cache_keys.shape[2]
    columns = out_weight.shape[1]
    each = tokens // tp_count
    count = 4 * (ring // 2) + 4
    half = tokens * HEADS_DEV // 2
    parts = 2
    wide_part = columns // 2 // parts
    chips = tp_count // 2
    span = 2 * tokens
    total = prompt + span
    vmem = pl.BlockSpec(memory_space=pltpu.VMEM)
    smem = pl.BlockSpec(memory_space=pltpu.SMEM)
    anywhere = pl.BlockSpec(memory_space=pl.ANY)
    dma = pltpu.SemaphoreType.DMA
    sums = pl.pallas_call(
        lambda *refs: kernel(ring, tp_count, *refs),
        out_shape=jax.ShapeDtypeStruct((2 * each, columns), BF),
        in_specs=[anywhere, vmem, vmem, anywhere, anywhere] + [vmem] * 5 + [anywhere, anywhere, smem, anywhere],
        out_specs=vmem,
        scratch_shapes=[
            pltpu.VMEM((count, tokens, width // 2), BF),
            pltpu.VMEM((span, HD), BF),
            pltpu.VMEM((span, HD), BF),
            pltpu.VMEM((ring, 2, span, HD), BF),
            pltpu.VMEM((PIECES, prompt // 2, HD), BF),
            pltpu.VMEM((PIECES, prompt // 2, HD), BF),
            pltpu.VMEM((prompt, HD), BF),
            pltpu.VMEM((2 * HD, prompt), BF),
            pltpu.VMEM((prompt, 2 * HD), BF),
            pltpu.VMEM((2 * HD, total), BF),
            pltpu.VMEM((total, 2 * HD), BF),
            pltpu.VMEM((2, half, total), F32),
            pltpu.VMEM((2, half, total), BF),
            pltpu.VMEM((count, half, HD), F32),
            pltpu.VMEM((count, half, HD), F32),
            pltpu.VMEM((count, half, HD), F32),
            pltpu.VMEM((half, HD), F32),
            pltpu.VMEM((half, HD), F32),
            pltpu.VMEM((count, half + 32, HD), BF),
            pltpu.VMEM((count, half + 32, HD), BF),
            pltpu.VMEM((width, columns), BF),
            pltpu.VMEM((row_count, cache, HD), BF),
            pltpu.VMEM((row_count, cache, HD), BF),
            pltpu.VMEM((tokens, width), BF),
            pltpu.VMEM((2, parts, 2, chips, 2 * each, wide_part), BF),
            pltpu.VMEM((2, parts, chips, 2 * each, wide_part), BF),
            pltpu.VMEM((2, parts, chips, 2 * each, wide_part), BF),
            pltpu.VMEM((2, parts, chips, 2 * each, wide_part), BF),
            dma((ring + 1,)),
            dma((ring + 1,)),
            dma((2,)),
            dma((2,)),
            dma((1,)),
            dma((1,)),
            dma((ring,)),
            dma((ring,)),
            dma((PIECES,)),
            dma((PIECES,)),
            dma((PIECES,)),
            dma((PIECES,)),
            dma((count,)),
            dma((count,)),
            dma((2, parts)),
            dma((2, parts)),
            dma((2, parts, chips)),
            dma((2, parts, chips)),
            dma((7,)),
        ],
        compiler_params=pltpu.CompilerParams(
            collective_id=0, has_side_effects=True, vmem_limit_bytes=60 * 1024 * 1024
        ),
        name="serve",
    )(
        span_queries[0],
        span_keys[0],
        span_values[0],
        prompt_keys[0],
        prompt_values[0],
        block_owner,
        block_slot,
        decode_queries[0],
        decode_new_keys.reshape(row_count * step_count, HD),
        decode_new_values.reshape(row_count * step_count, HD),
        cache_keys[0],
        cache_values[0],
        cache_len,
        out_weight,
    )
    prefill, decode = pl.pallas_call(
        separate,
        out_shape=(
            jax.ShapeDtypeStruct((each, columns), BF),
            jax.ShapeDtypeStruct((row_count // tp_count, step_count, columns), BF),
        ),
        in_specs=[vmem],
        out_specs=(vmem, vmem),
        name="separate",
    )(sums)
    return (prefill[None], decode[None])


def solution(mesh):
    in_specs = (
        P("grp", "ctx", "tp"),
        P("grp", "ctx", "tp"),
        P("grp", "ctx", "tp"),
        P("grp", "ctx", "tp"),
        P("grp", "ctx", "tp"),
        P(),
        P(),
        P("grp", "ctx", None, "tp"),
        P("grp", "ctx", None, "tp"),
        P("grp", "ctx", None, "tp"),
        P("grp", "ctx", None, "tp"),
        P("grp", "ctx", None, "tp"),
        P("grp", "ctx"),
        P("tp", None),
    )
    out_specs = (P("grp", ("ctx", "tp"), None), P("grp", ("ctx", "tp"), None, None))
    return jax.shard_map(
        on_device, mesh=mesh, in_specs=in_specs, out_specs=out_specs, check_vma=False
    )
```

```python
import math

import jax
import jax.numpy as jnp
from jax import lax
from jax.experimental import pallas as pl
from jax.experimental.pallas import tpu as pltpu
from jax.sharding import PartitionSpec as P

HD = 128
BLOCK = 16
SLOTS = 8
HEADS_DEV = 8
PIECES = 8
NEG = -1e30
SCALE2 = HD**-0.5 * math.log2(math.e)
MESH = pl.DeviceIdType.MESH
BF = jnp.bfloat16
F32 = jnp.float32


def dot_nt(a, b):
    return lax.dot_general(a, b, (((1,), (1,)), ((), ())), preferred_element_type=F32)


def dot_nn(a, b):
    return jnp.dot(a, b, preferred_element_type=F32)


def split_query(q):
    scaled = q.astype(F32) * SCALE2
    high = scaled.astype(BF)
    low = (scaled - high.astype(F32)).astype(BF)
    return jnp.concatenate([high, low], axis=1)


def low_bits(x, size):
    return jnp.bitwise_and(x, size - 1)


def high_bits(x, size):
    return lax.shift_right_logical(x, size.bit_length() - 1)


def kernel(
    ring, tp_count,
    q_ref, sk_ref, sv_ref, pk_ref, pv_ref, owner_ref, slot_ref, dq_ref, dk_ref, dv_ref, ck_hbm, cv_hbm, len_ref, w_hbm,
    out_ref,
    qbuf, skv, skv_par, gath, rel, par, k_raw, v_raw, k_own, v_own, k_par, v_par,
    acc, mx, sm, in_m, in_l, obuf, oin,
    w, ck, cv, att, part, sib, pairs, got,
    q_send, q_recv, s_send, s_recv, sp_send, sp_recv, g_send, g_recv, r_send, r_recv, f_send, f_recv,
    o_send, o_recv, c_send, c_recv, p_send, p_recv, load,
):
    me = lax.axis_index("ctx")
    pool = lax.axis_index("grp")
    tp = lax.axis_index("tp")
    core = tp % 2
    chip = tp // 2
    chips = tp_count // 2
    y_hi = me // ring
    z = me % ring
    y = y_hi * 2 + pool
    far = ring // 2
    tokens = sk_ref.shape[0]
    prompt = pk_ref.shape[0]
    chunk = prompt // 4
    half_heads = HEADS_DEV // 2
    half_width = half_heads * HD
    half = tokens * half_heads
    right = y_hi * ring + (z + 1) % ring
    left = y_hi * ring + (z + ring - 1) % ring
    up_y = (y + 1) % 4
    down_y = (y + 3) % 4
    up = {"ctx": (up_y // 2) * ring + z, "grp": up_y % 2}
    down = {"ctx": (down_y // 2) * ring + z, "grp": down_y % 2}

    def remote(src, dst, send, recv, device):
        return pltpu.make_async_remote_copy(
            src_ref=src, dst_ref=dst, send_sem=send, recv_sem=recv, device_id=device, device_id_type=MESH
        )

    def pair(n):
        first = 4 * ((n + 1) // 2) + 2 * ((n + 1) % 2) * ((n + ring - 2) // (ring - 1))
        return first, first + 1 + 2 * (n // (ring - 1))

    def toward(n):
        return {"ctx": left + (right - left) * (n % 2)}

    def back(n):
        return {"ctx": right + (left - right) * (n % 2)}

    def whole_copy(n, src):
        u = pair(n)[0]
        return remote(src, qbuf.at[pl.ds(u, 2)], q_send.at[n], q_recv.at[n], toward(n))

    def half_copy(u, src):
        k = ring - 1 + (u % 4) // 3
        return remote(src, qbuf.at[u], q_send.at[k], q_recv.at[k], {"ctx": right + (left - right) * ((u % 4) // 3)})

    def span_copy(k):
        return remote(skv, gath.at[z, y_hi], s_send.at[k], s_recv.at[k], (up, down)[k])

    def span_relay():
        return remote(gath.at[z, down_y // 2], skv_par, sp_send.at[0], sp_recv.at[0], up)

    def gather_copy(i, at):
        return remote(gath.at[at], gath.at[at], g_send.at[i], g_recv.at[i], toward(i))

    def gather_z(i):
        return (z - (2 * (i % 2) - 1) * ((i + 1) // 2) + ring) % ring

    def piece_rows(p):
        return ((p % 2) * 2 + p // 4) * chunk

    def piece_copy(p):
        src = (k_raw if (p // 2) % 2 == 0 else v_raw).at[pl.ds(piece_rows(p), chunk)]
        return remote(src, rel.at[p], r_send.at[p], r_recv.at[p], (up, down)[p % 2])

    def piece_relay(p):
        return remote(rel.at[p], par.at[p], f_send.at[p], f_recv.at[p], (up, down)[p % 2])

    def forward_piece(p):
        piece_copy(p).wait_recv()
        piece_relay(p).start()

    loads = [
        pltpu.make_async_copy(pk_ref, k_raw, load.at[0]),
        pltpu.make_async_copy(pv_ref, v_raw, load.at[1]),
        pltpu.make_async_copy(q_ref.at[:, pl.ds(0, half_width)], qbuf.at[0], load.at[2]),
        pltpu.make_async_copy(q_ref.at[:, pl.ds(half_width, half_width)], qbuf.at[1], load.at[3]),
        pltpu.make_async_copy(ck_hbm, ck, load.at[4]),
        pltpu.make_async_copy(cv_hbm, cv, load.at[5]),
        pltpu.make_async_copy(w_hbm, w, load.at[6]),
    ]
    for item in loads[:4]:
        item.start()

    other_core = {"tp": tp + 1 - 2 * core}
    other_chips = [{"tp": 2 * ((chip + k) % chips) + core} for k in range(1, chips)]
    barrier = pltpu.get_barrier_semaphore()
    for device in [{"ctx": right}, {"ctx": left}, up, down, other_core] + other_chips:
        pl.semaphore_signal(barrier, inc=1, device_id=device, device_id_type=MESH)
    skv[0:tokens, :] = sk_ref[...]
    skv[tokens : 2 * tokens, :] = sv_ref[...]
    for item in loads[:4]:
        item.wait()
    pl.semaphore_wait(barrier, 4 + chips)

    whole_copy(1, qbuf.at[pl.ds(0, 2)]).start()
    whole_copy(2, qbuf.at[pl.ds(0, 2)]).start()
    for p in range(PIECES):
        piece_copy(p).start()
    span_copy(0).start()
    span_copy(1).start()
    for item in loads[4:]:
        item.start()

    def put_keys(dst, at, rows):
        size = rows.shape[0]
        dst[at : at + size, 0:HD] = rows
        dst[at : at + size, HD : 2 * HD] = rows

    put_keys(k_own, 0, k_raw[...])
    v_own[:, 0:HD] = v_raw[...]
    v_own[:, HD : 2 * HD] = jnp.ones((prompt, HD), BF)
    v_par[:, HD : 2 * HD] = jnp.ones((v_par.shape[0], HD), BF)

    def queries_of(u):
        parts = [qbuf[u, :, h * HD : (h + 1) * HD] for h in range(half_heads)]
        return split_query(jnp.concatenate(parts, axis=0))

    def attend_own(halves):
        for u in halves:
            scores = dot_nt(queries_of(u), k_own[...])
            top = jnp.max(scores, axis=1, keepdims=True)
            out = dot_nn(jnp.exp2(scores - top).astype(BF), v_own[...])
            mx[u] = jnp.broadcast_to(top, (half, HD))
            acc[u] = out[:, 0:HD]
            sm[u] = out[:, HD : 2 * HD]

    def attend_partner(halves):
        for u in halves:
            query_z = (z - (1 - 2 * ((u % 4) // 2)) * (u // 4) + 2 * ring) % ring
            query_ctx = y_hi * ring + query_z
            partner = (1 - y_hi) * ring + z
            scores = dot_nt(queries_of(u), k_par[...])
            token = low_bits(lax.broadcasted_iota(jnp.int32, (half, 2 * tokens), 0), tokens)
            key = lax.broadcasted_iota(jnp.int32, (half, 2 * tokens), 1)
            key_pos = jnp.where(key < tokens, me * tokens + key, partner * tokens + key - tokens)
            seen = jnp.where(key_pos <= query_ctx * tokens + token, scores[:, prompt:], NEG)
            before = mx[u, :, 0:1]
            top = jnp.maximum(
                jnp.max(scores[:, 0:prompt], axis=1, keepdims=True), jnp.max(seen, axis=1, keepdims=True)
            )
            top = jnp.maximum(top, before)
            weights = jnp.concatenate(
                [jnp.exp2(scores[:, 0:prompt] - top).astype(BF), jnp.exp2(seen - top).astype(BF)], axis=1
            )
            out = dot_nn(weights, v_par[...])
            keep = jnp.exp2(before - top)
            mx[u] = jnp.broadcast_to(top, (half, HD))
            acc[u] = acc[u] * keep + out[:, 0:HD]
            sm[u] = sm[u] * keep + out[:, HD : 2 * HD]

    def own_step(n, carry):
        halves = pair(n)

        @pl.when(jnp.logical_and(n % 2 == 1, n < ring - 1))
        def _():
            for m in (n, n + 1):
                whole_copy(m, qbuf.at[pl.ds(0, 2)]).wait_recv()

        @pl.when(jnp.logical_and(n % 2 == 1, n < ring - 3))
        def _():
            for m in (n, n + 1):
                whole_copy(m + 2, qbuf.at[pl.ds(pair(m)[0], 2)]).start()

        @pl.when(n == ring - 3)
        def _():
            half_copy(4 * far, qbuf.at[4 * far - 4]).start()
            half_copy(4 * far + 3, qbuf.at[4 * far - 1]).start()

        @pl.when(n == ring - 1)
        def _():
            for u in (4 * far, 4 * far + 3):
                half_copy(u, qbuf.at[0]).wait_recv()

        attend_own(halves)

        @pl.when(n == 0)
        def _():
            for k in range(2):
                span_copy(k).wait_recv()
            span_relay().start()
            gather_copy(1, z).start()
            gather_copy(2, z).start()

        for c in range(PIECES // 2):
            @pl.when(n == min(c + 2, ring - 1))
            def _():
                forward_piece(2 * c)
                forward_piece(2 * c + 1)

        @pl.when(n > 0)
        def _():
            at = gather_z(n)
            gather_copy(n, at).wait_recv()

            @pl.when(n + 2 < ring)
            def _():
                gather_copy(n + 2, at).start()

        return carry

    lax.fori_loop(0, ring, own_step, 0)

    each = tokens // tp_count
    parts = part.shape[1]
    wide_part = part.shape[5]
    step = min(512, wide_part)
    width = w.shape[1] // 2

    def core_copy(which, j):
        return remote(part.at[which, j, 1 - core], sib.at[which, j], c_send.at[which, j], c_recv.at[which, j], other_core)

    def chip_copy(which, j, k):
        return remote(
            pairs.at[which, j, (chip + k) % chips],
            got.at[which, j, k],
            p_send.at[which, j, k],
            p_recv.at[which, j, k],
            other_chips[k - 1],
        )

    def project(which):
        for j in range(parts):
            def columns(i, carry):
                at = pl.multiple_of(i * step, step)
                from_w = pl.multiple_of(at + j * wide_part, step)
                first = dot_nn(att[...], w[:, pl.ds(from_w, step)])
                second = dot_nn(att[...], w[:, pl.ds(pl.multiple_of(from_w + width, step), step)])
                for k in range(tp_count):
                    rows_of = slice(k * each, (k + 1) * each)
                    both = jnp.concatenate([first[rows_of], second[rows_of]], axis=0).astype(BF)
                    part[which, j, k % 2, k // 2, :, pl.ds(at, step)] = both
                return carry

            lax.fori_loop(0, wide_part // step, columns, 0)
            core_copy(which, j).start()

    def add_cores(which, j):
        core_copy(which, j).wait_recv()
        pairs[which, j] = (part[which, j, core].astype(F32) + sib[which, j].astype(F32)).astype(BF)
        for k in range(1, chips):
            chip_copy(which, j, k).start()

    def summed(which, j):
        total = part[which, j, core, chip].astype(F32) + sib[which, j, chip].astype(F32)
        for k in range(1, chips):
            chip_copy(which, j, k).wait_recv()
            total = total + got[which, j, k].astype(F32)
        return total

    for item in loads[4:]:
        item.wait()

    ctx_count = 2 * ring
    span_total = ctx_count * tokens
    blocks = owner_ref.shape[1]
    per_dev = tokens // BLOCK
    token_at = lax.broadcasted_iota(jnp.int32, (blocks, span_total), 1)
    block_at = lax.broadcasted_iota(jnp.int32, (blocks, span_total), 0)
    ring_at = high_bits(token_at, 2 * tokens)
    side_at = low_bits(high_bits(token_at, tokens), 2)
    block_of = (side_at * ring + ring_at) * per_dev + high_bits(low_bits(token_at, tokens), BLOCK)
    expand = jnp.where(block_of == block_at, 1.0, 0.0).astype(BF)
    other = 1 - pool
    owner_row = jnp.where(other == 0, owner_ref[0:1, :], owner_ref[1:2, :])
    slot_row = jnp.where(other == 0, slot_ref[0:1, :], slot_ref[1:2, :])
    owners = dot_nn(jnp.broadcast_to(owner_row, (8, blocks)).astype(F32).astype(BF), expand)[0:1, :]
    slots = dot_nn(jnp.broadcast_to(slot_row, (8, blocks)).astype(F32).astype(BF), expand)[0:1, :]
    slot_tokens = SLOTS * BLOCK
    wanted = jnp.where(owners == me.astype(F32), slots, -1.0).astype(jnp.int32)
    source = lax.broadcasted_iota(jnp.int32, (1, span_total), 1)
    wanted = wanted * BLOCK + low_bits(source, BLOCK)
    place = lax.broadcasted_iota(jnp.int32, (slot_tokens, span_total), 0)
    picked = jnp.where(place == wanted, 1.0, 0.0).astype(BF)
    gath_k = gath[:, :, 0:tokens, :].reshape(span_total, HD)
    gath_v = gath[:, :, tokens : 2 * tokens, :].reshape(span_total, HD)
    slot_k = dot_nn(picked, gath_k).astype(BF)
    slot_v = dot_nn(picked, gath_v).astype(BF)
    filled = dot_nt(jnp.ones((8, span_total), BF), picked)[0:1, :]

    steps = 4
    group = BLOCK // steps
    cache = ck.shape[1]
    new_pad = jnp.zeros((HD - dk_ref.shape[0], HD), BF)
    dec_rows = HEADS_DEV * BLOCK
    row_id = low_bits(lax.broadcasted_iota(jnp.int32, (dec_rows, HD), 0), BLOCK)
    col_id = lax.broadcasted_iota(jnp.int32, (dec_rows, HD), 1)
    crow_id = high_bits(low_bits(lax.broadcasted_iota(jnp.int32, (dec_rows, group * cache), 0), BLOCK), steps)
    ccol_id = high_bits(lax.broadcasted_iota(jnp.int32, (dec_rows, group * cache), 1), cache)
    one_row = lax.broadcasted_iota(jnp.int32, (1, group * cache), 1)

    def decode_group(g, carry):
        at = pl.ds(pl.multiple_of(g * BLOCK, BLOCK), BLOCK)
        asked = dq_ref[pl.ds(g * group, group)].astype(F32).reshape(BLOCK, HEADS_DEV * HD)
        queries = jnp.concatenate([asked[:, h * HD : (h + 1) * HD] for h in range(HEADS_DEV)], axis=0).astype(BF)
        keys = jnp.concatenate(
            [ck[pl.ds(g * group, group)].reshape(group * cache, HD), slot_k, dk_ref[...], new_pad], axis=0
        )
        values = jnp.concatenate(
            [cv[pl.ds(g * group, group)].reshape(group * cache, HD), slot_v, dv_ref[...], new_pad], axis=0
        )
        raw = dot_nt(queries, keys) * SCALE2
        live = jnp.zeros((1, group * cache), jnp.int32)
        for r in range(group):
            live = jnp.where(high_bits(one_row, cache) == r, len_ref[0, g * group + r], live)
        key_row = jnp.where(low_bits(one_row, cache) < live, high_bits(one_row, cache), -1)
        s_cache = jnp.where(crow_id == key_row, raw[:, 0 : group * cache], NEG)
        s_slot = jnp.where(filled > 0.5, raw[:, group * cache : group * cache + slot_tokens], NEG)
        here = g * BLOCK + row_id
        see_new = (high_bits(here, steps) == high_bits(col_id, steps)) & (col_id <= here)
        s_new = jnp.where(see_new, raw[:, group * cache + slot_tokens :], NEG)
        masked = jnp.concatenate([s_cache, s_slot, s_new], axis=1)
        top = jnp.max(masked, axis=1, keepdims=True)
        shares = jnp.exp2(masked - top)
        total = jnp.sum(shares, axis=1, keepdims=True)
        out = (dot_nn(shares.astype(BF), values) / total).astype(BF)
        for h in range(HEADS_DEV):
            att[at, h * HD : (h + 1) * HD] = out[h * BLOCK : (h + 1) * BLOCK]
        return carry

    lax.fori_loop(0, dq_ref.shape[0] // group, decode_group, 0)
    project(1)

    span_relay().wait_recv()
    span = 2 * tokens
    put_keys(k_par, prompt, jnp.concatenate([sk_ref[...], skv_par[0:tokens, :]], axis=0))
    v_par[prompt : prompt + tokens, 0:HD] = sv_ref[...]
    v_par[prompt + tokens : prompt + span, 0:HD] = skv_par[tokens:span, :]
    for j in range(parts):
        add_cores(1, j)
    for p in range(PIECES):
        piece_relay(p).wait_recv()
        at = piece_rows(p)
        if (p // 2) % 2 == 0:
            put_keys(k_par, at, par[p])
        else:
            v_par[at : at + chunk, 0:HD] = par[p]

    def out_copy(u):
        return remote(
            obuf.at[u], oin.at[u], o_send.at[u], o_recv.at[u], {"ctx": left + (right - left) * ((u % 4) // 2)}
        )

    lane = lax.broadcasted_iota(jnp.int32, (8, HD), 1)

    def merge(u, box):
        out_copy(box).wait_recv()
        carried = oin[box, half : half + 32, :].astype(F32)
        stats = carried[0:8] + carried[8:16] + carried[16:24]
        for a in range(half // 8):
            in_m[8 * a : 8 * a + 8, :] = jnp.broadcast_to(stats[:, a : a + 1], (8, HD))
            in_l[8 * a : 8 * a + 8, :] = jnp.broadcast_to(stats[:, a + 64 : a + 65], (8, HD))
        top = jnp.maximum(mx[u], in_m[...])
        keep = jnp.exp2(mx[u] - top)
        add = jnp.exp2(in_m[...] - top)
        acc[u] = acc[u] * keep + oin[box, 0:half, :].astype(F32) * add
        sm[u] = sm[u] * keep + in_l[...] * add
        mx[u] = top

    def pack(u):
        obuf[u, 0:half, :] = acc[u].astype(BF)
        stats = jnp.zeros((8, HD), F32)
        for a in range(half // 8):
            at = pl.ds(8 * a, 8)
            stats = jnp.where(lane == a, mx[u, at, :], stats)
            stats = jnp.where(lane == a + 64, sm[u, at, :], stats)
        first = stats.astype(BF).astype(F32)
        second = (stats - first).astype(BF).astype(F32)
        third = stats - first - second
        obuf[u, half : half + 32, :] = jnp.concatenate(
            [first, second, third, jnp.zeros((8, HD), F32)], axis=0
        ).astype(BF)

    def last_step(m, carry):
        n = ring - 1 - m
        halves = pair(n)
        attend_partner(halves)
        for u in halves:
            d, r = u // 4, u % 4

            @pl.when(jnp.logical_or(d + 1 < far, jnp.logical_and(d + 1 == far, r * (r - 3) == 0)))
            def _():
                merge(u, u + 4)

            pack(u)
            out_copy(u).start()
        return carry

    lax.fori_loop(0, ring - 1, last_step, 0)
    attend_partner((0, 1))
    for u in range(2):
        merge(u, u + 4)
        merge(u, u + 6)
        done = (acc[u] / sm[u]).astype(BF)
        for h in range(half_heads):
            column = (u * half_heads + h) * HD
            att[:, column : column + HD] = done[h * tokens : (h + 1) * tokens]
    project(0)
    for j in range(parts):
        add_cores(0, j)
    for j in range(parts):
        decode_sum = summed(1, j)
        prefill_sum = summed(0, j)
        for c in range(2):
            rows_of = slice(c * each, (c + 1) * each)
            both = jnp.concatenate([prefill_sum[rows_of], decode_sum[rows_of]], axis=0).astype(BF)
            out_ref[:, c * width + j * wide_part : c * width + (j + 1) * wide_part] = both

    for n in range(1, ring - 1):
        whole_copy(n, qbuf.at[pl.ds(0, 2)]).wait_send()
        for u in pair(n):
            out_copy(u).wait_send()
    for u in (4 * far, 4 * far + 3):
        half_copy(u, qbuf.at[0]).wait_send()
        out_copy(u).wait_send()
    for k in range(2):
        span_copy(k).wait_send()
    span_relay().wait_send()
    for i in range(1, ring):
        gather_copy(i, z).wait_send()
    for p in range(PIECES):
        piece_copy(p).wait_send()
        piece_relay(p).wait_send()
    for which in range(2):
        for j in range(parts):
            core_copy(which, j).wait_send()
            for k in range(1, chips):
                chip_copy(which, j, k).wait_send()


def separate(sums_ref, prefill_ref, decode_ref):
    each = prefill_ref.shape[0]
    sums = sums_ref[...].astype(F32)
    prefill_ref[...] = sums[0:each].astype(BF)
    steps = decode_ref.shape[1]
    for r in range(decode_ref.shape[0]):
        decode_ref[r] = sums[each + r * steps : each + (r + 1) * steps].astype(BF)


def on_device(
    span_queries,
    span_keys,
    span_values,
    prompt_keys,
    prompt_values,
    block_owner,
    block_slot,
    decode_queries,
    decode_new_keys,
    decode_new_values,
    cache_keys,
    cache_values,
    cache_len,
    out_weight,
):
    ring = lax.axis_size("ctx") // 2
    tp_count = lax.axis_size("tp")
    tokens = span_queries.shape[1]
    width = span_queries.shape[2]
    prompt = prompt_keys.shape[1]
    row_count, step_count = decode_queries.shape[1:3]
    cache = cache_keys.shape[2]
    columns = out_weight.shape[1]
    each = tokens // tp_count
    count = 4 * (ring // 2) + 4
    half = tokens * HEADS_DEV // 2
    parts = 2
    wide_part = columns // 2 // parts
    chips = tp_count // 2
    span = 2 * tokens
    total = prompt + span
    vmem = pl.BlockSpec(memory_space=pltpu.VMEM)
    smem = pl.BlockSpec(memory_space=pltpu.SMEM)
    anywhere = pl.BlockSpec(memory_space=pl.ANY)
    dma = pltpu.SemaphoreType.DMA
    sums = pl.pallas_call(
        lambda *refs: kernel(ring, tp_count, *refs),
        out_shape=jax.ShapeDtypeStruct((2 * each, columns), BF),
        in_specs=[anywhere, vmem, vmem, anywhere, anywhere] + [vmem] * 5 + [anywhere, anywhere, smem, anywhere],
        out_specs=vmem,
        scratch_shapes=[
            pltpu.VMEM((count, tokens, width // 2), BF),
            pltpu.VMEM((span, HD), BF),
            pltpu.VMEM((span, HD), BF),
            pltpu.VMEM((ring, 2, span, HD), BF),
            pltpu.VMEM((PIECES, prompt // 4, HD), BF),
            pltpu.VMEM((PIECES, prompt // 4, HD), BF),
            pltpu.VMEM((prompt, HD), BF),
            pltpu.VMEM((prompt, HD), BF),
            pltpu.VMEM((prompt, 2 * HD), BF),
            pltpu.VMEM((prompt, 2 * HD), BF),
            pltpu.VMEM((total, 2 * HD), BF),
            pltpu.VMEM((total, 2 * HD), BF),
            pltpu.VMEM((count, half, HD), F32),
            pltpu.VMEM((count, half, HD), F32),
            pltpu.VMEM((count, half, HD), F32),
            pltpu.VMEM((half, HD), F32),
            pltpu.VMEM((half, HD), F32),
            pltpu.VMEM((count, half + 32, HD), BF),
            pltpu.VMEM((count, half + 32, HD), BF),
            pltpu.VMEM((width, columns), BF),
            pltpu.VMEM((row_count, cache, HD), BF),
            pltpu.VMEM((row_count, cache, HD), BF),
            pltpu.VMEM((tokens, width), BF),
            pltpu.VMEM((2, parts, 2, chips, 2 * each, wide_part), BF),
            pltpu.VMEM((2, parts, chips, 2 * each, wide_part), BF),
            pltpu.VMEM((2, parts, chips, 2 * each, wide_part), BF),
            pltpu.VMEM((2, parts, chips, 2 * each, wide_part), BF),
            dma((ring + 1,)),
            dma((ring + 1,)),
            dma((2,)),
            dma((2,)),
            dma((1,)),
            dma((1,)),
            dma((ring,)),
            dma((ring,)),
            dma((PIECES,)),
            dma((PIECES,)),
            dma((PIECES,)),
            dma((PIECES,)),
            dma((count,)),
            dma((count,)),
            dma((2, parts)),
            dma((2, parts)),
            dma((2, parts, chips)),
            dma((2, parts, chips)),
            dma((7,)),
        ],
        compiler_params=pltpu.CompilerParams(
            collective_id=0, has_side_effects=True, vmem_limit_bytes=60 * 1024 * 1024
        ),
        name="serve",
    )(
        span_queries[0],
        span_keys[0],
        span_values[0],
        prompt_keys[0],
        prompt_values[0],
        block_owner,
        block_slot,
        decode_queries[0],
        decode_new_keys.reshape(row_count * step_count, HD),
        decode_new_values.reshape(row_count * step_count, HD),
        cache_keys[0],
        cache_values[0],
        cache_len,
        out_weight,
    )
    prefill, decode = pl.pallas_call(
        separate,
        out_shape=(
            jax.ShapeDtypeStruct((each, columns), BF),
            jax.ShapeDtypeStruct((row_count // tp_count, step_count, columns), BF),
        ),
        in_specs=[vmem],
        out_specs=(vmem, vmem),
        name="separate",
    )(sums)
    return (prefill[None], decode[None])


def solution(mesh):
    in_specs = (
        P("grp", "ctx", "tp"),
        P("grp", "ctx", "tp"),
        P("grp", "ctx", "tp"),
        P("grp", "ctx", "tp"),
        P("grp", "ctx", "tp"),
        P(),
        P(),
        P("grp", "ctx", None, "tp"),
        P("grp", "ctx", None, "tp"),
        P("grp", "ctx", None, "tp"),
        P("grp", "ctx", None, "tp"),
        P("grp", "ctx", None, "tp"),
        P("grp", "ctx"),
        P("tp", None),
    )
    out_specs = (P("grp", ("ctx", "tp"), None), P("grp", ("ctx", "tp"), None, None))
    return jax.shard_map(
        on_device, mesh=mesh, in_specs=in_specs, out_specs=out_specs, check_vma=False
    )
```

```python
import math

import jax
import jax.numpy as jnp
from jax import lax
from jax.experimental import pallas as pl
from jax.experimental.pallas import tpu as pltpu
from jax.sharding import PartitionSpec as P

HD = 128
BLOCK = 16
SLOTS = 8
HEADS_DEV = 8
PIECES = 8
NEG = -1e30
SCALE2 = HD**-0.5 * math.log2(math.e)
MESH = pl.DeviceIdType.MESH
BF = jnp.bfloat16
F32 = jnp.float32


def dot_nt(a, b):
    return lax.dot_general(a, b, (((1,), (1,)), ((), ())), preferred_element_type=F32)


def dot_nn(a, b):
    return jnp.dot(a, b, preferred_element_type=F32)


def split_query(q):
    scaled = q.astype(F32) * SCALE2
    high = scaled.astype(BF)
    low = (scaled - high.astype(F32)).astype(BF)
    return jnp.concatenate([high, low], axis=1)


def low_bits(x, size):
    return jnp.bitwise_and(x, size - 1)


def high_bits(x, size):
    return lax.shift_right_logical(x, size.bit_length() - 1)


def kernel(
    ring, tp_count,
    q_ref, sk_ref, sv_ref, pk_ref, pv_ref, owner_ref, slot_ref, dq_ref, dk_ref, dv_ref, ck_hbm, cv_hbm, len_ref, w_hbm,
    out_ref,
    qbuf, skv, skv_par, gath, rel, par, k_raw, v_raw, k_own, v_own, k_par, v_par,
    acc, mx, sm, in_m, in_l, obuf, oin,
    w, ck, cv, att, part, sib, pairs, got,
    q_send, q_recv, s_send, s_recv, sp_send, sp_recv, g_send, g_recv, r_send, r_recv, f_send, f_recv,
    o_send, o_recv, c_send, c_recv, p_send, p_recv, load,
):
    me = lax.axis_index("ctx")
    pool = lax.axis_index("grp")
    tp = lax.axis_index("tp")
    core = tp % 2
    chip = tp // 2
    chips = tp_count // 2
    y_hi = me // ring
    z = me % ring
    y = y_hi * 2 + pool
    tokens = sk_ref.shape[0]
    prompt = pk_ref.shape[0]
    chunk = prompt // 4
    half_heads = HEADS_DEV // 2
    half = tokens * half_heads
    right = y_hi * ring + (z + 1) % ring
    left = y_hi * ring + (z + ring - 1) % ring
    up_y = (y + 1) % 4
    down_y = (y + 3) % 4
    up = {"ctx": (up_y // 2) * ring + z, "grp": up_y % 2}
    down = {"ctx": (down_y // 2) * ring + z, "grp": down_y % 2}

    def remote(src, dst, send, recv, device):
        return pltpu.make_async_remote_copy(
            src_ref=src, dst_ref=dst, send_sem=send, recv_sem=recv, device_id=device, device_id_type=MESH
        )

    def toward(i):
        return {"ctx": left + (right - left) * (i % 2)}

    def back(i):
        return {"ctx": right + (left - right) * (i % 2)}

    def source_z(i):
        return (z - (2 * (i % 2) - 1) * ((i + 1) // 2) + ring) % ring

    def query_copy(i, src):
        return remote(src, qbuf.at[i], q_send.at[i], q_recv.at[i], toward(i))

    def span_copy(k):
        return remote(skv, gath.at[z, y_hi], s_send.at[k], s_recv.at[k], (up, down)[k])

    def span_relay():
        return remote(gath.at[z, down_y // 2], skv_par, sp_send.at[0], sp_recv.at[0], up)

    def gather_copy(i, at):
        return remote(gath.at[at], gath.at[at], g_send.at[i], g_recv.at[i], toward(i))

    def piece_rows(p):
        return ((p % 2) * 2 + p // 4) * chunk

    def piece_copy(p):
        src = (k_raw if (p // 2) % 2 == 0 else v_raw).at[pl.ds(piece_rows(p), chunk)]
        return remote(src, rel.at[p], r_send.at[p], r_recv.at[p], (up, down)[p % 2])

    def piece_relay(p):
        return remote(rel.at[p], par.at[p], f_send.at[p], f_recv.at[p], (up, down)[p % 2])

    def forward_piece(p):
        piece_copy(p).wait_recv()
        piece_relay(p).start()

    loads = [
        pltpu.make_async_copy(pk_ref, k_raw, load.at[0]),
        pltpu.make_async_copy(pv_ref, v_raw, load.at[1]),
        pltpu.make_async_copy(q_ref, qbuf.at[0], load.at[2]),
        pltpu.make_async_copy(ck_hbm, ck, load.at[3]),
        pltpu.make_async_copy(cv_hbm, cv, load.at[4]),
        pltpu.make_async_copy(w_hbm, w, load.at[5]),
    ]
    for item in loads[:3]:
        item.start()

    other_core = {"tp": tp + 1 - 2 * core}
    other_chips = [{"tp": 2 * ((chip + k) % chips) + core} for k in range(1, chips)]
    barrier = pltpu.get_barrier_semaphore()
    for device in [{"ctx": right}, {"ctx": left}, up, down, other_core] + other_chips:
        pl.semaphore_signal(barrier, inc=1, device_id=device, device_id_type=MESH)
    skv[0:tokens, :] = sk_ref[...]
    skv[tokens : 2 * tokens, :] = sv_ref[...]
    for item in loads[:3]:
        item.wait()
    pl.semaphore_wait(barrier, 4 + chips)

    query_copy(1, qbuf.at[0]).start()
    query_copy(2, qbuf.at[0]).start()
    span_copy(0).start()
    span_copy(1).start()
    for p in range(PIECES):
        piece_copy(p).start()
    for item in loads[3:]:
        item.start()

    def put_keys(dst, at, rows):
        size = rows.shape[0]
        dst[at : at + size, 0:HD] = rows
        dst[at : at + size, HD : 2 * HD] = rows

    put_keys(k_own, 0, k_raw[...])
    v_own[:, 0:HD] = v_raw[...]
    v_own[:, HD : 2 * HD] = jnp.ones((prompt, HD), BF)
    v_par[:, HD : 2 * HD] = jnp.ones((v_par.shape[0], HD), BF)

    spans = [pl.ds(0, half), pl.ds(half, half)]

    def queries_of(i):
        halves = []
        for b in range(2):
            heads = range(b * half_heads, (b + 1) * half_heads)
            halves.append(split_query(jnp.concatenate([qbuf[i, :, h * HD : (h + 1) * HD] for h in heads], axis=0)))
        return halves

    def attend_own(i):
        results = []
        for queries in queries_of(i):
            scores = dot_nt(queries, k_own[...])
            top = jnp.max(scores, axis=1, keepdims=True)
            results.append((top, dot_nn(jnp.exp2(scores - top).astype(BF), v_own[...])))
        for at, (top, out) in zip(spans, results):
            mx[i, at, :] = jnp.broadcast_to(top, (half, HD))
            acc[i, at, :] = out[:, 0:HD]
            sm[i, at, :] = out[:, HD : 2 * HD]

    def attend_partner(i):
        query_ctx = y_hi * ring + source_z(i)
        partner = (1 - y_hi) * ring + z
        token = low_bits(lax.broadcasted_iota(jnp.int32, (half, 2 * tokens), 0), tokens)
        key = lax.broadcasted_iota(jnp.int32, (half, 2 * tokens), 1)
        key_pos = jnp.where(key < tokens, me * tokens + key, partner * tokens + key - tokens)
        visible = key_pos <= query_ctx * tokens + token
        befores = [mx[i, at, 0:1] for at in spans]
        results = []
        for queries, before in zip(queries_of(i), befores):
            scores = dot_nt(queries, k_par[...])
            seen = jnp.where(visible, scores[:, prompt:], NEG)
            top = jnp.maximum(
                jnp.max(scores[:, 0:prompt], axis=1, keepdims=True), jnp.max(seen, axis=1, keepdims=True)
            )
            top = jnp.maximum(top, before)
            weights = jnp.concatenate(
                [jnp.exp2(scores[:, 0:prompt] - top).astype(BF), jnp.exp2(seen - top).astype(BF)], axis=1
            )
            results.append((top, dot_nn(weights, v_par[...])))
        for at, before, (top, out) in zip(spans, befores, results):
            keep = jnp.exp2(before - top)
            mx[i, at, :] = jnp.broadcast_to(top, (half, HD))
            acc[i, at, :] = acc[i, at, :] * keep + out[:, 0:HD]
            sm[i, at, :] = sm[i, at, :] * keep + out[:, HD : 2 * HD]

    def own_step(n, carry):
        for c in range(2):
            @pl.when(jnp.logical_and(n % 2 == 1, n + c < ring))
            def _():
                query_copy(n + c, qbuf.at[0]).wait_recv()

            @pl.when(jnp.logical_and(n % 2 == 1, n + c + 2 < ring))
            def _():
                query_copy(n + c + 2, qbuf.at[n + c]).start()

        attend_own(n)

        @pl.when(n == 0)
        def _():
            for k in range(2):
                span_copy(k).wait_recv()
            span_relay().start()
            gather_copy(1, z).start()
            gather_copy(2, z).start()

        for c in range(PIECES // 2):
            @pl.when(n == min(c + 2, ring - 1))
            def _():
                forward_piece(2 * c)
                forward_piece(2 * c + 1)

        @pl.when(n > 0)
        def _():
            at = source_z(n)
            gather_copy(n, at).wait_recv()

            @pl.when(n + 2 < ring)
            def _():
                gather_copy(n + 2, at).start()

        return carry

    lax.fori_loop(0, ring, own_step, 0)

    each = tokens // tp_count
    parts = part.shape[1]
    wide_part = part.shape[5]
    step = min(512, wide_part)
    width = w.shape[1] // 2

    def core_copy(which, j):
        return remote(part.at[which, j, 1 - core], sib.at[which, j], c_send.at[which, j], c_recv.at[which, j], other_core)

    def chip_copy(which, j, k):
        return remote(
            pairs.at[which, j, (chip + k) % chips],
            got.at[which, j, k],
            p_send.at[which, j, k],
            p_recv.at[which, j, k],
            other_chips[k - 1],
        )

    def project(which):
        for j in range(parts):
            def columns(i, carry):
                at = pl.multiple_of(i * step, step)
                from_w = pl.multiple_of(at + j * wide_part, step)
                first = dot_nn(att[...], w[:, pl.ds(from_w, step)])
                second = dot_nn(att[...], w[:, pl.ds(pl.multiple_of(from_w + width, step), step)])
                for k in range(tp_count):
                    rows_of = slice(k * each, (k + 1) * each)
                    both = jnp.concatenate([first[rows_of], second[rows_of]], axis=0).astype(BF)
                    part[which, j, k % 2, k // 2, :, pl.ds(at, step)] = both
                return carry

            lax.fori_loop(0, wide_part // step, columns, 0)
            core_copy(which, j).start()

    def add_cores(which, j):
        core_copy(which, j).wait_recv()
        pairs[which, j] = (part[which, j, core].astype(F32) + sib[which, j].astype(F32)).astype(BF)
        for k in range(1, chips):
            chip_copy(which, j, k).start()

    def summed(which, j):
        total = part[which, j, core, chip].astype(F32) + sib[which, j, chip].astype(F32)
        for k in range(1, chips):
            chip_copy(which, j, k).wait_recv()
            total = total + got[which, j, k].astype(F32)
        return total

    for item in loads[3:]:
        item.wait()

    ctx_count = 2 * ring
    span_total = ctx_count * tokens
    blocks = owner_ref.shape[1]
    per_dev = tokens // BLOCK
    token_at = lax.broadcasted_iota(jnp.int32, (blocks, span_total), 1)
    block_at = lax.broadcasted_iota(jnp.int32, (blocks, span_total), 0)
    ring_at = high_bits(token_at, 2 * tokens)
    side_at = low_bits(high_bits(token_at, tokens), 2)
    block_of = (side_at * ring + ring_at) * per_dev + high_bits(low_bits(token_at, tokens), BLOCK)
    expand = jnp.where(block_of == block_at, 1.0, 0.0).astype(BF)
    other = 1 - pool
    owner_row = jnp.where(other == 0, owner_ref[0:1, :], owner_ref[1:2, :])
    slot_row = jnp.where(other == 0, slot_ref[0:1, :], slot_ref[1:2, :])
    owners = dot_nn(jnp.broadcast_to(owner_row, (8, blocks)).astype(F32).astype(BF), expand)[0:1, :]
    slots = dot_nn(jnp.broadcast_to(slot_row, (8, blocks)).astype(F32).astype(BF), expand)[0:1, :]
    slot_tokens = SLOTS * BLOCK
    wanted = jnp.where(owners == me.astype(F32), slots, -1.0).astype(jnp.int32)
    source = lax.broadcasted_iota(jnp.int32, (1, span_total), 1)
    wanted = wanted * BLOCK + low_bits(source, BLOCK)
    place = lax.broadcasted_iota(jnp.int32, (slot_tokens, span_total), 0)
    picked = jnp.where(place == wanted, 1.0, 0.0).astype(BF)
    gath_k = gath[:, :, 0:tokens, :].reshape(span_total, HD)
    gath_v = gath[:, :, tokens : 2 * tokens, :].reshape(span_total, HD)
    slot_k = dot_nn(picked, gath_k).astype(BF)
    slot_v = dot_nn(picked, gath_v).astype(BF)
    filled = dot_nt(jnp.ones((8, span_total), BF), picked)[0:1, :]

    steps = 4
    group = BLOCK // steps
    cache = ck.shape[1]
    new_pad = jnp.zeros((HD - dk_ref.shape[0], HD), BF)
    dec_rows = HEADS_DEV * BLOCK
    row_id = low_bits(lax.broadcasted_iota(jnp.int32, (dec_rows, HD), 0), BLOCK)
    col_id = lax.broadcasted_iota(jnp.int32, (dec_rows, HD), 1)
    crow_id = high_bits(low_bits(lax.broadcasted_iota(jnp.int32, (dec_rows, group * cache), 0), BLOCK), steps)
    ccol_id = high_bits(lax.broadcasted_iota(jnp.int32, (dec_rows, group * cache), 1), cache)
    one_row = lax.broadcasted_iota(jnp.int32, (1, group * cache), 1)

    def decode_group(g, carry):
        at = pl.ds(pl.multiple_of(g * BLOCK, BLOCK), BLOCK)
        asked = dq_ref[pl.ds(g * group, group)].astype(F32).reshape(BLOCK, HEADS_DEV * HD)
        queries = jnp.concatenate([asked[:, h * HD : (h + 1) * HD] for h in range(HEADS_DEV)], axis=0).astype(BF)
        keys = jnp.concatenate(
            [ck[pl.ds(g * group, group)].reshape(group * cache, HD), slot_k, dk_ref[...], new_pad], axis=0
        )
        values = jnp.concatenate(
            [cv[pl.ds(g * group, group)].reshape(group * cache, HD), slot_v, dv_ref[...], new_pad], axis=0
        )
        raw = dot_nt(queries, keys) * SCALE2
        live = jnp.zeros((1, group * cache), jnp.int32)
        for r in range(group):
            live = jnp.where(high_bits(one_row, cache) == r, len_ref[0, g * group + r], live)
        key_row = jnp.where(low_bits(one_row, cache) < live, high_bits(one_row, cache), -1)
        s_cache = jnp.where(crow_id == key_row, raw[:, 0 : group * cache], NEG)
        s_slot = jnp.where(filled > 0.5, raw[:, group * cache : group * cache + slot_tokens], NEG)
        here = g * BLOCK + row_id
        see_new = (high_bits(here, steps) == high_bits(col_id, steps)) & (col_id <= here)
        s_new = jnp.where(see_new, raw[:, group * cache + slot_tokens :], NEG)
        masked = jnp.concatenate([s_cache, s_slot, s_new], axis=1)
        top = jnp.max(masked, axis=1, keepdims=True)
        shares = jnp.exp2(masked - top)
        total = jnp.sum(shares, axis=1, keepdims=True)
        out = (dot_nn(shares.astype(BF), values) / total).astype(BF)
        for h in range(HEADS_DEV):
            att[at, h * HD : (h + 1) * HD] = out[h * BLOCK : (h + 1) * BLOCK]
        return carry

    lax.fori_loop(0, dq_ref.shape[0] // group, decode_group, 0)
    project(1)

    span_relay().wait_recv()
    span = 2 * tokens
    put_keys(k_par, prompt, jnp.concatenate([sk_ref[...], skv_par[0:tokens, :]], axis=0))
    v_par[prompt : prompt + tokens, 0:HD] = sv_ref[...]
    v_par[prompt + tokens : prompt + span, 0:HD] = skv_par[tokens:span, :]
    for j in range(parts):
        add_cores(1, j)
    for p in range(PIECES):
        piece_relay(p).wait_recv()
        at = piece_rows(p)
        if (p // 2) % 2 == 0:
            put_keys(k_par, at, par[p])
        else:
            v_par[at : at + chunk, 0:HD] = par[p]

    rows = 2 * half

    def out_copy(i):
        return remote(obuf.at[i], oin.at[i], o_send.at[i], o_recv.at[i], back(i))

    lane = lax.broadcasted_iota(jnp.int32, (8, HD), 1)
    group_lanes = [(8 * a, (a % 8) * 16 + a // 8) for a in range(rows // 8)]

    def merge(i, box):
        out_copy(box).wait_recv()
        carried = oin[box, rows : rows + 32, :].astype(F32)
        stats = carried[0:8] + carried[8:16] + carried[16:24]
        for at, a in group_lanes:
            in_m[at : at + 8, :] = jnp.broadcast_to(stats[:, a : a + 1], (8, HD))
            in_l[at : at + 8, :] = jnp.broadcast_to(stats[:, a + 8 : a + 9], (8, HD))
        top = jnp.maximum(mx[i], in_m[...])
        keep = jnp.exp2(mx[i] - top)
        add = jnp.exp2(in_m[...] - top)
        acc[i] = acc[i] * keep + oin[box, 0:rows, :].astype(F32) * add
        sm[i] = sm[i] * keep + in_l[...] * add
        mx[i] = top

    def pack(i):
        obuf[i, 0:rows, :] = acc[i].astype(BF)
        stats = jnp.zeros((8, HD), F32)
        for at, a in group_lanes:
            stats = jnp.where(lane == a, mx[i, pl.ds(at, 8), :], stats)
            stats = jnp.where(lane == a + 8, sm[i, pl.ds(at, 8), :], stats)
        first = stats.astype(BF).astype(F32)
        second = (stats - first).astype(BF).astype(F32)
        third = stats - first - second
        obuf[i, rows : rows + 32, :] = jnp.concatenate(
            [first, second, third, jnp.zeros((8, HD), F32)], axis=0
        ).astype(BF)

    def partner_step(m, carry):
        i = ring - 1 - m
        attend_partner(i)

        @pl.when(i + 2 < ring)
        def _():
            merge(i, i + 2)

        pack(i)
        out_copy(i).start()
        return carry

    lax.fori_loop(0, ring - 1, partner_step, 0)
    attend_partner(0)
    merge(0, 2)
    merge(0, 1)
    done = (acc[0] / sm[0]).astype(BF)
    for h in range(HEADS_DEV):
        att[:, h * HD : (h + 1) * HD] = done[h * tokens : (h + 1) * tokens]
    project(0)
    for j in range(parts):
        add_cores(0, j)
    for j in range(parts):
        decode_sum = summed(1, j)
        prefill_sum = summed(0, j)
        for c in range(2):
            rows_of = slice(c * each, (c + 1) * each)
            both = jnp.concatenate([prefill_sum[rows_of], decode_sum[rows_of]], axis=0).astype(BF)
            out_ref[:, c * width + j * wide_part : c * width + (j + 1) * wide_part] = both

    for i in range(1, ring):
        query_copy(i, qbuf.at[0]).wait_send()
        out_copy(i).wait_send()
    for k in range(2):
        span_copy(k).wait_send()
    span_relay().wait_send()
    for i in range(1, ring):
        gather_copy(i, z).wait_send()
    for p in range(PIECES):
        piece_copy(p).wait_send()
        piece_relay(p).wait_send()
    for which in range(2):
        for j in range(parts):
            core_copy(which, j).wait_send()
            for k in range(1, chips):
                chip_copy(which, j, k).wait_send()


def separate(sums_ref, prefill_ref, decode_ref):
    each = prefill_ref.shape[0]
    sums = sums_ref[...].astype(F32)
    prefill_ref[...] = sums[0:each].astype(BF)
    steps = decode_ref.shape[1]
    for r in range(decode_ref.shape[0]):
        decode_ref[r] = sums[each + r * steps : each + (r + 1) * steps].astype(BF)


def on_device(
    span_queries,
    span_keys,
    span_values,
    prompt_keys,
    prompt_values,
    block_owner,
    block_slot,
    decode_queries,
    decode_new_keys,
    decode_new_values,
    cache_keys,
    cache_values,
    cache_len,
    out_weight,
):
    ring = lax.axis_size("ctx") // 2
    tp_count = lax.axis_size("tp")
    tokens = span_queries.shape[1]
    width = span_queries.shape[2]
    prompt = prompt_keys.shape[1]
    row_count, step_count = decode_queries.shape[1:3]
    cache = cache_keys.shape[2]
    columns = out_weight.shape[1]
    each = tokens // tp_count
    rows = tokens * HEADS_DEV
    parts = 2
    wide_part = columns // 2 // parts
    chips = tp_count // 2
    span = 2 * tokens
    total = prompt + span
    vmem = pl.BlockSpec(memory_space=pltpu.VMEM)
    smem = pl.BlockSpec(memory_space=pltpu.SMEM)
    anywhere = pl.BlockSpec(memory_space=pl.ANY)
    dma = pltpu.SemaphoreType.DMA
    sums = pl.pallas_call(
        lambda *refs: kernel(ring, tp_count, *refs),
        out_shape=jax.ShapeDtypeStruct((2 * each, columns), BF),
        in_specs=[anywhere, vmem, vmem, anywhere, anywhere] + [vmem] * 5 + [anywhere, anywhere, smem, anywhere],
        out_specs=vmem,
        scratch_shapes=[
            pltpu.VMEM((ring, tokens, width), BF),
            pltpu.VMEM((span, HD), BF),
            pltpu.VMEM((span, HD), BF),
            pltpu.VMEM((ring, 2, span, HD), BF),
            pltpu.VMEM((PIECES, prompt // 4, HD), BF),
            pltpu.VMEM((PIECES, prompt // 4, HD), BF),
            pltpu.VMEM((prompt, HD), BF),
            pltpu.VMEM((prompt, HD), BF),
            pltpu.VMEM((prompt, 2 * HD), BF),
            pltpu.VMEM((prompt, 2 * HD), BF),
            pltpu.VMEM((total, 2 * HD), BF),
            pltpu.VMEM((total, 2 * HD), BF),
            pltpu.VMEM((ring, rows, HD), F32),
            pltpu.VMEM((ring, rows, HD), F32),
            pltpu.VMEM((ring, rows, HD), F32),
            pltpu.VMEM((rows, HD), F32),
            pltpu.VMEM((rows, HD), F32),
            pltpu.VMEM((ring, rows + 32, HD), BF),
            pltpu.VMEM((ring, rows + 32, HD), BF),
            pltpu.VMEM((width, columns), BF),
            pltpu.VMEM((row_count, cache, HD), BF),
            pltpu.VMEM((row_count, cache, HD), BF),
            pltpu.VMEM((tokens, width), BF),
            pltpu.VMEM((2, parts, 2, chips, 2 * each, wide_part), BF),
            pltpu.VMEM((2, parts, chips, 2 * each, wide_part), BF),
            pltpu.VMEM((2, parts, chips, 2 * each, wide_part), BF),
            pltpu.VMEM((2, parts, chips, 2 * each, wide_part), BF),
            dma((ring,)),
            dma((ring,)),
            dma((2,)),
            dma((2,)),
            dma((1,)),
            dma((1,)),
            dma((ring,)),
            dma((ring,)),
            dma((PIECES,)),
            dma((PIECES,)),
            dma((PIECES,)),
            dma((PIECES,)),
            dma((ring,)),
            dma((ring,)),
            dma((2, parts)),
            dma((2, parts)),
            dma((2, parts, chips)),
            dma((2, parts, chips)),
            dma((6,)),
        ],
        compiler_params=pltpu.CompilerParams(
            collective_id=0, has_side_effects=True, vmem_limit_bytes=60 * 1024 * 1024
        ),
        name="serve",
    )(
        span_queries[0],
        span_keys[0],
        span_values[0],
        prompt_keys[0],
        prompt_values[0],
        block_owner,
        block_slot,
        decode_queries[0],
        decode_new_keys.reshape(row_count * step_count, HD),
        decode_new_values.reshape(row_count * step_count, HD),
        cache_keys[0],
        cache_values[0],
        cache_len,
        out_weight,
    )
    prefill, decode = pl.pallas_call(
        separate,
        out_shape=(
            jax.ShapeDtypeStruct((each, columns), BF),
            jax.ShapeDtypeStruct((row_count // tp_count, step_count, columns), BF),
        ),
        in_specs=[vmem],
        out_specs=(vmem, vmem),
        name="separate",
    )(sums)
    return (prefill[None], decode[None])


def solution(mesh):
    in_specs = (
        P("grp", "ctx", "tp"),
        P("grp", "ctx", "tp"),
        P("grp", "ctx", "tp"),
        P("grp", "ctx", "tp"),
        P("grp", "ctx", "tp"),
        P(),
        P(),
        P("grp", "ctx", None, "tp"),
        P("grp", "ctx", None, "tp"),
        P("grp", "ctx", None, "tp"),
        P("grp", "ctx", None, "tp"),
        P("grp", "ctx", None, "tp"),
        P("grp", "ctx"),
        P("tp", None),
    )
    out_specs = (P("grp", ("ctx", "tp"), None), P("grp", ("ctx", "tp"), None, None))
    return jax.shard_map(
        on_device, mesh=mesh, in_specs=in_specs, out_specs=out_specs, check_vma=False
    )
```

```python
import math

import jax
import jax.numpy as jnp
from jax import lax
from jax.experimental import pallas as pl
from jax.experimental.pallas import tpu as pltpu
from jax.sharding import PartitionSpec as P

HD = 128
BLOCK = 16
SLOTS = 8
HEADS_DEV = 8
PIECES = 8
NEG = -1e30
SCALE2 = HD**-0.5 * math.log2(math.e)
MESH = pl.DeviceIdType.MESH
BF = jnp.bfloat16
F32 = jnp.float32


def dot_nt(a, b):
    return lax.dot_general(a, b, (((1,), (1,)), ((), ())), preferred_element_type=F32)


def dot_nn(a, b):
    return jnp.dot(a, b, preferred_element_type=F32)


def low_bits(x, size):
    return jnp.bitwise_and(x, size - 1)


def high_bits(x, size):
    return lax.shift_right_logical(x, size.bit_length() - 1)


def kernel(
    ring, tp_count,
    q_ref, sk_ref, sv_ref, pk_ref, pv_ref, owner_ref, slot_ref, dq_ref, dk_ref, dv_ref, ck_hbm, cv_hbm, len_ref, w_hbm,
    out_ref,
    qbuf, skv, skv_par, gath, rel, k_own, v_own, k_par, v_par,
    acc, mx, sm, in_m, in_l, obuf, oin,
    w, ck, cv, att, part, sib, pairs, got,
    q_send, q_recv, s_send, s_recv, sp_send, sp_recv, g_send, g_recv, r_send, r_recv, f_send, f_recv,
    o_send, o_recv, c_send, c_recv, p_send, p_recv, load,
):
    me = lax.axis_index("ctx")
    pool = lax.axis_index("grp")
    tp = lax.axis_index("tp")
    core = tp % 2
    chip = tp // 2
    chips = tp_count // 2
    y_hi = me // ring
    z = me % ring
    y = y_hi * 2 + pool
    tokens = sk_ref.shape[0]
    prompt = pk_ref.shape[0]
    chunk = prompt // 4
    right = y_hi * ring + (z + 1) % ring
    left = y_hi * ring + (z + ring - 1) % ring
    up_y = (y + 1) % 4
    down_y = (y + 3) % 4
    up = {"ctx": (up_y // 2) * ring + z, "grp": up_y % 2}
    down = {"ctx": (down_y // 2) * ring + z, "grp": down_y % 2}

    def remote(src, dst, send, recv, device):
        return pltpu.make_async_remote_copy(
            src_ref=src, dst_ref=dst, send_sem=send, recv_sem=recv, device_id=device, device_id_type=MESH
        )

    def toward(i):
        return {"ctx": left + (right - left) * (i % 2)}

    def back(i):
        return {"ctx": right + (left - right) * (i % 2)}

    def source_z(i):
        return (z - (2 * (i % 2) - 1) * ((i + 1) // 2) + ring) % ring

    def query_copy(i, src):
        return remote(src, qbuf.at[i], q_send.at[i], q_recv.at[i], toward(i))

    def span_copy(k):
        return remote(skv, gath.at[z, y_hi], s_send.at[k], s_recv.at[k], (up, down)[k])

    def span_relay():
        return remote(gath.at[z, down_y // 2], skv_par, sp_send.at[0], sp_recv.at[0], up)

    def gather_copy(i, at):
        return remote(gath.at[at], gath.at[at], g_send.at[i], g_recv.at[i], toward(i))

    def piece_rows(p):
        return ((p % 2) * 2 + p // 4) * chunk

    def piece_copy(p):
        src = (k_own if (p // 2) % 2 == 0 else v_own).at[pl.ds(piece_rows(p), chunk)]
        return remote(src, rel.at[p], r_send.at[p], r_recv.at[p], (up, down)[p % 2])

    def piece_relay(p):
        dst = (k_par if (p // 2) % 2 == 0 else v_par).at[pl.ds(piece_rows(p), chunk)]
        return remote(rel.at[p], dst, f_send.at[p], f_recv.at[p], (up, down)[p % 2])

    def forward_piece(p):
        piece_copy(p).wait_recv()
        piece_relay(p).start()

    loads = [
        pltpu.make_async_copy(pk_ref, k_own, load.at[0]),
        pltpu.make_async_copy(pv_ref, v_own, load.at[1]),
        pltpu.make_async_copy(q_ref, qbuf.at[0], load.at[2]),
        pltpu.make_async_copy(ck_hbm, ck, load.at[3]),
        pltpu.make_async_copy(cv_hbm, cv, load.at[4]),
        pltpu.make_async_copy(w_hbm, w, load.at[5]),
    ]
    for item in loads[:3]:
        item.start()

    other_core = {"tp": tp + 1 - 2 * core}
    other_chips = [{"tp": 2 * ((chip + k) % chips) + core} for k in range(1, chips)]
    barrier = pltpu.get_barrier_semaphore()
    for device in [{"ctx": right}, {"ctx": left}, up, down, other_core] + other_chips:
        pl.semaphore_signal(barrier, inc=1, device_id=device, device_id_type=MESH)
    skv[0:tokens, :] = sk_ref[...]
    skv[tokens : 2 * tokens, :] = sv_ref[...]
    for item in loads[:3]:
        item.wait()
    pl.semaphore_wait(barrier, 4 + chips)

    query_copy(1, qbuf.at[0]).start()
    query_copy(2, qbuf.at[0]).start()
    span_copy(0).start()
    span_copy(1).start()
    for p in range(PIECES):
        piece_copy(p).start()
    for item in loads[3:]:
        item.start()

    rows = tokens * HEADS_DEV

    def queries_of(i):
        return jnp.concatenate([qbuf[i, :, h * HD : (h + 1) * HD] for h in range(HEADS_DEV)], axis=0)

    def attend_own(i):
        scores = dot_nt(queries_of(i), k_own[...])
        top = jnp.max(scores, axis=1, keepdims=True)
        weights = jnp.exp2((scores - top) * SCALE2)
        total = jnp.sum(weights, axis=1, keepdims=True)
        out = dot_nn(weights.astype(BF), v_own[...])
        mx[i] = jnp.broadcast_to(top, (rows, HD))
        sm[i] = jnp.broadcast_to(total, (rows, HD))
        acc[i] = out

    def attend_partner(i):
        query_ctx = y_hi * ring + source_z(i)
        partner = (1 - y_hi) * ring + z
        token = low_bits(lax.broadcasted_iota(jnp.int32, (rows, 2 * tokens), 0), tokens)
        key = lax.broadcasted_iota(jnp.int32, (rows, 2 * tokens), 1)
        key_pos = jnp.where(key < tokens, me * tokens + key, partner * tokens + key - tokens)
        visible = key_pos <= query_ctx * tokens + token
        before = mx[i, :, 0:1]
        scores = dot_nt(queries_of(i), k_par[...])
        seen = jnp.where(visible, scores[:, prompt:], NEG)
        top = jnp.maximum(
            jnp.max(scores[:, 0:prompt], axis=1, keepdims=True), jnp.max(seen, axis=1, keepdims=True)
        )
        top = jnp.maximum(top, before)
        weights = jnp.concatenate(
            [jnp.exp2((scores[:, 0:prompt] - top) * SCALE2), jnp.exp2((seen - top) * SCALE2)], axis=1
        )
        total = jnp.sum(weights, axis=1, keepdims=True)
        out = dot_nn(weights.astype(BF), v_par[...])
        keep = jnp.exp2((before - top) * SCALE2)
        mx[i] = jnp.broadcast_to(top, (rows, HD))
        sm[i] = sm[i] * keep + total
        acc[i] = acc[i] * keep + out

    def own_step(n, carry):
        for c in range(2):
            @pl.when(jnp.logical_and(n % 2 == 1, n + c < ring))
            def _():
                query_copy(n + c, qbuf.at[0]).wait_recv()

            @pl.when(jnp.logical_and(n % 2 == 1, n + c + 2 < ring))
            def _():
                query_copy(n + c + 2, qbuf.at[n + c]).start()

        attend_own(n)

        @pl.when(n == 0)
        def _():
            for k in range(2):
                span_copy(k).wait_recv()
            span_relay().start()
            gather_copy(1, z).start()
            gather_copy(2, z).start()

        for c in range(PIECES // 2):
            @pl.when(n == min(c + 2, ring - 1))
            def _():
                forward_piece(2 * c)
                forward_piece(2 * c + 1)

        @pl.when(n > 0)
        def _():
            at = source_z(n)
            gather_copy(n, at).wait_recv()

            @pl.when(n + 2 < ring)
            def _():
                gather_copy(n + 2, at).start()

        return carry

    lax.fori_loop(0, ring, own_step, 0)

    each = tokens // tp_count
    parts = part.shape[1]
    wide_part = part.shape[5]
    step = min(512, wide_part)
    width = w.shape[1] // 2

    def core_copy(which, j):
        return remote(part.at[which, j, 1 - core], sib.at[which, j], c_send.at[which, j], c_recv.at[which, j], other_core)

    def chip_copy(which, j, k):
        return remote(
            pairs.at[which, j, (chip + k) % chips],
            got.at[which, j, k],
            p_send.at[which, j, k],
            p_recv.at[which, j, k],
            other_chips[k - 1],
        )

    def project(which):
        for j in range(parts):
            def columns(i, carry):
                at = pl.multiple_of(i * step, step)
                from_w = pl.multiple_of(at + j * wide_part, step)
                first = dot_nn(att[...], w[:, pl.ds(from_w, step)])
                second = dot_nn(att[...], w[:, pl.ds(pl.multiple_of(from_w + width, step), step)])
                for k in range(tp_count):
                    rows_of = slice(k * each, (k + 1) * each)
                    both = jnp.concatenate([first[rows_of], second[rows_of]], axis=0).astype(BF)
                    part[which, j, k % 2, k // 2, :, pl.ds(at, step)] = both
                return carry

            lax.fori_loop(0, wide_part // step, columns, 0)
            core_copy(which, j).start()

    def add_cores(which, j):
        core_copy(which, j).wait_recv()
        pairs[which, j] = (part[which, j, core].astype(F32) + sib[which, j].astype(F32)).astype(BF)
        for k in range(1, chips):
            chip_copy(which, j, k).start()

    def summed(which, j):
        total = part[which, j, core, chip].astype(F32) + sib[which, j, chip].astype(F32)
        for k in range(1, chips):
            chip_copy(which, j, k).wait_recv()
            total = total + got[which, j, k].astype(F32)
        return total

    for item in loads[3:]:
        item.wait()

    ctx_count = 2 * ring
    span_total = ctx_count * tokens
    blocks = owner_ref.shape[1]
    per_dev = tokens // BLOCK
    token_at = lax.broadcasted_iota(jnp.int32, (blocks, span_total), 1)
    block_at = lax.broadcasted_iota(jnp.int32, (blocks, span_total), 0)
    ring_at = high_bits(token_at, 2 * tokens)
    side_at = low_bits(high_bits(token_at, tokens), 2)
    block_of = (side_at * ring + ring_at) * per_dev + high_bits(low_bits(token_at, tokens), BLOCK)
    expand = jnp.where(block_of == block_at, 1.0, 0.0).astype(BF)
    other = 1 - pool
    owner_row = jnp.where(other == 0, owner_ref[0:1, :], owner_ref[1:2, :])
    slot_row = jnp.where(other == 0, slot_ref[0:1, :], slot_ref[1:2, :])
    owners = dot_nn(jnp.broadcast_to(owner_row, (8, blocks)).astype(F32).astype(BF), expand)[0:1, :]
    slots = dot_nn(jnp.broadcast_to(slot_row, (8, blocks)).astype(F32).astype(BF), expand)[0:1, :]
    slot_tokens = SLOTS * BLOCK
    wanted = jnp.where(owners == me.astype(F32), slots, -1.0).astype(jnp.int32)
    source = lax.broadcasted_iota(jnp.int32, (1, span_total), 1)
    wanted = wanted * BLOCK + low_bits(source, BLOCK)
    place = lax.broadcasted_iota(jnp.int32, (slot_tokens, span_total), 0)
    picked = jnp.where(place == wanted, 1.0, 0.0).astype(BF)
    gath_k = gath[:, :, 0:tokens, :].reshape(span_total, HD)
    gath_v = gath[:, :, tokens : 2 * tokens, :].reshape(span_total, HD)
    slot_k = dot_nn(picked, gath_k).astype(BF)
    slot_v = dot_nn(picked, gath_v).astype(BF)
    filled = dot_nt(jnp.ones((8, span_total), BF), picked)[0:1, :]

    steps = 4
    group = BLOCK // steps
    cache = ck.shape[1]
    new_pad = jnp.zeros((HD - dk_ref.shape[0], HD), BF)
    dec_rows = HEADS_DEV * BLOCK
    row_id = low_bits(lax.broadcasted_iota(jnp.int32, (dec_rows, HD), 0), BLOCK)
    col_id = lax.broadcasted_iota(jnp.int32, (dec_rows, HD), 1)
    crow_id = high_bits(low_bits(lax.broadcasted_iota(jnp.int32, (dec_rows, group * cache), 0), BLOCK), steps)
    ccol_id = high_bits(lax.broadcasted_iota(jnp.int32, (dec_rows, group * cache), 1), cache)
    one_row = lax.broadcasted_iota(jnp.int32, (1, group * cache), 1)

    def decode_group(g, carry):
        at = pl.ds(pl.multiple_of(g * BLOCK, BLOCK), BLOCK)
        asked = dq_ref[pl.ds(g * group, group)].astype(F32).reshape(BLOCK, HEADS_DEV * HD)
        queries = jnp.concatenate([asked[:, h * HD : (h + 1) * HD] for h in range(HEADS_DEV)], axis=0).astype(BF)
        keys = jnp.concatenate(
            [ck[pl.ds(g * group, group)].reshape(group * cache, HD), slot_k, dk_ref[...], new_pad], axis=0
        )
        values = jnp.concatenate(
            [cv[pl.ds(g * group, group)].reshape(group * cache, HD), slot_v, dv_ref[...], new_pad], axis=0
        )
        raw = dot_nt(queries, keys) * SCALE2
        live = jnp.zeros((1, group * cache), jnp.int32)
        for r in range(group):
            live = jnp.where(high_bits(one_row, cache) == r, len_ref[0, g * group + r], live)
        key_row = jnp.where(low_bits(one_row, cache) < live, high_bits(one_row, cache), -1)
        s_cache = jnp.where(crow_id == key_row, raw[:, 0 : group * cache], NEG)
        s_slot = jnp.where(filled > 0.5, raw[:, group * cache : group * cache + slot_tokens], NEG)
        here = g * BLOCK + row_id
        see_new = (high_bits(here, steps) == high_bits(col_id, steps)) & (col_id <= here)
        s_new = jnp.where(see_new, raw[:, group * cache + slot_tokens :], NEG)
        masked = jnp.concatenate([s_cache, s_slot, s_new], axis=1)
        top = jnp.max(masked, axis=1, keepdims=True)
        shares = jnp.exp2(masked - top)
        total = jnp.sum(shares, axis=1, keepdims=True)
        out = (dot_nn(shares.astype(BF), values) / total).astype(BF)
        for h in range(HEADS_DEV):
            att[at, h * HD : (h + 1) * HD] = out[h * BLOCK : (h + 1) * BLOCK]
        return carry

    lax.fori_loop(0, dq_ref.shape[0] // group, decode_group, 0)
    project(1)

    span_relay().wait_recv()
    span = 2 * tokens
    k_par[prompt : prompt + tokens, :] = sk_ref[...]
    k_par[prompt + tokens : prompt + span, :] = skv_par[0:tokens, :]
    v_par[prompt : prompt + tokens, :] = sv_ref[...]
    v_par[prompt + tokens : prompt + span, :] = skv_par[tokens:span, :]
    for j in range(parts):
        add_cores(1, j)
    for p in range(PIECES):
        piece_relay(p).wait_recv()

    def out_copy(i):
        return remote(obuf.at[i], oin.at[i], o_send.at[i], o_recv.at[i], back(i))

    lane = lax.broadcasted_iota(jnp.int32, (8, HD), 1)
    group_lanes = [(8 * a, (a % 8) * 16 + a // 8) for a in range(rows // 8)]

    def merge(i, box):
        out_copy(box).wait_recv()
        carried = oin[box, rows : rows + 32, :].astype(F32)
        stats = carried[0:8] + carried[8:16] + carried[16:24]
        for at, a in group_lanes:
            in_m[at : at + 8, :] = jnp.broadcast_to(stats[:, a : a + 1], (8, HD))
            in_l[at : at + 8, :] = jnp.broadcast_to(stats[:, a + 8 : a + 9], (8, HD))
        top = jnp.maximum(mx[i], in_m[...])
        keep = jnp.exp2((mx[i] - top) * SCALE2)
        add = jnp.exp2((in_m[...] - top) * SCALE2)
        acc[i] = acc[i] * keep + oin[box, 0:rows, :].astype(F32) * add
        sm[i] = sm[i] * keep + in_l[...] * add
        mx[i] = top

    def pack(i):
        obuf[i, 0:rows, :] = acc[i].astype(BF)
        stats = jnp.zeros((8, HD), F32)
        for at, a in group_lanes:
            stats = jnp.where(lane == a, mx[i, pl.ds(at, 8), :], stats)
            stats = jnp.where(lane == a + 8, sm[i, pl.ds(at, 8), :], stats)
        first = stats.astype(BF).astype(F32)
        second = (stats - first).astype(BF).astype(F32)
        third = stats - first - second
        obuf[i, rows : rows + 32, :] = jnp.concatenate(
            [first, second, third, jnp.zeros((8, HD), F32)], axis=0
        ).astype(BF)

    def partner_step(m, carry):
        i = ring - 1 - m
        attend_partner(i)

        @pl.when(i + 2 < ring)
        def _():
            merge(i, i + 2)

        pack(i)
        out_copy(i).start()
        return carry

    lax.fori_loop(0, ring - 1, partner_step, 0)
    attend_partner(0)
    merge(0, 2)
    merge(0, 1)
    done = (acc[0] / sm[0]).astype(BF)
    for h in range(HEADS_DEV):
        att[:, h * HD : (h + 1) * HD] = done[h * tokens : (h + 1) * tokens]
    project(0)
    for j in range(parts):
        add_cores(0, j)
    for j in range(parts):
        decode_sum = summed(1, j)
        prefill_sum = summed(0, j)
        for c in range(2):
            rows_of = slice(c * each, (c + 1) * each)
            both = jnp.concatenate([prefill_sum[rows_of], decode_sum[rows_of]], axis=0).astype(BF)
            out_ref[:, c * width + j * wide_part : c * width + (j + 1) * wide_part] = both

    for i in range(1, ring):
        query_copy(i, qbuf.at[0]).wait_send()
        out_copy(i).wait_send()
    for k in range(2):
        span_copy(k).wait_send()
    span_relay().wait_send()
    for i in range(1, ring):
        gather_copy(i, z).wait_send()
    for p in range(PIECES):
        piece_copy(p).wait_send()
        piece_relay(p).wait_send()
    for which in range(2):
        for j in range(parts):
            core_copy(which, j).wait_send()
            for k in range(1, chips):
                chip_copy(which, j, k).wait_send()


def separate(sums_ref, prefill_ref, decode_ref):
    each = prefill_ref.shape[0]
    sums = sums_ref[...].astype(F32)
    prefill_ref[...] = sums[0:each].astype(BF)
    steps = decode_ref.shape[1]
    for r in range(decode_ref.shape[0]):
        decode_ref[r] = sums[each + r * steps : each + (r + 1) * steps].astype(BF)


def on_device(
    span_queries,
    span_keys,
    span_values,
    prompt_keys,
    prompt_values,
    block_owner,
    block_slot,
    decode_queries,
    decode_new_keys,
    decode_new_values,
    cache_keys,
    cache_values,
    cache_len,
    out_weight,
):
    ring = lax.axis_size("ctx") // 2
    tp_count = lax.axis_size("tp")
    tokens = span_queries.shape[1]
    width = span_queries.shape[2]
    prompt = prompt_keys.shape[1]
    row_count, step_count = decode_queries.shape[1:3]
    cache = cache_keys.shape[2]
    columns = out_weight.shape[1]
    each = tokens // tp_count
    rows = tokens * HEADS_DEV
    parts = 2
    wide_part = columns // 2 // parts
    chips = tp_count // 2
    span = 2 * tokens
    total = prompt + span
    vmem = pl.BlockSpec(memory_space=pltpu.VMEM)
    smem = pl.BlockSpec(memory_space=pltpu.SMEM)
    anywhere = pl.BlockSpec(memory_space=pl.ANY)
    dma = pltpu.SemaphoreType.DMA
    sums = pl.pallas_call(
        lambda *refs: kernel(ring, tp_count, *refs),
        out_shape=jax.ShapeDtypeStruct((2 * each, columns), BF),
        in_specs=[anywhere, vmem, vmem, anywhere, anywhere] + [vmem] * 5 + [anywhere, anywhere, smem, anywhere],
        out_specs=vmem,
        scratch_shapes=[
            pltpu.VMEM((ring, tokens, width), BF),
            pltpu.VMEM((span, HD), BF),
            pltpu.VMEM((span, HD), BF),
            pltpu.VMEM((ring, 2, span, HD), BF),
            pltpu.VMEM((PIECES, prompt // 4, HD), BF),
            pltpu.VMEM((prompt, HD), BF),
            pltpu.VMEM((prompt, HD), BF),
            pltpu.VMEM((total, HD), BF),
            pltpu.VMEM((total, HD), BF),
            pltpu.VMEM((ring, rows, HD), F32),
            pltpu.VMEM((ring, rows, HD), F32),
            pltpu.VMEM((ring, rows, HD), F32),
            pltpu.VMEM((rows, HD), F32),
            pltpu.VMEM((rows, HD), F32),
            pltpu.VMEM((ring, rows + 32, HD), BF),
            pltpu.VMEM((ring, rows + 32, HD), BF),
            pltpu.VMEM((width, columns), BF),
            pltpu.VMEM((row_count, cache, HD), BF),
            pltpu.VMEM((row_count, cache, HD), BF),
            pltpu.VMEM((tokens, width), BF),
            pltpu.VMEM((2, parts, 2, chips, 2 * each, wide_part), BF),
            pltpu.VMEM((2, parts, chips, 2 * each, wide_part), BF),
            pltpu.VMEM((2, parts, chips, 2 * each, wide_part), BF),
            pltpu.VMEM((2, parts, chips, 2 * each, wide_part), BF),
            dma((ring,)),
            dma((ring,)),
            dma((2,)),
            dma((2,)),
            dma((1,)),
            dma((1,)),
            dma((ring,)),
            dma((ring,)),
            dma((PIECES,)),
            dma((PIECES,)),
            dma((PIECES,)),
            dma((PIECES,)),
            dma((ring,)),
            dma((ring,)),
            dma((2, parts)),
            dma((2, parts)),
            dma((2, parts, chips)),
            dma((2, parts, chips)),
            dma((6,)),
        ],
        compiler_params=pltpu.CompilerParams(
            collective_id=0, has_side_effects=True, vmem_limit_bytes=60 * 1024 * 1024
        ),
        name="serve",
    )(
        span_queries[0],
        span_keys[0],
        span_values[0],
        prompt_keys[0],
        prompt_values[0],
        block_owner,
        block_slot,
        decode_queries[0],
        decode_new_keys.reshape(row_count * step_count, HD),
        decode_new_values.reshape(row_count * step_count, HD),
        cache_keys[0],
        cache_values[0],
        cache_len,
        out_weight,
    )
    prefill, decode = pl.pallas_call(
        separate,
        out_shape=(
            jax.ShapeDtypeStruct((each, columns), BF),
            jax.ShapeDtypeStruct((row_count // tp_count, step_count, columns), BF),
        ),
        in_specs=[vmem],
        out_specs=(vmem, vmem),
        name="separate",
    )(sums)
    return (prefill[None], decode[None])


def solution(mesh):
    in_specs = (
        P("grp", "ctx", "tp"),
        P("grp", "ctx", "tp"),
        P("grp", "ctx", "tp"),
        P("grp", "ctx", "tp"),
        P("grp", "ctx", "tp"),
        P(),
        P(),
        P("grp", "ctx", None, "tp"),
        P("grp", "ctx", None, "tp"),
        P("grp", "ctx", None, "tp"),
        P("grp", "ctx", None, "tp"),
        P("grp", "ctx", None, "tp"),
        P("grp", "ctx"),
        P("tp", None),
    )
    out_specs = (P("grp", ("ctx", "tp"), None), P("grp", ("ctx", "tp"), None, None))
    return jax.shard_map(
        on_device, mesh=mesh, in_specs=in_specs, out_specs=out_specs, check_vma=False
    )
```

```python
import math

import jax
import jax.numpy as jnp
from jax import lax
from jax.experimental import pallas as pl
from jax.experimental.pallas import tpu as pltpu
from jax.sharding import PartitionSpec as P

HD = 128
BLOCK = 16
SLOTS = 8
HEADS_DEV = 8
PIECES = 8
TILE = 256
ROWS = 64
NEG = -1e30
SCALE2 = HD**-0.5 * math.log2(math.e)
MESH = pl.DeviceIdType.MESH
BF = jnp.bfloat16
F32 = jnp.float32


def dot_nt(a, b):
    return lax.dot_general(a, b, (((1,), (1,)), ((), ())), preferred_element_type=F32)


def dot_nn(a, b):
    return jnp.dot(a, b, preferred_element_type=F32)


def split_query(q):
    scaled = q.astype(F32) * SCALE2
    high = scaled.astype(BF)
    low = (scaled - high.astype(F32)).astype(BF)
    return jnp.concatenate([high, low], axis=1)


def low_bits(x, size):
    return jnp.bitwise_and(x, size - 1)


def high_bits(x, size):
    return lax.shift_right_logical(x, size.bit_length() - 1)


def kernel(
    ring, tp_count,
    q_ref, sk_ref, sv_ref, pk_ref, pv_ref, owner_ref, slot_ref, dq_ref, dk_ref, dv_ref, ck_hbm, cv_hbm, len_ref, w_hbm,
    out_ref,
    qbuf, skv, skv_par, gath, rel, par, k_raw, v_raw, k_own, v_own, k_par, v_par, raised, shares,
    acc, mx, sm, in_m, in_l, obuf, oin,
    w, ck, cv, att, part, sib, pairs, got,
    q_send, q_recv, s_send, s_recv, sp_send, sp_recv, g_send, g_recv, r_send, r_recv, f_send, f_recv,
    o_send, o_recv, c_send, c_recv, p_send, p_recv, load,
):
    me = lax.axis_index("ctx")
    pool = lax.axis_index("grp")
    tp = lax.axis_index("tp")
    core = tp % 2
    chip = tp // 2
    chips = tp_count // 2
    y_hi = me // ring
    z = me % ring
    y = y_hi * 2 + pool
    tokens = sk_ref.shape[0]
    prompt = pk_ref.shape[0]
    chunk = prompt // 4
    half_heads = HEADS_DEV // 2
    half = tokens * half_heads
    right = y_hi * ring + (z + 1) % ring
    left = y_hi * ring + (z + ring - 1) % ring
    up_y = (y + 1) % 4
    down_y = (y + 3) % 4
    up = {"ctx": (up_y // 2) * ring + z, "grp": up_y % 2}
    down = {"ctx": (down_y // 2) * ring + z, "grp": down_y % 2}

    def remote(src, dst, send, recv, device):
        return pltpu.make_async_remote_copy(
            src_ref=src, dst_ref=dst, send_sem=send, recv_sem=recv, device_id=device, device_id_type=MESH
        )

    def toward(i):
        return {"ctx": left + (right - left) * (i % 2)}

    def back(i):
        return {"ctx": right + (left - right) * (i % 2)}

    def source_z(i):
        return (z - (2 * (i % 2) - 1) * ((i + 1) // 2) + ring) % ring

    def query_copy(i, src):
        return remote(src, qbuf.at[i], q_send.at[i], q_recv.at[i], toward(i))

    def span_copy(k):
        return remote(skv, gath.at[z, y_hi], s_send.at[k], s_recv.at[k], (up, down)[k])

    def span_relay():
        return remote(gath.at[z, down_y // 2], skv_par, sp_send.at[0], sp_recv.at[0], up)

    def gather_copy(i, at):
        return remote(gath.at[at], gath.at[at], g_send.at[i], g_recv.at[i], toward(i))

    def piece_rows(p):
        return ((p % 2) * 2 + p // 4) * chunk

    def piece_copy(p):
        src = (k_raw if (p // 2) % 2 == 0 else v_raw).at[pl.ds(piece_rows(p), chunk)]
        return remote(src, rel.at[p], r_send.at[p], r_recv.at[p], (up, down)[p % 2])

    def piece_relay(p):
        return remote(rel.at[p], par.at[p], f_send.at[p], f_recv.at[p], (up, down)[p % 2])

    def forward_piece(p):
        piece_copy(p).wait_recv()
        piece_relay(p).start()

    loads = [
        pltpu.make_async_copy(pk_ref, k_raw, load.at[0]),
        pltpu.make_async_copy(pv_ref, v_raw, load.at[1]),
        pltpu.make_async_copy(q_ref, qbuf.at[0], load.at[2]),
        pltpu.make_async_copy(ck_hbm, ck, load.at[3]),
        pltpu.make_async_copy(cv_hbm, cv, load.at[4]),
        pltpu.make_async_copy(w_hbm, w, load.at[5]),
    ]
    for item in loads[:3]:
        item.start()

    other_core = {"tp": tp + 1 - 2 * core}
    other_chips = [{"tp": 2 * ((chip + k) % chips) + core} for k in range(1, chips)]
    barrier = pltpu.get_barrier_semaphore()
    for device in [{"ctx": right}, {"ctx": left}, up, down, other_core] + other_chips:
        pl.semaphore_signal(barrier, inc=1, device_id=device, device_id_type=MESH)
    skv[0:tokens, :] = sk_ref[...]
    skv[tokens : 2 * tokens, :] = sv_ref[...]
    for item in loads[:3]:
        item.wait()
    pl.semaphore_wait(barrier, 4 + chips)

    query_copy(1, qbuf.at[0]).start()
    query_copy(2, qbuf.at[0]).start()
    span_copy(0).start()
    span_copy(1).start()
    for p in range(PIECES):
        piece_copy(p).start()
    for item in loads[3:]:
        item.start()

    def put_keys(dst, at, rows):
        size = rows.shape[0]
        turned = rows.T
        dst[0:HD, at : at + size] = turned
        dst[HD : 2 * HD, at : at + size] = turned

    for c in range(4):
        put_keys(k_own, c * chunk, k_raw[c * chunk : (c + 1) * chunk])
    v_own[:, 0:HD] = v_raw[...]
    v_own[:, HD : 2 * HD] = jnp.ones((prompt, HD), BF)
    v_par[:, HD : 2 * HD] = jnp.ones((v_par.shape[0], HD), BF)

    spans = [pl.ds(0, half), pl.ds(half, half)]

    def queries_of(i):
        halves = []
        for b in range(2):
            heads = range(b * half_heads, (b + 1) * half_heads)
            halves.append(split_query(jnp.concatenate([qbuf[i, :, h * HD : (h + 1) * HD] for h in heads], axis=0)))
        return halves

    def attend(i, keys, values, span):
        total = keys.shape[1]
        tiles = [(a, min(TILE, total - a)) for a in range(0, total, TILE)]
        queries = queries_of(i)
        befores = [mx[i, at, 0:1] for at in spans] if span else None
        top = [None, None]
        out = [None, None]

        def score(b, a, size):
            s = dot_nn(queries[b], keys[:, a : a + size])
            if span and a == prompt:
                query_ctx = y_hi * ring + source_z(i)
                partner = (1 - y_hi) * ring + z
                token = low_bits(lax.broadcasted_iota(jnp.int32, (half, 2 * tokens), 0), tokens)
                key = lax.broadcasted_iota(jnp.int32, (half, 2 * tokens), 1)
                key_pos = jnp.where(key < tokens, me * tokens + key, partner * tokens + key - tokens)
                s = jnp.where(key_pos <= query_ctx * tokens + token, s, NEG)
            raised[b, :, a : a + size] = s
            for c in range(0, size, HD):
                piece = s[:, c : c + HD]
                top[b] = piece if top[b] is None else jnp.maximum(top[b], piece)

        def settle(b):
            top[b] = jnp.max(top[b], axis=1, keepdims=True)
            if span:
                top[b] = jnp.maximum(top[b], befores[b])

        def weigh(b, a, size):
            for r in range(0, half, ROWS):
                less = raised[b, r : r + ROWS, a : a + size] - top[b][r : r + ROWS]
                shares[b, r : r + ROWS, a : a + size] = jnp.exp2(less).astype(BF)

        def blend(b, a, end):
            piece = dot_nn(shares[b, :, a:end], values[a:end, :])
            out[b] = piece if out[b] is None else out[b] + piece

        middle = len(tiles) // 2
        cut = tiles[middle][0]
        for tile in tiles:
            score(0, *tile)
        settle(0)
        for tile in tiles:
            score(1, *tile)
            weigh(0, *tile)
        settle(1)
        blend(0, 0, cut)
        for tile in tiles[:middle]:
            weigh(1, *tile)
        blend(0, cut, total)
        blend(1, 0, cut)
        for tile in tiles[middle:]:
            weigh(1, *tile)
        blend(1, cut, total)
        for b, at in enumerate(spans):
            if span:
                keep = jnp.exp2(befores[b] - top[b])
                acc[i, at, :] = acc[i, at, :] * keep + out[b][:, 0:HD]
                sm[i, at, :] = sm[i, at, :] * keep + out[b][:, HD : 2 * HD]
            else:
                acc[i, at, :] = out[b][:, 0:HD]
                sm[i, at, :] = out[b][:, HD : 2 * HD]
            mx[i, at, :] = jnp.broadcast_to(top[b], (half, HD))

    def own_step(n, carry):
        for c in range(2):
            @pl.when(jnp.logical_and(n % 2 == 1, n + c < ring))
            def _():
                query_copy(n + c, qbuf.at[0]).wait_recv()

            @pl.when(jnp.logical_and(n % 2 == 1, n + c + 2 < ring))
            def _():
                query_copy(n + c + 2, qbuf.at[n + c]).start()

        attend(n, k_own, v_own, False)

        @pl.when(n == 0)
        def _():
            for k in range(2):
                span_copy(k).wait_recv()
            span_relay().start()
            gather_copy(1, z).start()
            gather_copy(2, z).start()

        for c in range(PIECES // 2):
            @pl.when(n == min(c + 2, ring - 1))
            def _():
                forward_piece(2 * c)
                forward_piece(2 * c + 1)

        @pl.when(n > 0)
        def _():
            at = source_z(n)
            gather_copy(n, at).wait_recv()

            @pl.when(n + 2 < ring)
            def _():
                gather_copy(n + 2, at).start()

        return carry

    lax.fori_loop(0, ring, own_step, 0)

    each = tokens // tp_count
    parts = part.shape[1]
    wide_part = part.shape[5]
    step = min(512, wide_part)
    width = w.shape[1] // 2

    def core_copy(which, j):
        return remote(part.at[which, j, 1 - core], sib.at[which, j], c_send.at[which, j], c_recv.at[which, j], other_core)

    def chip_copy(which, j, k):
        return remote(
            pairs.at[which, j, (chip + k) % chips],
            got.at[which, j, k],
            p_send.at[which, j, k],
            p_recv.at[which, j, k],
            other_chips[k - 1],
        )

    def project(which):
        for j in range(parts):
            def columns(i, carry):
                at = pl.multiple_of(i * step, step)
                from_w = pl.multiple_of(at + j * wide_part, step)
                first = dot_nn(att[...], w[:, pl.ds(from_w, step)])
                second = dot_nn(att[...], w[:, pl.ds(pl.multiple_of(from_w + width, step), step)])
                for k in range(tp_count):
                    rows_of = slice(k * each, (k + 1) * each)
                    both = jnp.concatenate([first[rows_of], second[rows_of]], axis=0).astype(BF)
                    part[which, j, k % 2, k // 2, :, pl.ds(at, step)] = both
                return carry

            lax.fori_loop(0, wide_part // step, columns, 0)
            core_copy(which, j).start()

    def add_cores(which, j):
        core_copy(which, j).wait_recv()
        pairs[which, j] = (part[which, j, core].astype(F32) + sib[which, j].astype(F32)).astype(BF)
        for k in range(1, chips):
            chip_copy(which, j, k).start()

    def summed(which, j):
        total = part[which, j, core, chip].astype(F32) + sib[which, j, chip].astype(F32)
        for k in range(1, chips):
            chip_copy(which, j, k).wait_recv()
            total = total + got[which, j, k].astype(F32)
        return total

    for item in loads[3:]:
        item.wait()

    ctx_count = 2 * ring
    span_total = ctx_count * tokens
    blocks = owner_ref.shape[1]
    per_dev = tokens // BLOCK
    token_at = lax.broadcasted_iota(jnp.int32, (blocks, span_total), 1)
    block_at = lax.broadcasted_iota(jnp.int32, (blocks, span_total), 0)
    ring_at = high_bits(token_at, 2 * tokens)
    side_at = low_bits(high_bits(token_at, tokens), 2)
    block_of = (side_at * ring + ring_at) * per_dev + high_bits(low_bits(token_at, tokens), BLOCK)
    expand = jnp.where(block_of == block_at, 1.0, 0.0).astype(BF)
    other = 1 - pool
    owner_row = jnp.where(other == 0, owner_ref[0:1, :], owner_ref[1:2, :])
    slot_row = jnp.where(other == 0, slot_ref[0:1, :], slot_ref[1:2, :])
    owners = dot_nn(jnp.broadcast_to(owner_row, (8, blocks)).astype(F32).astype(BF), expand)[0:1, :]
    slots = dot_nn(jnp.broadcast_to(slot_row, (8, blocks)).astype(F32).astype(BF), expand)[0:1, :]
    slot_tokens = SLOTS * BLOCK
    wanted = jnp.where(owners == me.astype(F32), slots, -1.0).astype(jnp.int32)
    source = lax.broadcasted_iota(jnp.int32, (1, span_total), 1)
    wanted = wanted * BLOCK + low_bits(source, BLOCK)
    place = lax.broadcasted_iota(jnp.int32, (slot_tokens, span_total), 0)
    picked = jnp.where(place == wanted, 1.0, 0.0).astype(BF)
    gath_k = gath[:, :, 0:tokens, :].reshape(span_total, HD)
    gath_v = gath[:, :, tokens : 2 * tokens, :].reshape(span_total, HD)
    slot_k = dot_nn(picked, gath_k).astype(BF)
    slot_v = dot_nn(picked, gath_v).astype(BF)
    filled = dot_nt(jnp.ones((8, span_total), BF), picked)[0:1, :]

    steps = 4
    group = BLOCK // steps
    cache = ck.shape[1]
    new_pad = jnp.zeros((HD - dk_ref.shape[0], HD), BF)
    dec_rows = HEADS_DEV * BLOCK
    row_id = low_bits(lax.broadcasted_iota(jnp.int32, (dec_rows, HD), 0), BLOCK)
    col_id = lax.broadcasted_iota(jnp.int32, (dec_rows, HD), 1)
    crow_id = high_bits(low_bits(lax.broadcasted_iota(jnp.int32, (dec_rows, group * cache), 0), BLOCK), steps)
    ccol_id = high_bits(lax.broadcasted_iota(jnp.int32, (dec_rows, group * cache), 1), cache)
    one_row = lax.broadcasted_iota(jnp.int32, (1, group * cache), 1)

    def decode_group(g, carry):
        at = pl.ds(pl.multiple_of(g * BLOCK, BLOCK), BLOCK)
        asked = dq_ref[pl.ds(g * group, group)].astype(F32).reshape(BLOCK, HEADS_DEV * HD)
        queries = jnp.concatenate([asked[:, h * HD : (h + 1) * HD] for h in range(HEADS_DEV)], axis=0).astype(BF)
        keys = jnp.concatenate(
            [ck[pl.ds(g * group, group)].reshape(group * cache, HD), slot_k, dk_ref[...], new_pad], axis=0
        )
        values = jnp.concatenate(
            [cv[pl.ds(g * group, group)].reshape(group * cache, HD), slot_v, dv_ref[...], new_pad], axis=0
        )
        raw = dot_nt(queries, keys) * SCALE2
        live = jnp.zeros((1, group * cache), jnp.int32)
        for r in range(group):
            live = jnp.where(high_bits(one_row, cache) == r, len_ref[0, g * group + r], live)
        key_row = jnp.where(low_bits(one_row, cache) < live, high_bits(one_row, cache), -1)
        s_cache = jnp.where(crow_id == key_row, raw[:, 0 : group * cache], NEG)
        s_slot = jnp.where(filled > 0.5, raw[:, group * cache : group * cache + slot_tokens], NEG)
        here = g * BLOCK + row_id
        see_new = (high_bits(here, steps) == high_bits(col_id, steps)) & (col_id <= here)
        s_new = jnp.where(see_new, raw[:, group * cache + slot_tokens :], NEG)
        masked = jnp.concatenate([s_cache, s_slot, s_new], axis=1)
        top = jnp.max(masked, axis=1, keepdims=True)
        shares = jnp.exp2(masked - top)
        total = jnp.sum(shares, axis=1, keepdims=True)
        out = (dot_nn(shares.astype(BF), values) / total).astype(BF)
        for h in range(HEADS_DEV):
            att[at, h * HD : (h + 1) * HD] = out[h * BLOCK : (h + 1) * BLOCK]
        return carry

    lax.fori_loop(0, dq_ref.shape[0] // group, decode_group, 0)
    project(1)

    span_relay().wait_recv()
    span = 2 * tokens
    put_keys(k_par, prompt, jnp.concatenate([sk_ref[...], skv_par[0:tokens, :]], axis=0))
    v_par[prompt : prompt + tokens, 0:HD] = sv_ref[...]
    v_par[prompt + tokens : prompt + span, 0:HD] = skv_par[tokens:span, :]
    for j in range(parts):
        add_cores(1, j)
    for p in range(PIECES):
        piece_relay(p).wait_recv()
        at = piece_rows(p)
        if (p // 2) % 2 == 0:
            put_keys(k_par, at, par[p])
        else:
            v_par[at : at + chunk, 0:HD] = par[p]

    rows = 2 * half

    def out_copy(i):
        return remote(obuf.at[i], oin.at[i], o_send.at[i], o_recv.at[i], back(i))

    lane = lax.broadcasted_iota(jnp.int32, (8, HD), 1)
    group_lanes = [(8 * a, (a % 8) * 16 + a // 8) for a in range(rows // 8)]

    def merge(i, box):
        out_copy(box).wait_recv()
        carried = oin[box, rows : rows + 32, :].astype(F32)
        stats = carried[0:8] + carried[8:16] + carried[16:24]
        for at, a in group_lanes:
            in_m[at : at + 8, :] = jnp.broadcast_to(stats[:, a : a + 1], (8, HD))
            in_l[at : at + 8, :] = jnp.broadcast_to(stats[:, a + 8 : a + 9], (8, HD))
        top = jnp.maximum(mx[i], in_m[...])
        keep = jnp.exp2(mx[i] - top)
        add = jnp.exp2(in_m[...] - top)
        acc[i] = acc[i] * keep + oin[box, 0:rows, :].astype(F32) * add
        sm[i] = sm[i] * keep + in_l[...] * add
        mx[i] = top

    def pack(i):
        obuf[i, 0:rows, :] = acc[i].astype(BF)
        stats = jnp.zeros((8, HD), F32)
        for at, a in group_lanes:
            stats = jnp.where(lane == a, mx[i, pl.ds(at, 8), :], stats)
            stats = jnp.where(lane == a + 8, sm[i, pl.ds(at, 8), :], stats)
        first = stats.astype(BF).astype(F32)
        second = (stats - first).astype(BF).astype(F32)
        third = stats - first - second
        obuf[i, rows : rows + 32, :] = jnp.concatenate(
            [first, second, third, jnp.zeros((8, HD), F32)], axis=0
        ).astype(BF)

    def partner_step(m, carry):
        i = ring - 1 - m
        attend(i, k_par, v_par, True)

        @pl.when(i + 2 < ring)
        def _():
            merge(i, i + 2)

        pack(i)
        out_copy(i).start()
        return carry

    lax.fori_loop(0, ring - 1, partner_step, 0)
    attend(0, k_par, v_par, True)
    merge(0, 2)
    merge(0, 1)
    done = (acc[0] / sm[0]).astype(BF)
    for h in range(HEADS_DEV):
        att[:, h * HD : (h + 1) * HD] = done[h * tokens : (h + 1) * tokens]
    project(0)
    for j in range(parts):
        add_cores(0, j)
    for j in range(parts):
        decode_sum = summed(1, j)
        prefill_sum = summed(0, j)
        for c in range(2):
            rows_of = slice(c * each, (c + 1) * each)
            both = jnp.concatenate([prefill_sum[rows_of], decode_sum[rows_of]], axis=0).astype(BF)
            out_ref[:, c * width + j * wide_part : c * width + (j + 1) * wide_part] = both

    for i in range(1, ring):
        query_copy(i, qbuf.at[0]).wait_send()
        out_copy(i).wait_send()
    for k in range(2):
        span_copy(k).wait_send()
    span_relay().wait_send()
    for i in range(1, ring):
        gather_copy(i, z).wait_send()
    for p in range(PIECES):
        piece_copy(p).wait_send()
        piece_relay(p).wait_send()
    for which in range(2):
        for j in range(parts):
            core_copy(which, j).wait_send()
            for k in range(1, chips):
                chip_copy(which, j, k).wait_send()


def separate(sums_ref, prefill_ref, decode_ref):
    each = prefill_ref.shape[0]
    sums = sums_ref[...].astype(F32)
    prefill_ref[...] = sums[0:each].astype(BF)
    steps = decode_ref.shape[1]
    for r in range(decode_ref.shape[0]):
        decode_ref[r] = sums[each + r * steps : each + (r + 1) * steps].astype(BF)


def on_device(
    span_queries,
    span_keys,
    span_values,
    prompt_keys,
    prompt_values,
    block_owner,
    block_slot,
    decode_queries,
    decode_new_keys,
    decode_new_values,
    cache_keys,
    cache_values,
    cache_len,
    out_weight,
):
    ring = lax.axis_size("ctx") // 2
    tp_count = lax.axis_size("tp")
    tokens = span_queries.shape[1]
    width = span_queries.shape[2]
    prompt = prompt_keys.shape[1]
    row_count, step_count = decode_queries.shape[1:3]
    cache = cache_keys.shape[2]
    columns = out_weight.shape[1]
    each = tokens // tp_count
    rows = tokens * HEADS_DEV
    parts = 2
    wide_part = columns // 2 // parts
    chips = tp_count // 2
    span = 2 * tokens
    total = prompt + span
    vmem = pl.BlockSpec(memory_space=pltpu.VMEM)
    smem = pl.BlockSpec(memory_space=pltpu.SMEM)
    anywhere = pl.BlockSpec(memory_space=pl.ANY)
    dma = pltpu.SemaphoreType.DMA
    sums = pl.pallas_call(
        lambda *refs: kernel(ring, tp_count, *refs),
        out_shape=jax.ShapeDtypeStruct((2 * each, columns), BF),
        in_specs=[anywhere, vmem, vmem, anywhere, anywhere] + [vmem] * 5 + [anywhere, anywhere, smem, anywhere],
        out_specs=vmem,
        scratch_shapes=[
            pltpu.VMEM((ring, tokens, width), BF),
            pltpu.VMEM((span, HD), BF),
            pltpu.VMEM((span, HD), BF),
            pltpu.VMEM((ring, 2, span, HD), BF),
            pltpu.VMEM((PIECES, prompt // 4, HD), BF),
            pltpu.VMEM((PIECES, prompt // 4, HD), BF),
            pltpu.VMEM((prompt, HD), BF),
            pltpu.VMEM((prompt, HD), BF),
            pltpu.VMEM((2 * HD, prompt), BF),
            pltpu.VMEM((prompt, 2 * HD), BF),
            pltpu.VMEM((2 * HD, total), BF),
            pltpu.VMEM((total, 2 * HD), BF),
            pltpu.VMEM((2, rows // 2, total), F32),
            pltpu.VMEM((2, rows // 2, total), BF),
            pltpu.VMEM((ring, rows, HD), F32),
            pltpu.VMEM((ring, rows, HD), F32),
            pltpu.VMEM((ring, rows, HD), F32),
            pltpu.VMEM((rows, HD), F32),
            pltpu.VMEM((rows, HD), F32),
            pltpu.VMEM((ring, rows + 32, HD), BF),
            pltpu.VMEM((ring, rows + 32, HD), BF),
            pltpu.VMEM((width, columns), BF),
            pltpu.VMEM((row_count, cache, HD), BF),
            pltpu.VMEM((row_count, cache, HD), BF),
            pltpu.VMEM((tokens, width), BF),
            pltpu.VMEM((2, parts, 2, chips, 2 * each, wide_part), BF),
            pltpu.VMEM((2, parts, chips, 2 * each, wide_part), BF),
            pltpu.VMEM((2, parts, chips, 2 * each, wide_part), BF),
            pltpu.VMEM((2, parts, chips, 2 * each, wide_part), BF),
            dma((ring,)),
            dma((ring,)),
            dma((2,)),
            dma((2,)),
            dma((1,)),
            dma((1,)),
            dma((ring,)),
            dma((ring,)),
            dma((PIECES,)),
            dma((PIECES,)),
            dma((PIECES,)),
            dma((PIECES,)),
            dma((ring,)),
            dma((ring,)),
            dma((2, parts)),
            dma((2, parts)),
            dma((2, parts, chips)),
            dma((2, parts, chips)),
            dma((6,)),
        ],
        compiler_params=pltpu.CompilerParams(
            collective_id=0, has_side_effects=True, vmem_limit_bytes=60 * 1024 * 1024
        ),
        name="serve",
    )(
        span_queries[0],
        span_keys[0],
        span_values[0],
        prompt_keys[0],
        prompt_values[0],
        block_owner,
        block_slot,
        decode_queries[0],
        decode_new_keys.reshape(row_count * step_count, HD),
        decode_new_values.reshape(row_count * step_count, HD),
        cache_keys[0],
        cache_values[0],
        cache_len,
        out_weight,
    )
    prefill, decode = pl.pallas_call(
        separate,
        out_shape=(
            jax.ShapeDtypeStruct((each, columns), BF),
            jax.ShapeDtypeStruct((row_count // tp_count, step_count, columns), BF),
        ),
        in_specs=[vmem],
        out_specs=(vmem, vmem),
        name="separate",
    )(sums)
    return (prefill[None], decode[None])


def solution(mesh):
    in_specs = (
        P("grp", "ctx", "tp"),
        P("grp", "ctx", "tp"),
        P("grp", "ctx", "tp"),
        P("grp", "ctx", "tp"),
        P("grp", "ctx", "tp"),
        P(),
        P(),
        P("grp", "ctx", None, "tp"),
        P("grp", "ctx", None, "tp"),
        P("grp", "ctx", None, "tp"),
        P("grp", "ctx", None, "tp"),
        P("grp", "ctx", None, "tp"),
        P("grp", "ctx"),
        P("tp", None),
    )
    out_specs = (P("grp", ("ctx", "tp"), None), P("grp", ("ctx", "tp"), None, None))
    return jax.shard_map(
        on_device, mesh=mesh, in_specs=in_specs, out_specs=out_specs, check_vma=False
    )
```

```python
import math

import jax
import jax.numpy as jnp
from jax import lax
from jax.experimental import pallas as pl
from jax.experimental.pallas import tpu as pltpu
from jax.sharding import PartitionSpec as P

HD = 128
BLOCK = 16
SLOTS = 8
HEADS_DEV = 8
PIECES = 8
TILE = 256
ROWS = 64
NEG = -1e30
SCALE2 = HD**-0.5 * math.log2(math.e)
MESH = pl.DeviceIdType.MESH
BF = jnp.bfloat16
F32 = jnp.float32


def dot_nt(a, b):
    return lax.dot_general(a, b, (((1,), (1,)), ((), ())), preferred_element_type=F32)


def dot_nn(a, b):
    return jnp.dot(a, b, preferred_element_type=F32)


def split_query(q):
    scaled = q.astype(F32) * SCALE2
    high = scaled.astype(BF)
    low = (scaled - high.astype(F32)).astype(BF)
    return jnp.concatenate([high, low], axis=1)


def low_bits(x, size):
    return jnp.bitwise_and(x, size - 1)


def high_bits(x, size):
    return lax.shift_right_logical(x, size.bit_length() - 1)


def kernel(
    ring, tp_count,
    q_ref, sk_ref, sv_ref, pk_ref, pv_ref, owner_ref, slot_ref, dq_ref, dk_ref, dv_ref, ck_hbm, cv_hbm, len_ref, w_hbm,
    out_ref,
    qbuf, skv, skv_par, gath, rel, par, k_raw, v_raw, k_own, v_own, k_par, v_par, raised, shares,
    acc, mx, sm, in_m, in_l, obuf, oin,
    w, ck, cv, att, part, sib, pairs, got,
    q_send, q_recv, s_send, s_recv, sp_send, sp_recv, g_send, g_recv, r_send, r_recv, f_send, f_recv,
    o_send, o_recv, c_send, c_recv, p_send, p_recv, load,
):
    me = lax.axis_index("ctx")
    pool = lax.axis_index("grp")
    tp = lax.axis_index("tp")
    core = tp % 2
    chip = tp // 2
    chips = tp_count // 2
    y_hi = me // ring
    z = me % ring
    y = y_hi * 2 + pool
    tokens = sk_ref.shape[0]
    prompt = pk_ref.shape[0]
    chunk = prompt // 4
    half_heads = HEADS_DEV // 2
    half = tokens * half_heads
    right = y_hi * ring + (z + 1) % ring
    left = y_hi * ring + (z + ring - 1) % ring
    up_y = (y + 1) % 4
    down_y = (y + 3) % 4
    up = {"ctx": (up_y // 2) * ring + z, "grp": up_y % 2}
    down = {"ctx": (down_y // 2) * ring + z, "grp": down_y % 2}

    def remote(src, dst, send, recv, device):
        return pltpu.make_async_remote_copy(
            src_ref=src, dst_ref=dst, send_sem=send, recv_sem=recv, device_id=device, device_id_type=MESH
        )

    def toward(i):
        return {"ctx": left + (right - left) * (i % 2)}

    def back(i):
        return {"ctx": right + (left - right) * (i % 2)}

    def source_z(i):
        return (z - (2 * (i % 2) - 1) * ((i + 1) // 2) + ring) % ring

    def query_copy(i, src):
        return remote(src, qbuf.at[i], q_send.at[i], q_recv.at[i], toward(i))

    def span_copy(k):
        return remote(skv, gath.at[z, y_hi], s_send.at[k], s_recv.at[k], (up, down)[k])

    def span_relay():
        return remote(gath.at[z, down_y // 2], skv_par, sp_send.at[0], sp_recv.at[0], up)

    def gather_copy(i, at):
        return remote(gath.at[at], gath.at[at], g_send.at[i], g_recv.at[i], toward(i))

    def piece_rows(p):
        return ((p % 2) * 2 + p // 4) * chunk

    def piece_copy(p):
        src = (k_raw if (p // 2) % 2 == 0 else v_raw).at[pl.ds(piece_rows(p), chunk)]
        return remote(src, rel.at[p], r_send.at[p], r_recv.at[p], (up, down)[p % 2])

    def piece_relay(p):
        return remote(rel.at[p], par.at[p], f_send.at[p], f_recv.at[p], (up, down)[p % 2])

    def forward_piece(p):
        piece_copy(p).wait_recv()
        piece_relay(p).start()

    loads = [
        pltpu.make_async_copy(pk_ref, k_raw, load.at[0]),
        pltpu.make_async_copy(pv_ref, v_raw, load.at[1]),
        pltpu.make_async_copy(q_ref, qbuf.at[0], load.at[2]),
        pltpu.make_async_copy(ck_hbm, ck, load.at[3]),
        pltpu.make_async_copy(cv_hbm, cv, load.at[4]),
        pltpu.make_async_copy(w_hbm, w, load.at[5]),
    ]
    for item in loads[:3]:
        item.start()

    other_core = {"tp": tp + 1 - 2 * core}
    other_chips = [{"tp": 2 * ((chip + k) % chips) + core} for k in range(1, chips)]
    barrier = pltpu.get_barrier_semaphore()
    for device in [{"ctx": right}, {"ctx": left}, up, down, other_core] + other_chips:
        pl.semaphore_signal(barrier, inc=1, device_id=device, device_id_type=MESH)
    skv[0:tokens, :] = sk_ref[...]
    skv[tokens : 2 * tokens, :] = sv_ref[...]
    for item in loads[:3]:
        item.wait()
    pl.semaphore_wait(barrier, 4 + chips)

    query_copy(1, qbuf.at[0]).start()
    query_copy(2, qbuf.at[0]).start()
    span_copy(0).start()
    span_copy(1).start()
    for p in range(PIECES):
        piece_copy(p).start()
    for item in loads[3:]:
        item.start()

    def put_keys(dst, at, rows):
        size = rows.shape[0]
        turned = rows.T
        dst[0:HD, at : at + size] = turned
        dst[HD : 2 * HD, at : at + size] = turned

    for c in range(4):
        put_keys(k_own, c * chunk, k_raw[c * chunk : (c + 1) * chunk])
    v_own[:, 0:HD] = v_raw[...]
    v_own[:, HD : 2 * HD] = jnp.ones((prompt, HD), BF)
    v_par[:, HD : 2 * HD] = jnp.ones((v_par.shape[0], HD), BF)

    spans = [pl.ds(0, half), pl.ds(half, half)]

    def queries_of(i, b):
        heads = range(b * half_heads, (b + 1) * half_heads)
        return split_query(jnp.concatenate([qbuf[i, :, h * HD : (h + 1) * HD] for h in heads], axis=0))

    def attend(shards, keys, values, span):
        total = keys.shape[1]
        tiles = [(a, min(TILE, total - a)) for a in range(0, total, TILE)]
        halves = [(i, b) for i in shards for b in range(2)]
        count = len(halves)
        queries = [queries_of(i, b) for i, b in halves]
        befores = [mx[i, spans[b], 0:1] for i, b in halves] if span else None
        top = [None] * count
        out = [None] * count

        def score(b, a, size):
            s = dot_nn(queries[b], keys[:, a : a + size])
            if span and a == prompt:
                query_ctx = y_hi * ring + source_z(halves[b][0])
                partner = (1 - y_hi) * ring + z
                token = low_bits(lax.broadcasted_iota(jnp.int32, (half, 2 * tokens), 0), tokens)
                key = lax.broadcasted_iota(jnp.int32, (half, 2 * tokens), 1)
                key_pos = jnp.where(key < tokens, me * tokens + key, partner * tokens + key - tokens)
                s = jnp.where(key_pos <= query_ctx * tokens + token, s, NEG)
            raised[b, :, a : a + size] = s
            for c in range(0, size, HD):
                piece = s[:, c : c + HD]
                top[b] = piece if top[b] is None else jnp.maximum(top[b], piece)

        def settle(b):
            top[b] = jnp.max(top[b], axis=1, keepdims=True)
            if span:
                top[b] = jnp.maximum(top[b], befores[b])

        def weigh(b, a, size):
            for r in range(0, half, ROWS):
                less = raised[b, r : r + ROWS, a : a + size] - top[b][r : r + ROWS]
                shares[b, r : r + ROWS, a : a + size] = jnp.exp2(less).astype(BF)

        def blend(b, a, end):
            piece = dot_nn(shares[b, :, a:end], values[a:end, :])
            out[b] = piece if out[b] is None else out[b] + piece

        middle = len(tiles) // 2
        cut = tiles[middle][0]
        for p in range(count):
            for c, tile in enumerate(tiles):
                score(p, *tile)
                if p >= 1:
                    weigh(p - 1, *tile)
                if p >= 2 and c == 0:
                    blend(p - 2, 0, cut)
                if p >= 2 and c == middle:
                    blend(p - 2, cut, total)
            settle(p)
        blend(count - 2, 0, cut)
        for tile in tiles[:middle]:
            weigh(count - 1, *tile)
        blend(count - 2, cut, total)
        blend(count - 1, 0, cut)
        for tile in tiles[middle:]:
            weigh(count - 1, *tile)
        blend(count - 1, cut, total)
        for h, (i, b) in enumerate(halves):
            at = spans[b]
            if span:
                keep = jnp.exp2(befores[h] - top[h])
                acc[i, at, :] = acc[i, at, :] * keep + out[h][:, 0:HD]
                sm[i, at, :] = sm[i, at, :] * keep + out[h][:, HD : 2 * HD]
            else:
                acc[i, at, :] = out[h][:, 0:HD]
                sm[i, at, :] = out[h][:, HD : 2 * HD]
            mx[i, at, :] = jnp.broadcast_to(top[h], (half, HD))

    def own_step(k, carry):
        for c in range(1, 3):
            m = 2 * k + c

            @pl.when(m < ring)
            def _():
                query_copy(m, qbuf.at[0]).wait_recv()

            @pl.when(m + 2 < ring)
            def _():
                query_copy(m + 2, qbuf.at[m]).start()

        @pl.when(k == 0)
        def _():
            for c in range(2):
                span_copy(c).wait_recv()
            span_relay().start()
            gather_copy(1, z).start()
            gather_copy(2, z).start()

        attend((2 * k, 2 * k + 1), k_own, v_own, False)

        for c in range(PIECES // 2):
            @pl.when(k == min(c, ring // 2 - 1, 2))
            def _():
                forward_piece(2 * c)
                forward_piece(2 * c + 1)

        for c in range(1, 3):
            m = 2 * k + c

            @pl.when(m < ring)
            def _():
                gather_copy(m, source_z(m)).wait_recv()

            @pl.when(m + 2 < ring)
            def _():
                gather_copy(m + 2, source_z(m)).start()

        return carry

    lax.fori_loop(0, ring // 2, own_step, 0)

    each = tokens // tp_count
    parts = part.shape[1]
    wide_part = part.shape[5]
    step = min(512, wide_part)
    width = w.shape[1] // 2

    def core_copy(which, j):
        return remote(part.at[which, j, 1 - core], sib.at[which, j], c_send.at[which, j], c_recv.at[which, j], other_core)

    def chip_copy(which, j, k):
        return remote(
            pairs.at[which, j, (chip + k) % chips],
            got.at[which, j, k],
            p_send.at[which, j, k],
            p_recv.at[which, j, k],
            other_chips[k - 1],
        )

    def project(which):
        for j in range(parts):
            def columns(i, carry):
                at = pl.multiple_of(i * step, step)
                from_w = pl.multiple_of(at + j * wide_part, step)
                first = dot_nn(att[...], w[:, pl.ds(from_w, step)])
                second = dot_nn(att[...], w[:, pl.ds(pl.multiple_of(from_w + width, step), step)])
                for k in range(tp_count):
                    rows_of = slice(k * each, (k + 1) * each)
                    both = jnp.concatenate([first[rows_of], second[rows_of]], axis=0).astype(BF)
                    part[which, j, k % 2, k // 2, :, pl.ds(at, step)] = both
                return carry

            lax.fori_loop(0, wide_part // step, columns, 0)
            core_copy(which, j).start()

    def add_cores(which, j):
        core_copy(which, j).wait_recv()
        pairs[which, j] = (part[which, j, core].astype(F32) + sib[which, j].astype(F32)).astype(BF)
        for k in range(1, chips):
            chip_copy(which, j, k).start()

    def summed(which, j):
        total = part[which, j, core, chip].astype(F32) + sib[which, j, chip].astype(F32)
        for k in range(1, chips):
            chip_copy(which, j, k).wait_recv()
            total = total + got[which, j, k].astype(F32)
        return total

    for item in loads[3:]:
        item.wait()

    ctx_count = 2 * ring
    span_total = ctx_count * tokens
    blocks = owner_ref.shape[1]
    per_dev = tokens // BLOCK
    token_at = lax.broadcasted_iota(jnp.int32, (blocks, span_total), 1)
    block_at = lax.broadcasted_iota(jnp.int32, (blocks, span_total), 0)
    ring_at = high_bits(token_at, 2 * tokens)
    side_at = low_bits(high_bits(token_at, tokens), 2)
    block_of = (side_at * ring + ring_at) * per_dev + high_bits(low_bits(token_at, tokens), BLOCK)
    expand = jnp.where(block_of == block_at, 1.0, 0.0).astype(BF)
    other = 1 - pool
    owner_row = jnp.where(other == 0, owner_ref[0:1, :], owner_ref[1:2, :])
    slot_row = jnp.where(other == 0, slot_ref[0:1, :], slot_ref[1:2, :])
    owners = dot_nn(jnp.broadcast_to(owner_row, (8, blocks)).astype(F32).astype(BF), expand)[0:1, :]
    slots = dot_nn(jnp.broadcast_to(slot_row, (8, blocks)).astype(F32).astype(BF), expand)[0:1, :]
    slot_tokens = SLOTS * BLOCK
    wanted = jnp.where(owners == me.astype(F32), slots, -1.0).astype(jnp.int32)
    source = lax.broadcasted_iota(jnp.int32, (1, span_total), 1)
    wanted = wanted * BLOCK + low_bits(source, BLOCK)
    place = lax.broadcasted_iota(jnp.int32, (slot_tokens, span_total), 0)
    picked = jnp.where(place == wanted, 1.0, 0.0).astype(BF)
    gath_k = gath[:, :, 0:tokens, :].reshape(span_total, HD)
    gath_v = gath[:, :, tokens : 2 * tokens, :].reshape(span_total, HD)
    slot_k = dot_nn(picked, gath_k).astype(BF)
    slot_v = dot_nn(picked, gath_v).astype(BF)
    filled = dot_nt(jnp.ones((8, span_total), BF), picked)[0:1, :]

    steps = 4
    group = BLOCK // steps
    cache = ck.shape[1]
    new_pad = jnp.zeros((HD - dk_ref.shape[0], HD), BF)
    dec_rows = HEADS_DEV * BLOCK
    row_id = low_bits(lax.broadcasted_iota(jnp.int32, (dec_rows, HD), 0), BLOCK)
    col_id = lax.broadcasted_iota(jnp.int32, (dec_rows, HD), 1)
    crow_id = high_bits(low_bits(lax.broadcasted_iota(jnp.int32, (dec_rows, group * cache), 0), BLOCK), steps)
    ccol_id = high_bits(lax.broadcasted_iota(jnp.int32, (dec_rows, group * cache), 1), cache)
    one_row = lax.broadcasted_iota(jnp.int32, (1, group * cache), 1)

    def decode_group(g, carry):
        at = pl.ds(pl.multiple_of(g * BLOCK, BLOCK), BLOCK)
        asked = dq_ref[pl.ds(g * group, group)].astype(F32).reshape(BLOCK, HEADS_DEV * HD)
        queries = jnp.concatenate([asked[:, h * HD : (h + 1) * HD] for h in range(HEADS_DEV)], axis=0).astype(BF)
        keys = jnp.concatenate(
            [ck[pl.ds(g * group, group)].reshape(group * cache, HD), slot_k, dk_ref[...], new_pad], axis=0
        )
        values = jnp.concatenate(
            [cv[pl.ds(g * group, group)].reshape(group * cache, HD), slot_v, dv_ref[...], new_pad], axis=0
        )
        raw = dot_nt(queries, keys) * SCALE2
        live = jnp.zeros((1, group * cache), jnp.int32)
        for r in range(group):
            live = jnp.where(high_bits(one_row, cache) == r, len_ref[0, g * group + r], live)
        key_row = jnp.where(low_bits(one_row, cache) < live, high_bits(one_row, cache), -1)
        s_cache = jnp.where(crow_id == key_row, raw[:, 0 : group * cache], NEG)
        s_slot = jnp.where(filled > 0.5, raw[:, group * cache : group * cache + slot_tokens], NEG)
        here = g * BLOCK + row_id
        see_new = (high_bits(here, steps) == high_bits(col_id, steps)) & (col_id <= here)
        s_new = jnp.where(see_new, raw[:, group * cache + slot_tokens :], NEG)
        masked = jnp.concatenate([s_cache, s_slot, s_new], axis=1)
        top = jnp.max(masked, axis=1, keepdims=True)
        shares = jnp.exp2(masked - top)
        total = jnp.sum(shares, axis=1, keepdims=True)
        out = (dot_nn(shares.astype(BF), values) / total).astype(BF)
        for h in range(HEADS_DEV):
            att[at, h * HD : (h + 1) * HD] = out[h * BLOCK : (h + 1) * BLOCK]
        return carry

    lax.fori_loop(0, dq_ref.shape[0] // group, decode_group, 0)
    project(1)

    span_relay().wait_recv()
    span = 2 * tokens
    put_keys(k_par, prompt, jnp.concatenate([sk_ref[...], skv_par[0:tokens, :]], axis=0))
    v_par[prompt : prompt + tokens, 0:HD] = sv_ref[...]
    v_par[prompt + tokens : prompt + span, 0:HD] = skv_par[tokens:span, :]
    for j in range(parts):
        add_cores(1, j)
    for p in range(PIECES):
        piece_relay(p).wait_recv()
        at = piece_rows(p)
        if (p // 2) % 2 == 0:
            put_keys(k_par, at, par[p])
        else:
            v_par[at : at + chunk, 0:HD] = par[p]

    rows = 2 * half

    def out_copy(i):
        return remote(obuf.at[i], oin.at[i], o_send.at[i], o_recv.at[i], back(i))

    lane = lax.broadcasted_iota(jnp.int32, (8, HD), 1)
    group_lanes = [(8 * a, (a % 8) * 16 + a // 8) for a in range(rows // 8)]

    def merge(i, box):
        out_copy(box).wait_recv()
        carried = oin[box, rows : rows + 32, :].astype(F32)
        stats = carried[0:8] + carried[8:16] + carried[16:24]
        for at, a in group_lanes:
            in_m[at : at + 8, :] = jnp.broadcast_to(stats[:, a : a + 1], (8, HD))
            in_l[at : at + 8, :] = jnp.broadcast_to(stats[:, a + 8 : a + 9], (8, HD))
        top = jnp.maximum(mx[i], in_m[...])
        keep = jnp.exp2(mx[i] - top)
        add = jnp.exp2(in_m[...] - top)
        acc[i] = acc[i] * keep + oin[box, 0:rows, :].astype(F32) * add
        sm[i] = sm[i] * keep + in_l[...] * add
        mx[i] = top

    def pack(i):
        obuf[i, 0:rows, :] = acc[i].astype(BF)
        stats = jnp.zeros((8, HD), F32)
        for at, a in group_lanes:
            stats = jnp.where(lane == a, mx[i, pl.ds(at, 8), :], stats)
            stats = jnp.where(lane == a + 8, sm[i, pl.ds(at, 8), :], stats)
        first = stats.astype(BF).astype(F32)
        second = (stats - first).astype(BF).astype(F32)
        third = stats - first - second
        obuf[i, rows : rows + 32, :] = jnp.concatenate(
            [first, second, third, jnp.zeros((8, HD), F32)], axis=0
        ).astype(BF)

    def partner_step(m, carry):
        k = ring // 2 - 1 - m
        attend((2 * k + 1, 2 * k), k_par, v_par, True)
        for i in (2 * k + 1, 2 * k):
            @pl.when(i + 2 < ring)
            def _():
                merge(i, i + 2)

            pack(i)
            out_copy(i).start()
        return carry

    lax.fori_loop(0, ring // 2 - 1, partner_step, 0)
    attend((1,), k_par, v_par, True)
    merge(1, 3)
    pack(1)
    out_copy(1).start()
    attend((0,), k_par, v_par, True)
    merge(0, 2)
    merge(0, 1)
    done = (acc[0] / sm[0]).astype(BF)
    for h in range(HEADS_DEV):
        att[:, h * HD : (h + 1) * HD] = done[h * tokens : (h + 1) * tokens]
    project(0)
    for j in range(parts):
        add_cores(0, j)
    for j in range(parts):
        decode_sum = summed(1, j)
        prefill_sum = summed(0, j)
        for c in range(2):
            rows_of = slice(c * each, (c + 1) * each)
            both = jnp.concatenate([prefill_sum[rows_of], decode_sum[rows_of]], axis=0).astype(BF)
            out_ref[:, c * width + j * wide_part : c * width + (j + 1) * wide_part] = both

    for i in range(1, ring):
        query_copy(i, qbuf.at[0]).wait_send()
        out_copy(i).wait_send()
    for k in range(2):
        span_copy(k).wait_send()
    span_relay().wait_send()
    for i in range(1, ring):
        gather_copy(i, z).wait_send()
    for p in range(PIECES):
        piece_copy(p).wait_send()
        piece_relay(p).wait_send()
    for which in range(2):
        for j in range(parts):
            core_copy(which, j).wait_send()
            for k in range(1, chips):
                chip_copy(which, j, k).wait_send()


def separate(sums_ref, prefill_ref, decode_ref):
    each = prefill_ref.shape[0]
    sums = sums_ref[...].astype(F32)
    prefill_ref[...] = sums[0:each].astype(BF)
    steps = decode_ref.shape[1]
    for r in range(decode_ref.shape[0]):
        decode_ref[r] = sums[each + r * steps : each + (r + 1) * steps].astype(BF)


def on_device(
    span_queries,
    span_keys,
    span_values,
    prompt_keys,
    prompt_values,
    block_owner,
    block_slot,
    decode_queries,
    decode_new_keys,
    decode_new_values,
    cache_keys,
    cache_values,
    cache_len,
    out_weight,
):
    ring = lax.axis_size("ctx") // 2
    tp_count = lax.axis_size("tp")
    tokens = span_queries.shape[1]
    width = span_queries.shape[2]
    prompt = prompt_keys.shape[1]
    row_count, step_count = decode_queries.shape[1:3]
    cache = cache_keys.shape[2]
    columns = out_weight.shape[1]
    each = tokens // tp_count
    rows = tokens * HEADS_DEV
    parts = 2
    wide_part = columns // 2 // parts
    chips = tp_count // 2
    span = 2 * tokens
    total = prompt + span
    vmem = pl.BlockSpec(memory_space=pltpu.VMEM)
    smem = pl.BlockSpec(memory_space=pltpu.SMEM)
    anywhere = pl.BlockSpec(memory_space=pl.ANY)
    dma = pltpu.SemaphoreType.DMA
    sums = pl.pallas_call(
        lambda *refs: kernel(ring, tp_count, *refs),
        out_shape=jax.ShapeDtypeStruct((2 * each, columns), BF),
        in_specs=[anywhere, vmem, vmem, anywhere, anywhere] + [vmem] * 5 + [anywhere, anywhere, smem, anywhere],
        out_specs=vmem,
        scratch_shapes=[
            pltpu.VMEM((ring, tokens, width), BF),
            pltpu.VMEM((span, HD), BF),
            pltpu.VMEM((span, HD), BF),
            pltpu.VMEM((ring, 2, span, HD), BF),
            pltpu.VMEM((PIECES, prompt // 4, HD), BF),
            pltpu.VMEM((PIECES, prompt // 4, HD), BF),
            pltpu.VMEM((prompt, HD), BF),
            pltpu.VMEM((prompt, HD), BF),
            pltpu.VMEM((2 * HD, prompt), BF),
            pltpu.VMEM((prompt, 2 * HD), BF),
            pltpu.VMEM((2 * HD, total), BF),
            pltpu.VMEM((total, 2 * HD), BF),
            pltpu.VMEM((4, rows // 2, total), F32),
            pltpu.VMEM((4, rows // 2, total), BF),
            pltpu.VMEM((ring, rows, HD), F32),
            pltpu.VMEM((ring, rows, HD), F32),
            pltpu.VMEM((ring, rows, HD), F32),
            pltpu.VMEM((rows, HD), F32),
            pltpu.VMEM((rows, HD), F32),
            pltpu.VMEM((ring, rows + 32, HD), BF),
            pltpu.VMEM((ring, rows + 32, HD), BF),
            pltpu.VMEM((width, columns), BF),
            pltpu.VMEM((row_count, cache, HD), BF),
            pltpu.VMEM((row_count, cache, HD), BF),
            pltpu.VMEM((tokens, width), BF),
            pltpu.VMEM((2, parts, 2, chips, 2 * each, wide_part), BF),
            pltpu.VMEM((2, parts, chips, 2 * each, wide_part), BF),
            pltpu.VMEM((2, parts, chips, 2 * each, wide_part), BF),
            pltpu.VMEM((2, parts, chips, 2 * each, wide_part), BF),
            dma((ring,)),
            dma((ring,)),
            dma((2,)),
            dma((2,)),
            dma((1,)),
            dma((1,)),
            dma((ring,)),
            dma((ring,)),
            dma((PIECES,)),
            dma((PIECES,)),
            dma((PIECES,)),
            dma((PIECES,)),
            dma((ring,)),
            dma((ring,)),
            dma((2, parts)),
            dma((2, parts)),
            dma((2, parts, chips)),
            dma((2, parts, chips)),
            dma((6,)),
        ],
        compiler_params=pltpu.CompilerParams(
            collective_id=0, has_side_effects=True, vmem_limit_bytes=60 * 1024 * 1024
        ),
        name="serve",
    )(
        span_queries[0],
        span_keys[0],
        span_values[0],
        prompt_keys[0],
        prompt_values[0],
        block_owner,
        block_slot,
        decode_queries[0],
        decode_new_keys.reshape(row_count * step_count, HD),
        decode_new_values.reshape(row_count * step_count, HD),
        cache_keys[0],
        cache_values[0],
        cache_len,
        out_weight,
    )
    prefill, decode = pl.pallas_call(
        separate,
        out_shape=(
            jax.ShapeDtypeStruct((each, columns), BF),
            jax.ShapeDtypeStruct((row_count // tp_count, step_count, columns), BF),
        ),
        in_specs=[vmem],
        out_specs=(vmem, vmem),
        name="separate",
    )(sums)
    return (prefill[None], decode[None])


def solution(mesh):
    in_specs = (
        P("grp", "ctx", "tp"),
        P("grp", "ctx", "tp"),
        P("grp", "ctx", "tp"),
        P("grp", "ctx", "tp"),
        P("grp", "ctx", "tp"),
        P(),
        P(),
        P("grp", "ctx", None, "tp"),
        P("grp", "ctx", None, "tp"),
        P("grp", "ctx", None, "tp"),
        P("grp", "ctx", None, "tp"),
        P("grp", "ctx", None, "tp"),
        P("grp", "ctx"),
        P("tp", None),
    )
    out_specs = (P("grp", ("ctx", "tp"), None), P("grp", ("ctx", "tp"), None, None))
    return jax.shard_map(
        on_device, mesh=mesh, in_specs=in_specs, out_specs=out_specs, check_vma=False
    )
```
